32 devices in a mesh: row: 8 (over z, x), col: 4 (over y, core).
Axes of the slice: x: 2, y: 2, z: 4, core: 2. Of those that a mesh axis runs over, the one named last changes fastest.
Arguments:
- kernel_tiles: float32 [1, 8, 2, 4, 1024, 1024], P(None, 'row', None, 'col'), may hold values from 0 to 2.5, as said below
- profile: int32 [2, 8], replicated, may hold values from 0 to 7, as said below
Outputs:
- factored: float32 [1, 8, 2, 4, 1024, 1024], P(None, 'row', None, 'col')
The draws below stay inside these ranges and needn't reach their ends.
Inputs may be any that keep to these rules, and one draw needn't show every extreme that they name: profile[0] never falls along the tile rows; profile[0, i] >= i - 5, and profile[0, i] = 0 for i <= 5; profile[1, i] is the last j with profile[0, j] <= i. `kernel_tiles`: symmetric; every tile outside the pattern is zero; the matrix restricted to the pattern is positive definite.
All inputs are finite; a program needn't handle non-finite values.
Results may differ from the reference program's by a relative error of at most 0.0001.
Values sent between devices are 32-bit elements; how exact they have to be, the bound alone decides.
No kernel may reach another device: no remote copies, remote signals or barrier semaphores. Data moves between devices by JAX's collectives and lax.ppermute only.
A program may use at most 256 MiB of HBM per device.

```python
import jax
import jax.numpy as jnp
from jax import lax

TILE = 1024
TR_DEV = 1
STEPS = 2
NT = 8
BAND = 5
TC_DEV = 2
N_ROW = 8
N_COL = 4


def banded_profile(key):
    key = jax.random.fold_in(key, 11)
    widths = jax.random.randint(key, (NT,), 1, BAND + 1)
    tile_ids = jnp.arange(NT, dtype=jnp.int32)
    widths = jnp.where(tile_ids <= BAND, BAND, widths)
    first_col = jnp.maximum(tile_ids - widths, 0)
    first_col = lax.cummax(first_col, axis=0)
    last_col = jnp.sum((first_col[None, :] <= tile_ids[:, None]).astype(jnp.int32), axis=1) - 1
    return jnp.stack([first_col, last_col]).astype(jnp.int32)


def draw_profile(key, part):
    return banded_profile(key)


def draw_kernel_tiles(key, part):
    profile = banded_profile(key)
    key = jax.random.fold_in(key, 5)
    key_points, key_noise = jax.random.split(key)
    points = jax.random.uniform(key_points, (3, NT, TILE), jnp.float32)
    noise = jax.random.uniform(key_noise, (NT, TILE), jnp.float32, 0.5, 1.5)
    last_col = profile[1]
    tile_ids = jnp.arange(NT, dtype=jnp.int32)
    lower_tile = jnp.minimum(tile_ids[:, None], tile_ids[None, :])
    upper_tile = jnp.maximum(tile_ids[:, None], tile_ids[None, :])
    taper = jnp.maximum(last_col[lower_tile] - upper_tile + 1, 0).astype(jnp.float32) / jnp.float32(BAND + 1)
    length_scale = jnp.float32(0.8 * float(TILE) ** (-1.0 / 3.0))
    inner = jnp.arange(TILE, dtype=jnp.int32)
    identity = (inner[:, None] == inner[None, :]).astype(jnp.float32)

    def tile_row(tile_index):
        own_points = points[:, tile_index]
        squared = jnp.zeros((NT, TILE, TILE), jnp.float32)
        for component in range(3):
            offset = own_points[component][None, :, None] - points[component][:, None, :]
            squared = squared + offset * offset
        values = jnp.exp(-jnp.sqrt(squared) / length_scale) * taper[tile_index][:, None, None]
        on_tile = (tile_ids == tile_index).astype(jnp.float32)[:, None, None]
        nugget = on_tile * identity[None] * noise[tile_index][None, :, None]
        return values + nugget
    all_rows = lax.map(tile_row, tile_ids)
    return all_rows.reshape(TR_DEV, N_ROW, TC_DEV, N_COL, TILE, TILE)


def setup_inputs(seed: int = 0) -> dict:
    arg_keys = jax.random.split(jax.random.key(seed), 3)
    return {
        "kernel_tiles": draw_kernel_tiles(jax.random.fold_in(arg_keys[2], 71), 0),
        "profile": draw_profile(jax.random.fold_in(arg_keys[2], 71), 0),
    }


def solve_right(block_tile, lower_factor):
    return lax.linalg.triangular_solve(lower_factor, block_tile, left_side=False, lower=True, transpose_a=True)

def reference(kernel_tiles, profile):
    count = TR_DEV * N_ROW
    matrix = kernel_tiles.reshape(count, count, TILE, TILE)
    indices = jnp.arange(count, dtype=jnp.int32)
    first_col = profile[0]
    last_col = profile[1]
    row_ids = indices[:, None]
    col_ids = indices[None, :]
    in_pattern = jnp.where(row_ids >= col_ids, first_col[:, None] <= col_ids, col_ids <= last_col[:, None])
    matrix = jnp.where(in_pattern[:, :, None, None], matrix, jnp.float32(0.0))
    for step in range(STEPS):
        diag_factor = jnp.linalg.cholesky(matrix[step, step])
        solved = jax.vmap(lambda block_tile: solve_right(block_tile, diag_factor))(matrix[:, step])
        below = indices > step
        panel = jnp.where(below[:, None, None], solved, jnp.float32(0.0))

        def row_update(pair):
            tile_row, left_tile = pair
            product = jnp.einsum('pq,jrq->jpr', left_tile, panel, precision=lax.Precision.HIGHEST)
            return tile_row - product
        matrix = lax.map(row_update, (matrix, panel))
        column = jnp.where(below[:, None, None], panel, matrix[:, step])
        column = column.at[step].set(diag_factor)
        matrix = matrix.at[:, step].set(column)
        upper = (indices > step)[:, None, None]
        matrix = matrix.at[step].set(jnp.where(upper, jnp.float32(0.0), matrix[step]))
    return matrix.reshape(kernel_tiles.shape)
```

```python
import jax
import jax.numpy as jnp
from jax import lax
from jax.experimental import pallas as pl
from jax.experimental.pallas import tpu as pltpu
from jax.sharding import PartitionSpec as P

SUB = 8
BASE = 128
BLOCK = 256
NN = ((1,), (0,))
NT = ((1,), (1,))
TN = ((0,), (0,))
VMEM = pl.BlockSpec(memory_space=pltpu.VMEM)


def dot(a, b, dims, precision=lax.Precision.HIGHEST):
    return lax.dot_general(
        a, b, (dims, ((), ())), precision=precision, preferred_element_type=jnp.float32
    )


def down(x, j):
    return jnp.broadcast_to(x[j : j + 1, :], x.shape)


def along(x, j):
    return jnp.broadcast_to(x[:, j : j + 1], x.shape)


def factor_base(diag):
    sub = lax.broadcasted_iota(jnp.int32, (SUB, BASE), 0)
    lane = lax.broadcasted_iota(jnp.int32, (SUB, BASE), 1)
    count = BASE // SUB
    left = [diag[SUB * t : SUB * t + SUB, :] for t in range(count)]
    right = [(lane == sub + SUB * t).astype(jnp.float32) for t in range(count)]
    upper, inverse = [], []
    for t in range(count):
        a, b = left[t], right[t]
        cols = [along(a, SUB * t + j) for j in range(SUB)]
        ua, ub, pivots = a, b, None
        for j in range(SUB):
            mine = sub == j
            pivot = down(cols[j], j)
            recip = 1.0 / pivot
            if j:
                ua = jnp.where(sub >= j, a, ua)
                ub = jnp.where(sub >= j, b, ub)
                pivots = jnp.where(sub >= j, pivot, pivots)
            else:
                pivots = pivot
            mult = cols[j]
            row = down(a, j) * recip
            a = jnp.where(mine, row, a - mult * row)
            row = down(b, j) * recip
            b = jnp.where(mine, row, b - mult * row)
            for k in range(j + 1, SUB):
                row = down(cols[k], j) * recip
                cols[k] = jnp.where(mine, row, cols[k] - mult * row)
        scale = lax.rsqrt(pivots)
        upper.append(jnp.where(lane >= sub + SUB * t, ua * scale, 0.0))
        inverse.append(ub * scale)
        if t + 1 < count:
            va = [down(a, j) for j in range(SUB)]
            vb = [down(b, j) for j in range(SUB)]
            for i in range(t + 1, count):
                mult = [along(left[i], SUB * t + j) for j in range(SUB)]
                for j in range(SUB):
                    left[i] = left[i] - mult[j] * va[j]
                    right[i] = right[i] - mult[j] * vb[j]
    return jnp.concatenate(upper, 0), jnp.concatenate(inverse, 0)


def factor_kernel(a_ref, f_ref, u_ref, *rest):
    n, m = a_ref.shape
    first, second = pl.ds(0, BASE), pl.ds(BASE, BASE)
    u1, x1 = factor_base(a_ref[first, first])
    u12 = dot(x1, a_ref[first, second], NN)
    u2, x2 = factor_base(a_ref[second, second] - dot(u12, u12, TN))
    x21 = -dot(x2, dot(u12, x1, TN), NN)
    zero = jnp.zeros((BASE, BASE), jnp.float32)
    u_ref[first, first] = u1
    u_ref[first, second] = u12
    u_ref[second, first] = zero
    u_ref[second, second] = u2
    f_ref[first, first] = x1
    f_ref[first, second] = zero
    f_ref[second, first] = x21
    f_ref[second, second] = x2
    x = f_ref[:, :BLOCK]
    for c in range(BLOCK, m, BLOCK):
        f_ref[:, c : c + BLOCK] = dot(x, a_ref[:BLOCK, c : c + BLOCK], NN)
    for r in range(BLOCK, n, BLOCK):
        lhs = f_ref[:, r : r + BLOCK].T
        for c in range(r, m, BLOCK):
            rest[0][r - BLOCK : r, c - BLOCK : c] = a_ref[r : r + BLOCK, c : c + BLOCK] - dot(
                lhs, f_ref[:, c : c + BLOCK], NN
            )


def factor_block(a):
    n, m = a.shape
    shapes = [(BLOCK, m), (BLOCK, BLOCK)]
    if n > BLOCK:
        shapes.append((n - BLOCK, m - BLOCK))
    return pl.pallas_call(
        factor_kernel,
        out_shape=[jax.ShapeDtypeStruct(s, jnp.float32) for s in shapes],
        in_specs=[VMEM],
        out_specs=[VMEM] * len(shapes),
        compiler_params=pltpu.CompilerParams(vmem_limit_bytes=48 << 20),
    )(a)


def schur_kernel(target_ref, *refs):
    out_ref = refs[-1]
    order = target_ref.shape[0]
    for r in range(0, order, BLOCK):
        for c in range(r, order, BLOCK):
            total = target_ref[r : r + BLOCK, c : c + BLOCK]
            for part in refs[:-1]:
                base = part.shape[1] - order
                total = total - dot(
                    part[:, base + r : base + r + BLOCK], part[:, base + c : base + c + BLOCK], TN
                )
            out_ref[r : r + BLOCK, c : c + BLOCK] = total


def schur(target, parts):
    return pl.pallas_call(
        schur_kernel,
        out_shape=jax.ShapeDtypeStruct(target.shape, jnp.float32),
        in_specs=[VMEM] * (1 + len(parts)),
        out_specs=VMEM,
        compiler_params=pltpu.CompilerParams(vmem_limit_bytes=48 << 20),
    )(target, *parts)


def on_owner(owner, fn, *operands):
    shapes = jax.eval_shape(fn, *operands)

    def nothing(*_):
        return jax.tree.map(lambda s: jnp.zeros(s.shape, s.dtype), shapes)

    return lax.cond(owner, fn, nothing, *operands)


def move(value, pairs, cols):
    flat = [(a * cols + b, c * cols + d) for (a, b), (c, d) in pairs]
    return lax.ppermute(value, ("row", "col"), flat)


def doubling(value, axis, root, size):
    reach = 1
    while reach < size:
        pairs = [
            ((root + i) % size, (root + i + reach) % size) for i in range(min(reach, size - reach))
        ]
        value = value + lax.ppermute(value, axis, pairs)
        reach *= 2
    return value


def pair_swap(pairs):
    return pairs + [(b, a) for a, b in pairs]


def spread(value, rows, cols):
    if cols != 4:
        return doubling(doubling(value, "row", 0, rows), "col", 0, cols)
    stages = [
        [((0, 0), (1, 0))],
        [((r, 0), (r, 2)) for r in (0, 1)],
        [((r, c), (r + 2, c)) for r in (0, 1) for c in (0, 2)],
        [((r, c), (r + 2, c)) for r in (2, 3) for c in (0, 2)],
        [((r, c), (r, c + 1)) for r in range(6) for c in (0, 2)],
    ]
    for pairs in stages:
        value = value + move(value, pairs, cols)
    return value


def pick(index, choices):
    return lax.switch(index, [lambda bufs, f=f: f(bufs) for f in choices[0]], choices[1])


def table(entries, rows, cols, row, col):
    flat = [entries.get((r, c), 0) for r in range(rows) for c in range(cols)]
    return jnp.array(flat, jnp.int32)[row * cols + col]


def on_device(kernel_tiles, profile):
    order = kernel_tiles.shape[-1]
    rows, cols = lax.axis_size("row"), lax.axis_size("col")
    row, col = lax.axis_index("row"), lax.axis_index("col")
    blocks = kernel_tiles.reshape(2, order, order)
    near, far = blocks[0], blocks[1]
    edge = cols + 2
    edge_live = profile[0, edge] <= 1
    owner = (row == 0) & (col == 0)
    workers = range(2, edge + 1)
    steps = order // BLOCK

    if cols == 4:
        swap0 = pair_swap([((r, 0), (r, 1)) for r in (0,) + tuple(workers)])
        r1 = move(near, swap0, cols)
        r2 = move(
            near,
            [((r, c), (r, c + 2)) for r in workers for c in (0, 1)] + [((1, 1), (0, 0))],
            cols,
        )
        r3 = move(
            near,
            pair_swap([((4, c), (5, c)) for c in (0, 1)])
            + [((r, c), (r + 4, c)) for r in (0, 1) for c in (2, 3)],
            cols,
        )
        r4 = move(near, [((r, c), (r - 2, c)) for r in (4, 5) for c in (0, 1)], cols)
        r5 = move(r2, pair_swap([((r, 2), (r, 3)) for r in workers]), cols)
        r6a = move(r4, pair_swap([((2, c), (3, c)) for c in (0, 1)]), cols)
        r6b = move(r2, pair_swap([((2, c), (3, c)) for c in (2, 3)]), cols)
        r6c = move(r3, pair_swap([((4, c), (5, c)) for c in (2, 3)]), cols)
        r7a = move(r3, [((4, 0), (4, 1)), ((5, 1), (5, 0))], cols)
        r7b = move(r4, [((2, 1), (2, 0)), ((3, 0), (3, 1))], cols)
        r7c = move(r6a, [((2, 0), (2, 1)), ((3, 1), (3, 0))], cols)
        r7d = move(r6b, [((2, 2), (2, 3)), ((3, 3), (3, 2))], cols)
        tile01, tile11 = r1, r2

        def row_pair():
            low = [lambda b: (b[0], b[1]), lambda b: (b[1], b[0])]
            low += [lambda b: (b[2], b[3]), lambda b: (b[3], b[2])]
            return lax.switch(col, low, (near, r1, r2, r5))

        def col_pair(pair):
            forms = [
                lambda b: b[0],
                lambda b: (b[4], b[8]),
                lambda b: (b[8], b[5]),
                lambda b: (b[5], b[8]),
                lambda b: (b[8], b[4]),
                lambda b: (b[8], b[3]),
                lambda b: (b[3], b[8]),
                lambda b: (b[9], b[6]),
                lambda b: (b[6], b[9]),
                lambda b: (b[3].T, b[7].T),
                lambda b: (b[7].T, b[3].T),
            ]
            entries = {
                (2, 0): 1, (2, 1): 11, (3, 0): 12, (3, 1): 4, (4, 1): 5, (5, 0): 6,
                (2, 3): 7, (3, 2): 8, (4, 2): 9, (4, 3): 9, (5, 2): 10, (5, 3): 10,
            }
            forms += [lambda b: (b[10], b[5]), lambda b: (b[5], b[10])]
            forms[5] = lambda b: (b[11], b[3])
            forms[6] = lambda b: (b[3], b[11])
            bufs = (pair, r1, r2, r3, r4, r6a, r6b, r6c, r7b, r7d, r7c, r7a)
            return lax.switch(table(entries, rows, cols, row, col), forms, bufs)
    else:
        zero = jnp.zeros_like(near)
        left0 = doubling(jnp.where(col == 0, near, zero), "col", 0, cols)
        left1 = doubling(jnp.where(col == 1, near, zero), "col", 1, cols)
        mine = jnp.where(col < 2, far, near)
        top0 = doubling(jnp.where(row == 0, mine, zero), "row", 0, rows)
        top1 = doubling(jnp.where(row == 1, mine, zero), "row", 1, rows)
        tile01 = move(near, [((0, 1), (0, 0))], cols)
        tile11 = move(near, [((1, 1), (0, 0))], cols)

        def row_pair():
            return left0, left1

        def col_pair(pair):
            return top0.T, top1.T

    def start(tile00, tile01):
        return tuple(factor_block(jnp.concatenate([tile00, tile01], 1)))

    def go_on(state):
        return tuple(factor_block(state))

    own0, diag0, pieces0 = [], [], []
    out = on_owner(owner, start, near, tile01)
    for p in range(steps):
        if p:
            out = on_owner(owner, go_on, out[2])
        own0.append(out[0])
        diag0.append(out[1])
        pieces0.append(spread(out[0], rows, cols))
    own1, diag1, pieces1 = [], [], []
    out = on_owner(owner, lambda t, *f: tuple(factor_block(schur(t, f))), tile11, *own0)
    for p in range(steps):
        if p:
            out = on_owner(owner, go_on, out[2])
        own1.append(out[0])
        diag1.append(out[1])
        pieces1.append(spread(out[0], rows, cols))
    corner = move(jnp.concatenate(diag1, 0), [((0, 0), (1, 1))], cols)

    def edge_tiles(args):
        near, j0, j1 = args
        pairs = [((edge - 2, c), (edge, c)) for c in range(cols)]
        tile = jnp.zeros_like(near)
        for r in range(2, edge + 1):
            tile = tile + move(near, [((edge, 1), (r, 2))], cols)
        return move(j0, pairs, cols), move(j1, pairs, cols), tile

    def edge_pieces(args):
        pairs = [((edge - 2, c), (edge, c)) for c in range(cols)]
        return tuple(move(f, pairs, cols) for f in args)

    is_worker = (row >= 2) & ((row < edge) | ((row == edge) & edge_live))

    def gather_pairs(_):
        pair = row_pair()
        return pair + tuple(col_pair(pair))

    def no_pairs(_):
        return (jnp.zeros_like(near),) * 4

    i0, i1, j0, j1 = lax.cond(is_worker, gather_pairs, no_pairs, 0)

    def with_edge(args):
        j0, j1, pieces = args
        e0, e1, tile = edge_tiles((near, j0, j1))
        if cols == 4:
            moved = edge_pieces(pieces)
            pieces = tuple(jnp.where(row == edge, m, f) for m, f in zip(moved, pieces))
        return jnp.where(row == edge, e0, j0), jnp.where(row == edge, e1, j1), tile, pieces

    def without_edge(args):
        j0, j1, pieces = args
        return j0, j1, jnp.zeros_like(near), pieces

    pieces = tuple(pieces0 + pieces1)
    j0, j1, edge_tile, pieces = lax.cond(edge_live, with_edge, without_edge, (j0, j1, pieces))

    def eliminate(panel, pieces):
        done = []
        for f in pieces:
            part = dot(panel[:, :BLOCK], f[:, :BLOCK], NT, lax.Precision.HIGH)
            done.append(part)
            if f.shape[1] > BLOCK:
                panel = panel[:, BLOCK:] - dot(part, f[:, BLOCK:], NN, lax.Precision.HIGH)
        return jnp.concatenate(done, 1)

    def work(args):
        i0, i1, j0, j1, edge_tile, pieces = args
        stacked = jnp.concatenate(
            [jnp.concatenate([i0, i1], 1), jnp.concatenate([j0, j1], 1)], 0
        )
        panel = eliminate(stacked, pieces)
        mine, other = panel[:order], panel[order:]
        target = jnp.where(col < 2, far, near) - dot(mine, other, NT, lax.Precision.HIGH)

        def edge_update(_):
            last = eliminate(edge_tile, pieces[steps:])
            return far - dot(mine[:, order:], last, NT, lax.Precision.HIGH)

        beyond = lax.cond(edge_live & (col == 2), edge_update, lambda _: far, 0)
        solved = jnp.where(col == 0, mine[:, :order], mine[:, order:])
        return jnp.stack(
            [jnp.where(col < 2, solved, target), jnp.where(col < 2, target, beyond)]
        )

    def lower(tops, diagonals):
        parts = []
        for p in range(steps):
            end = order - p * BLOCK
            parts.append(
                jnp.concatenate(
                    [jnp.zeros((BLOCK, p * BLOCK), jnp.float32), diagonals[p], tops[p][:, BLOCK:end]],
                    1,
                )
            )
        return jnp.concatenate(parts, 0).T

    def finish_top(args):
        pieces, own0, diag0, corner = args
        zero = jnp.zeros_like(near)
        kinds = [
            lambda: zero,
            lambda: lower(own0, diag0),
            lambda: jnp.concatenate([f[:, -order:] for f in pieces[:steps]], 0).T,
            lambda: lower(pieces[steps:], [corner[p * BLOCK : (p + 1) * BLOCK] for p in range(steps)]),
        ]
        kind = table({(0, 0): 1, (1, 0): 2, (1, 1): 3}, rows, cols, row, col)
        return jnp.stack([lax.switch(kind, kinds), zero])

    def finish_rest(args):
        return lax.cond(row < 2, finish_top, lambda _: blocks, args)

    result = lax.cond(
        is_worker,
        lambda a, b: work(a),
        lambda a, b: finish_rest(b),
        (i0, i1, j0, j1, edge_tile, pieces),
        (pieces, tuple(own0), tuple(diag0), corner),
    )
    return result.reshape(kernel_tiles.shape)


def solution(mesh):
    placed = (P(None, "row", None, "col", None, None), P())
    return jax.shard_map(
        on_device,
        mesh=mesh,
        in_specs=placed,
        out_specs=P(None, "row", None, "col", None, None),
        check_vma=False,
    )
```

```python
import jax
import jax.numpy as jnp
from jax import lax
from jax.experimental import pallas as pl
from jax.experimental.pallas import tpu as pltpu
from jax.sharding import PartitionSpec as P

SUB = 8
BASE = 128
BLOCK = 256
FIRST = (2, 4)
SECOND = (5, 7)
THIRD = (8,)
NN = ((1,), (0,))
NT = ((1,), (1,))
TN = ((0,), (0,))
ANY = pl.BlockSpec(memory_space=pl.ANY)
SMEM = pl.BlockSpec(memory_space=pltpu.SMEM)
DMA = pltpu.SemaphoreType.DMA
F32 = jnp.float32


def dot(a, b, dims, precision=lax.Precision.HIGHEST):
    return lax.dot_general(
        a, b, (dims, ((), ())), precision=precision, preferred_element_type=jnp.float32
    )


def down(x, j):
    return jnp.broadcast_to(x[j : j + 1, :], x.shape)


def along(x, j):
    return jnp.broadcast_to(x[:, j : j + 1], x.shape)


def factor_base(diag):
    sub = lax.broadcasted_iota(jnp.int32, (SUB, BASE), 0)
    lane = lax.broadcasted_iota(jnp.int32, (SUB, BASE), 1)
    count = BASE // SUB
    left = [diag[SUB * t : SUB * t + SUB, :] for t in range(count)]
    right = [(lane == sub + SUB * t).astype(jnp.float32) for t in range(count)]
    upper, inverse = [], []
    for t in range(count):
        a, b = left[t], right[t]
        cols = [along(a, SUB * t + j) for j in range(SUB)]
        ua, ub, pivots = a, b, None
        for j in range(SUB):
            mine = sub == j
            pivot = down(cols[j], j)
            recip = 1.0 / pivot
            if j:
                ua = jnp.where(sub >= j, a, ua)
                ub = jnp.where(sub >= j, b, ub)
                pivots = jnp.where(sub >= j, pivot, pivots)
            else:
                pivots = pivot
            mult = cols[j]
            row = down(a, j) * recip
            a = jnp.where(mine, row, a - mult * row)
            row = down(b, j) * recip
            b = jnp.where(mine, row, b - mult * row)
            for k in range(j + 1, SUB):
                row = down(cols[k], j) * recip
                cols[k] = jnp.where(mine, row, cols[k] - mult * row)
        scale = lax.rsqrt(pivots)
        upper.append(jnp.where(lane >= sub + SUB * t, ua * scale, 0.0))
        inverse.append(ub * scale)
        if t + 1 < count:
            va = [down(a, j) for j in range(SUB)]
            vb = [down(b, j) for j in range(SUB)]
            for i in range(t + 1, count):
                mult = [along(left[i], SUB * t + j) for j in range(SUB)]
                for j in range(SUB):
                    left[i] = left[i] - mult[j] * va[j]
                    right[i] = right[i] - mult[j] * vb[j]
    return jnp.concatenate(upper, 0), jnp.concatenate(inverse, 0)


def params(limit_mib=48):
    return pltpu.CompilerParams(vmem_limit_bytes=limit_mib << 20)


def shape(*dims):
    return jax.ShapeDtypeStruct(dims, F32)


def factor_kernel(kind, flag_ref, *refs):
    refs = list(refs)
    sources = [refs.pop(0) for _ in range({"first": 3, "next": 1, "schur": 6}[kind])]
    a_ref, f_ref, sems = refs[-3:]
    f_out = refs[0]
    rest_out = refs[1] if len(refs) > 4 else None
    n, m = a_ref.shape
    top, below = pl.ds(0, BLOCK), pl.ds(BLOCK, n - BLOCK)

    @pl.when(flag_ref[0] == 1)
    def _():
        copies = []

        def load(source, target):
            copies.append(pltpu.make_async_copy(source, target, sems.at[len(copies)]))
            copies[-1].start()

        if kind == "first":
            left, right, cut = pl.ds(0, n), pl.ds(n, n), n // 2 - BLOCK
            load(sources[0].at[0, top], a_ref.at[top, left])
            load(sources[1].at[top], a_ref.at[top, right])
            load(sources[0].at[0, below], a_ref.at[below, left])
            load(sources[1].at[pl.ds(BLOCK, cut)], a_ref.at[pl.ds(BLOCK, cut), right])
            load(sources[2], a_ref.at[pl.ds(n // 2, n // 2), right])
            needed = 2
        elif kind == "next":
            load(sources[0].at[top], a_ref.at[top])
            if n > BLOCK:
                load(sources[0].at[below], a_ref.at[below])
            needed = 1
        else:
            parts = refs[-4]
            for h in range(2):
                load(sources[h], a_ref.at[pl.ds(h * n // 2, n // 2)])
            for p, part in enumerate(sources[2:]):
                load(
                    part.at[:, pl.ds(part.shape[1] - n, n)],
                    parts.at[pl.ds(p * BLOCK, BLOCK)],
                )
            needed = len(copies)
        for copy in copies[:needed]:
            copy.wait()
        if kind == "schur":
            for r in range(0, n, BLOCK):
                lhs = parts[:, r : r + BLOCK].T
                for c in range(r, n, BLOCK):
                    a_ref[r : r + BLOCK, c : c + BLOCK] -= dot(lhs, parts[:, c : c + BLOCK], NN)

        first, second = pl.ds(0, BASE), pl.ds(BASE, BASE)
        sub = lax.broadcasted_iota(jnp.int32, (BASE, BASE), 0)
        lane = lax.broadcasted_iota(jnp.int32, (BASE, BASE), 1)
        x_ref = refs[-4] if kind != "schur" else refs[-5]

        def base(b, carry):
            rows = pl.ds(pl.multiple_of(b * BASE, BASE), BASE)
            u, x = factor_base(a_ref[rows, rows])
            f_ref[rows, rows] = jnp.where(sub <= lane, u, x)
            x_ref[rows, rows] = x

            @pl.when(b == 0)
            def _():
                u12 = dot(x, a_ref[first, second], NN)
                f_ref[first, second] = u12
                a_ref[second, second] -= dot(u12, u12, TN)

            return carry

        lax.fori_loop(0, BLOCK // BASE, base, 0)
        x21 = -dot(x_ref[second, second], dot(f_ref[first, second], x_ref[first, first], TN), NN)
        f_ref[second, first] = x21
        x_ref[second, first] = x21
        x_ref[first, second] = jnp.zeros((BASE, BASE), F32)
        x = x_ref[...]
        for c in range(BLOCK, m, BLOCK):
            f_ref[:, c : c + BLOCK] = dot(x, a_ref[top, c : c + BLOCK], NN)
        leaving = [pltpu.make_async_copy(f_ref, f_out, sems.at[len(copies)])]
        leaving[0].start()
        for copy in copies[needed:]:
            copy.wait()
        for r in range(BLOCK, n, BLOCK):
            lhs = f_ref[:, r : r + BLOCK].T
            for c in range(r, m, BLOCK):
                a_ref[r : r + BLOCK, c : c + BLOCK] -= dot(lhs, f_ref[:, c : c + BLOCK], NN)
            rows = pl.ds(r, BLOCK)
            leaving.append(
                pltpu.make_async_copy(
                    a_ref.at[rows, pl.ds(BLOCK, m - BLOCK)],
                    rest_out.at[pl.ds(r - BLOCK, BLOCK)],
                    sems.at[len(copies) + len(leaving)],
                )
            )
            leaving[-1].start()
        for copy in leaving:
            copy.wait()


def factor_block(kind, flag, n, m, *sources):
    shapes = [shape(BLOCK, m)]
    if n > BLOCK:
        shapes.append(shape(n - BLOCK, m - BLOCK))
    scratch = [pltpu.VMEM((BLOCK, BLOCK), F32)]
    if kind == "schur":
        scratch.append(pltpu.VMEM((n, n), F32))
    scratch += [pltpu.VMEM((n, m), F32), pltpu.VMEM((BLOCK, m), F32), DMA((12,))]
    out = pl.pallas_call(
        lambda *refs: factor_kernel(kind, *refs),
        out_shape=shapes,
        in_specs=[SMEM] + [ANY] * len(sources),
        out_specs=[ANY] * len(shapes),
        scratch_shapes=scratch,
        cost_estimate=pl.CostEstimate(
            flops=2_000_000_000, bytes_accessed=8 * n * m, transcendentals=0
        ),
        compiler_params=params(),
    )(flag, *sources)
    return out if n > BLOCK else (out[0], None)


def choose(index, options):
    def kernel(index_ref, *refs):
        *bufs, out_ref, sem = refs
        for k, buf in enumerate(bufs):

            @pl.when(index_ref[0] == k)
            def _():
                copy = pltpu.make_async_copy(buf, out_ref, sem)
                copy.start()
                copy.wait()

    return pl.pallas_call(
        kernel,
        out_shape=shape(*options[0].shape),
        in_specs=[SMEM] + [ANY] * len(options),
        out_specs=ANY,
        scratch_shapes=[DMA(())],
    )(index, *options)


def unset(like):
    return pl.pallas_call(
        lambda out_ref: None, out_shape=shape(*like.shape), in_specs=[], out_specs=ANY
    )()


def patch(flags, result, parts):
    def kernel(flags_ref, result_ref, *refs):
        *bufs, out_ref, sems = refs
        for k, buf in enumerate(bufs):

            @pl.when(flags_ref[k] == 1)
            def _():
                copy = pltpu.make_async_copy(buf, out_ref.at[k], sems.at[k])
                copy.start()
                copy.wait()

    return pl.pallas_call(
        kernel,
        out_shape=shape(*result.shape),
        in_specs=[SMEM] + [ANY] * (1 + len(parts)),
        out_specs=ANY,
        scratch_shapes=[DMA((len(parts),))],
        input_output_aliases={1: 0},
    )(flags, result, *parts)


def split(x):
    high = x.astype(jnp.bfloat16)
    return high, (x - high.astype(F32)).astype(jnp.bfloat16)


def dot3(a, b, dims):
    total = None
    for x, y in ((a[1], b[0]), (a[0], b[1]), (a[0], b[0])):
        part = lax.dot_general(x, y, (dims, ((), ())), preferred_element_type=F32)
        total = part if total is None else total + part
    return total


PASS, WORK, ZERO, LOWER0, PANEL0, LOWER1 = range(6)


def finish_kernel(n_raw, n_sets, meta_ref, *refs):
    tiles_ref, raws, refs = refs[0], refs[1 : 1 + n_raw], refs[1 + n_raw :]
    order = tiles_ref.shape[-1]
    steps = order // BLOCK
    count = 2 * steps
    sets = [refs[k * count : (k + 1) * count] for k in range(n_sets)]
    out_ref, p1_ref, z, t, high, low, *fs, sems = refs[n_sets * count :]
    role, transposed, which, col, edge = (meta_ref[k] for k in (0, 5, 6, 7, 8))
    half = pl.ds(0, order), pl.ds(order, order)
    mid = order // 2
    sources = [
        [tiles_ref.at[0, pl.ds(h * mid, mid)]] + [raws[2 * k + h] for k in range(n_raw // 2)]
        for h in range(2)
    ]

    def load_pieces(pieces):
        for k in range(n_sets):

            @pl.when(which == k)
            def _():
                for p in pieces:
                    pltpu.make_async_copy(sets[k][p], fs[p], sems.at[8 + p]).start()

    def await_piece(p):
        pltpu.make_async_copy(sets[0][p], fs[p], sems.at[8 + p]).wait()

    def move_out(source, target, sem):
        copy = pltpu.make_async_copy(source, target, sems.at[sem])
        copy.start()
        return copy

    @pl.when(role == PASS)
    def _():
        copies = [move_out(tiles_ref.at[k], out_ref.at[k], k) for k in range(2)]
        for copy in copies:
            copy.wait()

    @pl.when(role >= ZERO)
    def _():
        t[...] = jnp.zeros((order, order), F32)
        move_out(t, out_ref.at[1], 1).wait()

        def upper_block(p, q, lead):
            base = lead + (q - p) * BLOCK
            return fs[p][:, base : base + BLOCK].T

        def triangle(offset):
            sub = lax.broadcasted_iota(jnp.int32, (BLOCK, BLOCK), 0)
            lane = lax.broadcasted_iota(jnp.int32, (BLOCK, BLOCK), 1)
            for p in range(steps):
                for q in range(p, steps):
                    block = fs[offset + p][:, (q - p) * BLOCK : (q - p + 1) * BLOCK]
                    if p == q:
                        block = jnp.where(sub <= lane, block, 0.0)
                    t[q * BLOCK : (q + 1) * BLOCK, p * BLOCK : (p + 1) * BLOCK] = block.T

        for kind, pieces in (
            (LOWER0, range(steps)),
            (PANEL0, range(steps)),
            (LOWER1, range(steps, count)),
        ):

            @pl.when(role == kind)
            def _():
                load_pieces(pieces)
                for p in pieces:
                    await_piece(p)
                if kind == PANEL0:
                    for p in range(steps):
                        for q in range(steps):
                            t[q * BLOCK : (q + 1) * BLOCK, p * BLOCK : (p + 1) * BLOCK] = (
                                upper_block(p, q, order - p * BLOCK + p * BLOCK)
                            )
                else:
                    triangle(pieces[0])

        move_out(t, out_ref.at[0], 0).wait()

    @pl.when(role == WORK)
    def _():
        places = [
            [z.at[pl.ds(a * order + h * mid, mid), pl.ds(b * order, order)] for h in range(2)]
            for a in range(2)
            for b in range(2)
        ]
        for s, place in enumerate(places):
            for k in range(len(sources[0])):

                @pl.when(meta_ref[1 + s] == k)
                def _():
                    for h in range(2):
                        sem = sems.at[8 + count + 2 * s + h]
                        pltpu.make_async_copy(sources[h][k], place[h], sem).start()

        load_pieces(range(count))
        for slot, taken in ((1, col < 2), (0, col >= 2)):

            @pl.when(taken)
            def _():
                pltpu.make_async_copy(tiles_ref.at[slot], t, sems.at[4]).start()

        @pl.when(col >= 2)
        def _():
            move_out(tiles_ref.at[1], out_ref.at[1], 5)

        for s, place in enumerate(places):
            for h in range(2):
                sem = sems.at[8 + count + 2 * s + h]
                pltpu.make_async_copy(sources[h][1], place[h], sem).wait()

        @pl.when(transposed == 1)
        def _():
            for left in (0, order):
                for a in range(steps):
                    for b in range(a, steps):
                        ra = order + a * BLOCK, left + a * BLOCK
                        rb = order + b * BLOCK, left + b * BLOCK
                        upper = z[ra[0] : ra[0] + BLOCK, rb[1] : rb[1] + BLOCK].T
                        if a != b:
                            z[ra[0] : ra[0] + BLOCK, rb[1] : rb[1] + BLOCK] = z[
                                rb[0] : rb[0] + BLOCK, ra[1] : ra[1] + BLOCK
                            ].T
                        z[rb[0] : rb[0] + BLOCK, ra[1] : ra[1] + BLOCK] = upper

        sub = lax.broadcasted_iota(jnp.int32, (BLOCK, BLOCK), 0)
        lane = lax.broadcasted_iota(jnp.int32, (BLOCK, BLOCK), 1)
        for p in range(count):
            await_piece(p)
            packed = fs[p][:, :BLOCK]
            inverse = jnp.where(
                sub > lane, packed, jnp.where(sub == lane, 1.0 / packed, 0.0)
            )
            inverse = split(inverse)
            for rows in half:
                solved = dot3(
                    split(z[rows, p * BLOCK : (p + 1) * BLOCK]), inverse, NT
                )
                z[rows, p * BLOCK : (p + 1) * BLOCK] = solved
                solved = split(solved)
                high[rows, :] = solved[0]
                low[rows, :] = solved[1]

            def eliminate(q, carry):
                to = pl.ds(pl.multiple_of(q * BLOCK, BLOCK), BLOCK)
                u = split(fs[p][:, pl.ds(pl.multiple_of((q - p) * BLOCK, BLOCK), BLOCK)])
                for rows in half:
                    z[rows, to] -= dot3((high[rows, :], low[rows, :]), u, NN)
                return carry

            lax.fori_loop(p + 1, count, eliminate, 0)
            if p == 0:
                pltpu.make_async_copy(tiles_ref.at[0], t, sems.at[4]).wait()

            def update(r, carry):
                rows = pl.ds(pl.multiple_of(r * BLOCK, BLOCK), BLOCK)
                others = high[half[1], :], low[half[1], :]
                t[rows, :] -= dot3((high[rows, :], low[rows, :]), others, NT)
                return carry

            lax.fori_loop(0, steps, update, 0)

        @pl.when(col == 0)
        def _():
            move_out(z.at[half[0], half[0]], out_ref.at[0], 5)

        @pl.when(col == 1)
        def _():
            move_out(z.at[half[0], half[1]], out_ref.at[0], 5)

        for slot, taken in ((1, col < 2), (0, col >= 2)):

            @pl.when(taken)
            def _():
                move_out(t, out_ref.at[slot], 6)

        @pl.when((col == 2) & (edge == 1))
        def _():
            move_out(z.at[half[0], half[1]], p1_ref, 7).wait()

        pltpu.make_async_copy(t, out_ref.at[0], sems.at[5]).wait()
        pltpu.make_async_copy(t, out_ref.at[0], sems.at[6]).wait()


def finish(meta, tiles, raws, sets):
    order = tiles.shape[-1]
    count = len(sets[0])
    flat = [f for s in sets for f in s]
    scratch = [
        pltpu.VMEM((2 * order, 2 * order), F32),
        pltpu.VMEM((order, order), F32),
        pltpu.VMEM((2 * order, BLOCK), jnp.bfloat16),
        pltpu.VMEM((2 * order, BLOCK), jnp.bfloat16),
    ]
    scratch += [pltpu.VMEM(f.shape, F32) for f in sets[0]] + [DMA((16 + count,))]
    return pl.pallas_call(
        lambda *refs: finish_kernel(len(raws), len(sets), *refs),
        out_shape=[shape(*tiles.shape), shape(order, order)],
        in_specs=[SMEM] + [ANY] * (1 + len(raws) + len(flat)),
        out_specs=[ANY, ANY],
        scratch_shapes=scratch,
        cost_estimate=pl.CostEstimate(
            flops=60_000_000_000, bytes_accessed=64 << 20, transcendentals=0
        ),
        compiler_params=params(56),
    )(meta, tiles, *raws, *flat)


def move(value, pairs, cols):
    if isinstance(value, list):
        return [move(v, pairs, cols) for v in value]
    flat = [(a * cols + b, c * cols + d) for (a, b), (c, d) in pairs]
    return lax.ppermute(value, ("row", "col"), flat)


def doubling(value, axis, root, size):
    place = lax.rem(lax.axis_index(axis) - root + size, size)
    reach = 1
    while reach < size:
        pairs = [
            ((root + i) % size, (root + i + reach) % size) for i in range(min(reach, size - reach))
        ]
        value = jnp.where(place >= reach, lax.ppermute(value, axis, pairs), value)
        reach *= 2
    return value


def both_ways(pairs):
    return pairs + [(b, a) for a, b in pairs]


def eliminate_last(panel, pieces):
    done = []
    for f in pieces:
        packed = f[:, :BLOCK]
        inverse = jnp.tril(packed, -1) + jnp.diag(1.0 / jnp.diagonal(packed))
        part = dot(panel[:, :BLOCK], inverse, NT, lax.Precision.HIGH)
        done.append(part)
        if f.shape[1] > BLOCK:
            panel = panel[:, BLOCK:] - dot(part, f[:, BLOCK:], NN, lax.Precision.HIGH)
    return jnp.concatenate(done, 1)


def on_device(kernel_tiles, profile):
    order = kernel_tiles.shape[-1]
    rows, cols = lax.axis_size("row"), lax.axis_size("col")
    row, col = lax.axis_index("row"), lax.axis_index("col")
    tiles = kernel_tiles.reshape(2, order, order)
    near = [tiles[0, h * order // 2 : (h + 1) * order // 2] for h in range(2)]
    steps = order // BLOCK
    count = 2 * steps
    edge = cols + 2
    edge_live = profile[0, edge] <= 1
    owner = jnp.reshape(((row == 0) & (col == 0)).astype(jnp.int32), (1,))
    workers = range(2, edge)
    routed = cols == 4

    plan = [[[PASS, 0, 0, 0, 0, 0, 0, 0, 0, -1, -1, -1] for _ in range(cols)] for _ in range(rows)]
    for r in range(rows):
        for c in range(cols):
            plan[r][c][7] = c
            if r < 2:
                plan[r][c][0] = ZERO
            elif r < edge:
                plan[r][c][0] = WORK
    plan[0][0][0], plan[1][0][0], plan[1][1][0] = LOWER0, PANEL0, LOWER1

    if routed:
        r1 = move(near, both_ways([((r, 0), (r, 1)) for r in (0,) + tuple(workers)]), cols)
        r2 = move(
            near,
            [((r, c), (r, c + 2)) for r in workers for c in (0, 1)]
            + [((1, 1), (0, 0)), ((edge, 1), (edge, 3))],
            cols,
        )
        r3 = move(
            near,
            both_ways([((4, c), (5, c)) for c in (0, 1)])
            + [((r, c), (r + 4, c)) for r in (0, 1) for c in (2, 3)],
            cols,
        )
        r4 = move(near, [((r, c), (r - 2, c)) for r in (4, 5) for c in (0, 1)], cols)
        tile01 = r1
        for r in workers:
            plan[r][0][1:3] = [0, 1]
            plan[r][1][1:3] = [1, 0]
            plan[r][2][1:3] = [2, 5]
            plan[r][3][1:3] = [5, 2]
            for c in range(4):
                plan[r][c][3:5] = plan[r][c][1:3]
        for place, pair in {
            (2, 0): (4, 10), (2, 1): (11, 6), (3, 0): (6, 11), (3, 1): (10, 4),
            (4, 1): (9, 3), (5, 0): (3, 9), (2, 3): (12, 7), (3, 2): (7, 12),
            (4, 2): (3, 8), (4, 3): (3, 8), (5, 2): (8, 3), (5, 3): (8, 3),
        }.items():
            plan[place[0]][place[1]][3:5] = pair
        for r in (4, 5):
            for c in (2, 3):
                plan[r][c][5] = 1
        plan[1][1][6] = 1
        for r in workers:
            plan[r][1][6] = plan[r][3][6] = 2 if r < 4 else 3
            plan[r][3][6] = 4
        for r in (1,) + tuple(workers):
            plan[r][0][6] = plan[r][2][6] = 5
        plan[0][1][9], plan[1][1][9] = 0, 1
        for r in workers:
            plan[r][1][10] = 0 if r < 4 else 1
            plan[r][1][11] = 1 if r < 4 else 2
            plan[r][3][11] = 3
        plan[1][1][11] = 0
    else:
        mine = jnp.where(col < 2, tiles[1], tiles[0])
        mine = [mine[: order // 2], mine[order // 2 :]]
        left0 = [doubling(v, "col", 0, cols) for v in near]
        left1 = [doubling(v, "col", 1, cols) for v in near]
        top0 = [doubling(v, "row", 0, rows) for v in mine]
        top1 = [doubling(v, "row", 1, rows) for v in mine]
        tile01 = move(near, [((0, 1), (0, 0))], cols)
        tile11 = move(near, [((1, 1), (0, 0))], cols)
        raws = left0 + left1 + top0 + top1
        for r in range(rows):
            for c in range(cols):
                plan[r][c][1:6] = [1, 2, 3, 4, 1]
    meta = jnp.array(plan, jnp.int32)[row, col]
    meta = meta.at[8].set(edge_live.astype(jnp.int32))

    pieces, copies, state = [], [], None
    r5, r6a, r6b, r6c, e1, r7a, r7b, r7c, r7d = ([] for _ in range(9))
    stages = 6 if routed else 0
    late = []
    for slot in range(count + stages):
        arrived = []
        if slot < count:
            step, local = divmod(slot, steps)
            n = order - local * BLOCK
            if slot == 0:
                args = ("first", owner, n, 2 * n, tiles, *tile01)
            elif local == 0:
                args = ("schur", owner, n, n, *(r2 if routed else tile11), *pieces)
            else:
                args = ("next", owner, n, n + (1 - step) * order, state)
            piece, state = factor_block(*args)
            pieces.append(piece)
            copies.append([])
            if not routed:
                copies[-1].append(doubling(doubling(piece, "row", 0, rows), "col", 0, cols))
        if not routed:
            continue
        for k in range(1, stages + 1):
            p = slot - k
            if not 0 <= p < count:
                continue
            got = copies[p]
            if k == 1:
                got.append(move(pieces[p], [((0, 0), (0, 1))], cols))
            elif k == 2:
                got.append(move(got[0], [((0, 1), (1, 1))], cols))
            elif k == 3:
                via = choose(meta[9:10], [got[0], got[1]])
                got.append(move(via, [((r, 1), (r + 2, 1)) for r in (0, 1)], cols))
            elif k == 4:
                got.append(move(got[2], [((r, 1), (r + 2, 1)) for r in (2, 3)], cols))
            elif k == 5:
                via = choose(meta[10:11], [got[2], got[3]])
                got.append(move(via, [((r, 1), (r, 3)) for r in workers], cols))
            else:
                via = choose(meta[11:12], [got[1], got[2], got[3], got[4]])
                got.append(
                    move(
                        via,
                        [((r, c), (r, c - 1)) for r in workers for c in (1, 3)]
                        + [((1, 1), (1, 0))],
                        cols,
                    )
                )
            arrived.append(p)
        late = {
            FIRST[0]: lambda: [r2[0], r3[0], r4[0]],
            FIRST[1]: lambda: [r2[1], r3[1], r4[1]],
            SECOND[0]: lambda: [r5[0], r6a[0], r6b[0], r6c[0], e1[0]],
            SECOND[1]: lambda: [r5[1], r6a[1], r6b[1], r6c[1], e1[1]],
            THIRD[0]: lambda: [r7a[0], r7b[0], r7c[0], r7d[0]],
        }.get(slot, list)()
        last = [copies[p][-1] for p in arrived]
        flowing = ([pieces[slot]] if slot < count else []) + ([] if state is None else [state])
        flowing, last, late = lax.optimization_barrier((flowing, last, late))
        if slot < count:
            pieces[slot] = flowing[0]
        if state is not None:
            state = flowing[-1]
        for p, value in zip(arrived, last):
            copies[p][-1] = value
        for h in range(2):
            if slot == FIRST[h]:
                r2[h], r3[h], r4[h] = late
                r5.append(move(r2[h], both_ways([((r, 2), (r, 3)) for r in workers]), cols))
                r6a.append(move(r4[h], both_ways([((2, c), (3, c)) for c in (0, 1)]), cols))
                r6b.append(move(r2[h], both_ways([((2, c), (3, c)) for c in (2, 3)]), cols))
                r6c.append(move(r3[h], both_ways([((4, c), (5, c)) for c in (2, 3)]), cols))
                e1.append(move(r2[h], [((edge, 3), (edge - 2, 2))], cols))
            elif slot == SECOND[h]:
                r5[h], r6a[h], r6b[h], r6c[h], e1[h] = late
                r7a.append(move(r3[h], [((4, 0), (4, 1)), ((5, 1), (5, 0))], cols))
                r7b.append(move(r4[h], [((2, 1), (2, 0)), ((3, 0), (3, 1))], cols))
                r7c.append(move(r6a[h], [((2, 0), (2, 1)), ((3, 1), (3, 0))], cols))
                r7d.append(move(r6b[h], [((2, 2), (2, 3)), ((3, 3), (3, 2))], cols))
        if slot == THIRD[0]:
            r7a[0], r7b[0], r7c[0], r7d[0] = late

    if routed:
        sets = [pieces] + [[got[k] for got in copies] for k in (1, 2, 3, 4, 5)]
        raws = r1 + r2 + r3 + r4 + r5 + r6a + r6b + r6c + r7a + r7b + r7c + r7d
    else:
        sets = [[got[0] for got in copies]]

    def fetch(tile):
        if routed:
            e2 = move(tile, [((edge - 2, 2), (edge - 4, 2))], cols)
            e3 = move(tile + e2, [((r, 2), (r + 1, 2)) for r in (2, 4)], cols)
            return tile + e2 + e3
        total = jnp.zeros_like(tile)
        for r in workers:
            total = total + move(tile, [((edge, 1), (r, 2))], cols)
        return total

    result, panel1 = finish(meta, tiles, raws, sets)

    def edge_parts(args):
        panel1, edge_tile, last_pieces = args
        far = tiles[1]
        edge_tile = fetch(jnp.concatenate(edge_tile, 0))
        last = eliminate_last(edge_tile, last_pieces)
        column = far - dot(panel1, last, NT, lax.Precision.HIGH)
        sent = move(column, [((r, 2), (edge, r % cols)) for r in workers], cols).T
        solved = move(last, [((edge - 2, 2), (edge, 1)), ((edge - 1, 2), (edge, 2))], cols)
        corner = far - dot(solved, solved, NT, lax.Precision.HIGH)
        part0 = jnp.where(col == 1, solved, sent)
        part1 = jnp.where(row == edge, jnp.where(col == 2, corner, sent), column)
        return part0, part1

    def no_edge(args):
        return unset(tiles[0]), unset(tiles[0])

    parts = lax.cond(edge_live, edge_parts, no_edge, (panel1, e1 if routed else near, sets[-1][steps:]))
    at_edge = edge_live & (row == edge)
    flags = jnp.stack(
        [
            at_edge & (col >= 1),
            (at_edge & (col <= 2)) | (edge_live & (row >= 2) & (row < edge) & (col == 2)),
        ]
    ).astype(jnp.int32)
    return patch(flags, result, parts).reshape(kernel_tiles.shape)


def solution(mesh):
    placed = (P(None, "row", None, "col", None, None), P())
    return jax.shard_map(
        on_device,
        mesh=mesh,
        in_specs=placed,
        out_specs=P(None, "row", None, "col", None, None),
        check_vma=False,
    )
```

```python
import jax
import jax.numpy as jnp
from jax import lax
from jax.experimental import pallas as pl
from jax.experimental.pallas import tpu as pltpu
from jax.sharding import PartitionSpec as P

SUB = 8
BASE = 128
BLOCK = 256
FIRST = 3
SECOND = 6
THIRD = 8
NN = ((1,), (0,))
NT = ((1,), (1,))
TN = ((0,), (0,))
ANY = pl.BlockSpec(memory_space=pl.ANY)
SMEM = pl.BlockSpec(memory_space=pltpu.SMEM)
DMA = pltpu.SemaphoreType.DMA
F32 = jnp.float32


def dot(a, b, dims, precision=lax.Precision.HIGHEST):
    return lax.dot_general(
        a, b, (dims, ((), ())), precision=precision, preferred_element_type=jnp.float32
    )


def down(x, j):
    return jnp.broadcast_to(x[j : j + 1, :], x.shape)


def along(x, j):
    return jnp.broadcast_to(x[:, j : j + 1], x.shape)


def factor_base(diag):
    sub = lax.broadcasted_iota(jnp.int32, (SUB, BASE), 0)
    lane = lax.broadcasted_iota(jnp.int32, (SUB, BASE), 1)
    count = BASE // SUB
    left = [diag[SUB * t : SUB * t + SUB, :] for t in range(count)]
    right = [(lane == sub + SUB * t).astype(jnp.float32) for t in range(count)]
    upper, inverse = [], []
    for t in range(count):
        a, b = left[t], right[t]
        cols = [along(a, SUB * t + j) for j in range(SUB)]
        ua, ub, pivots = a, b, None
        for j in range(SUB):
            mine = sub == j
            pivot = down(cols[j], j)
            recip = 1.0 / pivot
            if j:
                ua = jnp.where(sub >= j, a, ua)
                ub = jnp.where(sub >= j, b, ub)
                pivots = jnp.where(sub >= j, pivot, pivots)
            else:
                pivots = pivot
            mult = cols[j]
            row = down(a, j) * recip
            a = jnp.where(mine, row, a - mult * row)
            row = down(b, j) * recip
            b = jnp.where(mine, row, b - mult * row)
            for k in range(j + 1, SUB):
                row = down(cols[k], j) * recip
                cols[k] = jnp.where(mine, row, cols[k] - mult * row)
        scale = lax.rsqrt(pivots)
        upper.append(jnp.where(lane >= sub + SUB * t, ua * scale, 0.0))
        inverse.append(ub * scale)
        if t + 1 < count:
            va = [down(a, j) for j in range(SUB)]
            vb = [down(b, j) for j in range(SUB)]
            for i in range(t + 1, count):
                mult = [along(left[i], SUB * t + j) for j in range(SUB)]
                for j in range(SUB):
                    left[i] = left[i] - mult[j] * va[j]
                    right[i] = right[i] - mult[j] * vb[j]
    return jnp.concatenate(upper, 0), jnp.concatenate(inverse, 0)


def params(limit_mib=48):
    return pltpu.CompilerParams(vmem_limit_bytes=limit_mib << 20)


def shape(*dims):
    return jax.ShapeDtypeStruct(dims, F32)


def factor_kernel(kind, flag_ref, *refs):
    refs = list(refs)
    sources = [refs.pop(0) for _ in range({"first": 2, "next": 1, "schur": 5}[kind])]
    a_ref, f_ref, sems = refs[-3:]
    f_out = refs[0]
    rest_out = refs[1] if len(refs) > 4 else None
    n, m = a_ref.shape
    top, below = pl.ds(0, BLOCK), pl.ds(BLOCK, n - BLOCK)

    @pl.when(flag_ref[0] == 1)
    def _():
        copies = []

        def load(source, target):
            copies.append(pltpu.make_async_copy(source, target, sems.at[len(copies)]))
            copies[-1].start()

        if kind == "first":
            for rows in (top, below):
                load(sources[0].at[0, rows], a_ref.at[rows, pl.ds(0, n)])
                load(sources[1].at[rows], a_ref.at[rows, pl.ds(n, n)])
            needed = 2
        elif kind == "next":
            load(sources[0].at[top], a_ref.at[top])
            if n > BLOCK:
                load(sources[0].at[below], a_ref.at[below])
            needed = 1
        else:
            parts = refs[-4]
            load(sources[0], a_ref)
            for p, part in enumerate(sources[1:]):
                load(
                    part.at[:, pl.ds(part.shape[1] - n, n)],
                    parts.at[pl.ds(p * BLOCK, BLOCK)],
                )
            needed = len(copies)
        for copy in copies[:needed]:
            copy.wait()
        if kind == "schur":
            for r in range(0, n, BLOCK):
                lhs = parts[:, r : r + BLOCK].T
                for c in range(r, n, BLOCK):
                    a_ref[r : r + BLOCK, c : c + BLOCK] -= dot(lhs, parts[:, c : c + BLOCK], NN)

        first, second = pl.ds(0, BASE), pl.ds(BASE, BASE)
        sub = lax.broadcasted_iota(jnp.int32, (BASE, BASE), 0)
        lane = lax.broadcasted_iota(jnp.int32, (BASE, BASE), 1)
        x_ref = refs[-4] if kind != "schur" else refs[-5]

        def base(b, carry):
            rows = pl.ds(pl.multiple_of(b * BASE, BASE), BASE)
            u, x = factor_base(a_ref[rows, rows])
            f_ref[rows, rows] = jnp.where(sub <= lane, u, x)
            x_ref[rows, rows] = x

            @pl.when(b == 0)
            def _():
                u12 = dot(x, a_ref[first, second], NN)
                f_ref[first, second] = u12
                a_ref[second, second] -= dot(u12, u12, TN)

            return carry

        lax.fori_loop(0, BLOCK // BASE, base, 0)
        x21 = -dot(x_ref[second, second], dot(f_ref[first, second], x_ref[first, first], TN), NN)
        f_ref[second, first] = x21
        x_ref[second, first] = x21
        x_ref[first, second] = jnp.zeros((BASE, BASE), F32)
        x = x_ref[...]
        for c in range(BLOCK, m, BLOCK):
            f_ref[:, c : c + BLOCK] = dot(x, a_ref[top, c : c + BLOCK], NN)
        leaving = [pltpu.make_async_copy(f_ref, f_out, sems.at[len(copies)])]
        leaving[0].start()
        for copy in copies[needed:]:
            copy.wait()
        for r in range(BLOCK, n, BLOCK):
            lhs = f_ref[:, r : r + BLOCK].T
            for c in range(r, m, BLOCK):
                a_ref[r : r + BLOCK, c : c + BLOCK] -= dot(lhs, f_ref[:, c : c + BLOCK], NN)
            rows = pl.ds(r, BLOCK)
            leaving.append(
                pltpu.make_async_copy(
                    a_ref.at[rows, pl.ds(BLOCK, m - BLOCK)],
                    rest_out.at[pl.ds(r - BLOCK, BLOCK)],
                    sems.at[len(copies) + len(leaving)],
                )
            )
            leaving[-1].start()
        for copy in leaving:
            copy.wait()


def factor_block(kind, flag, n, m, *sources):
    shapes = [shape(BLOCK, m)]
    if n > BLOCK:
        shapes.append(shape(n - BLOCK, m - BLOCK))
    scratch = [pltpu.VMEM((BLOCK, BLOCK), F32)]
    if kind == "schur":
        scratch.append(pltpu.VMEM((n, n), F32))
    scratch += [pltpu.VMEM((n, m), F32), pltpu.VMEM((BLOCK, m), F32), DMA((12,))]
    out = pl.pallas_call(
        lambda *refs: factor_kernel(kind, *refs),
        out_shape=shapes,
        in_specs=[SMEM] + [ANY] * len(sources),
        out_specs=[ANY] * len(shapes),
        scratch_shapes=scratch,
        cost_estimate=pl.CostEstimate(
            flops=2_000_000_000, bytes_accessed=8 * n * m, transcendentals=0
        ),
        compiler_params=params(),
    )(flag, *sources)
    return out if n > BLOCK else (out[0], None)


def choose(index, options):
    def kernel(index_ref, *refs):
        *bufs, out_ref, held, sem = refs
        for k, buf in enumerate(bufs):

            @pl.when(index_ref[0] == k)
            def _():
                copy = pltpu.make_async_copy(buf, held, sem)
                copy.start()
                copy.wait()

        @pl.when(index_ref[0] >= 0)
        def _():
            copy = pltpu.make_async_copy(held, out_ref, sem)
            copy.start()
            copy.wait()

    return pl.pallas_call(
        kernel,
        out_shape=shape(*options[0].shape),
        in_specs=[SMEM] + [ANY] * len(options),
        out_specs=ANY,
        scratch_shapes=[pltpu.VMEM(options[0].shape, F32), DMA(())],
        compiler_params=params(8),
    )(index, *options)


def unset(like):
    return pl.pallas_call(
        lambda out_ref: None, out_shape=shape(*like.shape), in_specs=[], out_specs=ANY
    )()


def patch(flags, result, parts):
    def kernel(flags_ref, result_ref, *refs):
        *bufs, out_ref, held, sem = refs
        for k, buf in enumerate(bufs):

            @pl.when(flags_ref[k] == 1)
            def _():
                for source, target in ((buf, held), (held, out_ref.at[k])):
                    copy = pltpu.make_async_copy(source, target, sem)
                    copy.start()
                    copy.wait()

    return pl.pallas_call(
        kernel,
        out_shape=shape(*result.shape),
        in_specs=[SMEM] + [ANY] * (1 + len(parts)),
        out_specs=ANY,
        scratch_shapes=[pltpu.VMEM(parts[0].shape, F32), DMA(())],
        input_output_aliases={1: 0},
        compiler_params=params(8),
    )(flags, result, *parts)


def split(x):
    high = x.astype(jnp.bfloat16)
    return high, (x - high.astype(F32)).astype(jnp.bfloat16)


def dot3(a, b, dims):
    total = None
    for x, y in ((a[1], b[0]), (a[0], b[1]), (a[0], b[0])):
        part = lax.dot_general(x, y, (dims, ((), ())), preferred_element_type=F32)
        total = part if total is None else total + part
    return total


PASS, WORK, ZERO, LOWER0, PANEL0, LOWER1 = range(6)


def finish_kernel(n_raw, n_sets, meta_ref, *refs):
    tiles_ref, raws, refs = refs[0], refs[1 : 1 + n_raw], refs[1 + n_raw :]
    order = tiles_ref.shape[-1]
    steps = order // BLOCK
    count = 2 * steps
    sets = [refs[k * count : (k + 1) * count] for k in range(n_sets)]
    out_ref, p1_ref, z, t, spare, high, low, *fs, sems = refs[n_sets * count :]
    role, transposed, which, col, edge = (meta_ref[k] for k in (0, 5, 6, 7, 8))
    half = pl.ds(0, order), pl.ds(order, order)
    sources = [tiles_ref.at[0]] + list(raws)

    def load_pieces(pieces):
        for k in range(n_sets):

            @pl.when(which == k)
            def _():
                for p in pieces:
                    pltpu.make_async_copy(sets[k][p], fs[p], sems.at[8 + p]).start()

    def await_piece(p):
        pltpu.make_async_copy(sets[0][p], fs[p], sems.at[8 + p]).wait()

    def move_out(source, target, sem):
        copy = pltpu.make_async_copy(source, target, sems.at[sem])
        copy.start()
        return copy

    @pl.when(role == PASS)
    def _():
        held = (t, spare)
        copies = [move_out(tiles_ref.at[k], held[k], k) for k in range(2)]
        for k in range(2):
            copies[k].wait()
            copies[k] = move_out(held[k], out_ref.at[k], k)
        for copy in copies:
            copy.wait()

    @pl.when(role >= ZERO)
    def _():
        t[...] = jnp.zeros((order, order), F32)
        move_out(t, out_ref.at[1], 1).wait()

        def upper_block(p, q, lead):
            base = lead + (q - p) * BLOCK
            return fs[p][:, base : base + BLOCK].T

        def triangle(offset):
            sub = lax.broadcasted_iota(jnp.int32, (BLOCK, BLOCK), 0)
            lane = lax.broadcasted_iota(jnp.int32, (BLOCK, BLOCK), 1)
            for p in range(steps):
                for q in range(p, steps):
                    block = fs[offset + p][:, (q - p) * BLOCK : (q - p + 1) * BLOCK]
                    if p == q:
                        block = jnp.where(sub <= lane, block, 0.0)
                    t[q * BLOCK : (q + 1) * BLOCK, p * BLOCK : (p + 1) * BLOCK] = block.T

        for kind, pieces in (
            (LOWER0, range(steps)),
            (PANEL0, range(steps)),
            (LOWER1, range(steps, count)),
        ):

            @pl.when(role == kind)
            def _():
                load_pieces(pieces)
                for p in pieces:
                    await_piece(p)
                if kind == PANEL0:
                    for p in range(steps):
                        for q in range(steps):
                            t[q * BLOCK : (q + 1) * BLOCK, p * BLOCK : (p + 1) * BLOCK] = (
                                upper_block(p, q, order - p * BLOCK + p * BLOCK)
                            )
                else:
                    triangle(pieces[0])

        move_out(t, out_ref.at[0], 0).wait()

    @pl.when(role == WORK)
    def _():
        places = [z.at[half[a], half[b]] for a in range(2) for b in range(2)]
        for s, place in enumerate(places):
            for k, source in enumerate(sources):

                @pl.when(meta_ref[1 + s] == k)
                def _():
                    pltpu.make_async_copy(source, place, sems.at[s]).start()

        load_pieces(range(count))
        for slot, taken in ((1, col < 2), (0, col >= 2)):

            @pl.when(taken)
            def _():
                pltpu.make_async_copy(tiles_ref.at[slot], t, sems.at[4]).start()

        @pl.when(col >= 2)
        def _():
            move_out(tiles_ref.at[1], spare, 5)

        for s, place in enumerate(places):
            pltpu.make_async_copy(sources[1], place, sems.at[s]).wait()

        @pl.when(transposed == 1)
        def _():
            for left in (0, order):
                for a in range(steps):
                    for b in range(a, steps):
                        ra = order + a * BLOCK, left + a * BLOCK
                        rb = order + b * BLOCK, left + b * BLOCK
                        upper = z[ra[0] : ra[0] + BLOCK, rb[1] : rb[1] + BLOCK].T
                        if a != b:
                            z[ra[0] : ra[0] + BLOCK, rb[1] : rb[1] + BLOCK] = z[
                                rb[0] : rb[0] + BLOCK, ra[1] : ra[1] + BLOCK
                            ].T
                        z[rb[0] : rb[0] + BLOCK, ra[1] : ra[1] + BLOCK] = upper

        sub = lax.broadcasted_iota(jnp.int32, (BLOCK, BLOCK), 0)
        lane = lax.broadcasted_iota(jnp.int32, (BLOCK, BLOCK), 1)
        for p in range(count):
            await_piece(p)
            packed = fs[p][:, :BLOCK]
            inverse = jnp.where(
                sub > lane, packed, jnp.where(sub == lane, 1.0 / packed, 0.0)
            )
            inverse = split(inverse)
            for rows in half:
                solved = dot3(
                    split(z[rows, p * BLOCK : (p + 1) * BLOCK]), inverse, NT
                )
                z[rows, p * BLOCK : (p + 1) * BLOCK] = solved
                solved = split(solved)
                high[rows, :] = solved[0]
                low[rows, :] = solved[1]

            def eliminate(q, carry):
                to = pl.ds(pl.multiple_of(q * BLOCK, BLOCK), BLOCK)
                u = split(fs[p][:, pl.ds(pl.multiple_of((q - p) * BLOCK, BLOCK), BLOCK)])
                for rows in half:
                    z[rows, to] -= dot3((high[rows, :], low[rows, :]), u, NN)
                return carry

            lax.fori_loop(p + 1, count, eliminate, 0)
            if p == 0:
                pltpu.make_async_copy(tiles_ref.at[0], t, sems.at[4]).wait()

            def update(r, carry):
                rows = pl.ds(pl.multiple_of(r * BLOCK, BLOCK), BLOCK)
                others = high[half[1], :], low[half[1], :]
                t[rows, :] -= dot3((high[rows, :], low[rows, :]), others, NT)
                return carry

            lax.fori_loop(0, steps, update, 0)

        @pl.when(col >= 2)
        def _():
            pltpu.make_async_copy(tiles_ref.at[1], spare, sems.at[5]).wait()
            move_out(spare, out_ref.at[1], 5)

        @pl.when(col == 0)
        def _():
            move_out(z.at[half[0], half[0]], out_ref.at[0], 5)

        @pl.when(col == 1)
        def _():
            move_out(z.at[half[0], half[1]], out_ref.at[0], 5)

        for slot, taken in ((1, col < 2), (0, col >= 2)):

            @pl.when(taken)
            def _():
                move_out(t, out_ref.at[slot], 6)

        @pl.when((col == 2) & (edge == 1))
        def _():
            move_out(z.at[half[0], half[1]], p1_ref, 7).wait()

        pltpu.make_async_copy(t, out_ref.at[0], sems.at[5]).wait()
        pltpu.make_async_copy(t, out_ref.at[0], sems.at[6]).wait()


def finish(meta, tiles, raws, sets):
    order = tiles.shape[-1]
    count = len(sets[0])
    flat = [f for s in sets for f in s]
    scratch = [
        pltpu.VMEM((2 * order, 2 * order), F32),
        pltpu.VMEM((order, order), F32),
        pltpu.VMEM((order, order), F32),
        pltpu.VMEM((2 * order, BLOCK), jnp.bfloat16),
        pltpu.VMEM((2 * order, BLOCK), jnp.bfloat16),
    ]
    scratch += [pltpu.VMEM(f.shape, F32) for f in sets[0]] + [DMA((8 + count,))]
    return pl.pallas_call(
        lambda *refs: finish_kernel(len(raws), len(sets), *refs),
        out_shape=[shape(*tiles.shape), shape(order, order)],
        in_specs=[SMEM] + [ANY] * (1 + len(raws) + len(flat)),
        out_specs=[ANY, ANY],
        scratch_shapes=scratch,
        cost_estimate=pl.CostEstimate(
            flops=60_000_000_000, bytes_accessed=64 << 20, transcendentals=0
        ),
        compiler_params=params(56),
    )(meta, tiles, *raws, *flat)


def move(value, pairs, cols):
    flat = [(a * cols + b, c * cols + d) for (a, b), (c, d) in pairs]
    return lax.ppermute(value, ("row", "col"), flat)


def doubling(value, axis, root, size):
    place = lax.rem(lax.axis_index(axis) - root + size, size)
    reach = 1
    while reach < size:
        pairs = [
            ((root + i) % size, (root + i + reach) % size) for i in range(min(reach, size - reach))
        ]
        value = jnp.where(place >= reach, lax.ppermute(value, axis, pairs), value)
        reach *= 2
    return value


def both_ways(pairs):
    return pairs + [(b, a) for a, b in pairs]


def eliminate_last(panel, pieces):
    done = []
    for f in pieces:
        packed = f[:, :BLOCK]
        inverse = jnp.tril(packed, -1) + jnp.diag(1.0 / jnp.diagonal(packed))
        part = dot(panel[:, :BLOCK], inverse, NT, lax.Precision.HIGH)
        done.append(part)
        if f.shape[1] > BLOCK:
            panel = panel[:, BLOCK:] - dot(part, f[:, BLOCK:], NN, lax.Precision.HIGH)
    return jnp.concatenate(done, 1)


def on_device(kernel_tiles, profile):
    order = kernel_tiles.shape[-1]
    rows, cols = lax.axis_size("row"), lax.axis_size("col")
    row, col = lax.axis_index("row"), lax.axis_index("col")
    tiles = kernel_tiles.reshape(2, order, order)
    near = tiles[0]
    steps = order // BLOCK
    count = 2 * steps
    edge = cols + 2
    edge_live = profile[0, edge] <= 1
    owner = jnp.reshape(((row == 0) & (col == 0)).astype(jnp.int32), (1,))
    workers = range(2, edge)
    routed = cols == 4

    plan = [[[PASS] + [0] * 8 + [-1] * 5 for _ in range(cols)] for _ in range(rows)]
    for r in range(rows):
        for c in range(cols):
            plan[r][c][7] = c
            if r < 2:
                plan[r][c][0] = ZERO
            elif r < edge:
                plan[r][c][0] = WORK
    plan[0][0][0], plan[1][0][0], plan[1][1][0] = LOWER0, PANEL0, LOWER1

    if routed:
        r1 = move(near, both_ways([((r, 0), (r, 1)) for r in (0,) + tuple(workers)]), cols)
        r2 = move(
            near,
            [((r, c), (r, c + 2)) for r in workers for c in (0, 1)]
            + [((1, 1), (0, 0)), ((edge, 1), (edge, 3))],
            cols,
        )
        r3 = move(
            near,
            both_ways([((4, c), (5, c)) for c in (0, 1)])
            + [((r, c), (r + 4, c)) for r in (0, 1) for c in (2, 3)],
            cols,
        )
        r4 = move(near, [((r, c), (r - 2, c)) for r in (4, 5) for c in (0, 1)], cols)
        tile01 = r1
        for r in workers:
            plan[r][0][1:3] = [0, 1]
            plan[r][1][1:3] = [1, 0]
            plan[r][2][1:3] = [2, 5]
            plan[r][3][1:3] = [5, 2]
            for c in range(4):
                plan[r][c][3:5] = plan[r][c][1:3]
        for place, pair in {
            (2, 0): (4, 7), (2, 1): (7, 6), (3, 0): (6, 7), (3, 1): (7, 4),
            (4, 1): (7, 3), (5, 0): (3, 7), (2, 3): (7, 6), (3, 2): (6, 7),
            (4, 2): (3, 6), (4, 3): (3, 6), (5, 2): (6, 3), (5, 3): (6, 3),
        }.items():
            plan[place[0]][place[1]][3:5] = pair
        for c in (0, 1):
            plan[2][c][12] = plan[3][c][12] = 2
        for c in (2, 3):
            plan[2][c][12] = plan[3][c][12] = 0
            plan[4][c][12] = plan[5][c][12] = 1
        plan[4][0][13] = plan[5][1][13] = 0
        plan[2][1][13] = plan[3][0][13] = 1
        plan[2][0][13] = plan[3][1][13] = plan[2][2][13] = plan[3][3][13] = 2
        for r in (4, 5):
            for c in (2, 3):
                plan[r][c][5] = 1
        plan[1][1][6] = 1
        for r in workers:
            plan[r][1][6] = plan[r][3][6] = 2 if r < 4 else 3
            plan[r][3][6] = 4
        for r in (1,) + tuple(workers):
            plan[r][0][6] = plan[r][2][6] = 5
        plan[0][1][9], plan[1][1][9] = 0, 1
        for r in workers:
            plan[r][1][10] = 0 if r < 4 else 1
            plan[r][1][11] = 1 if r < 4 else 2
            plan[r][3][11] = 3
        plan[1][1][11] = 0
    else:
        mine = jnp.where(col < 2, tiles[1], near)
        left0 = doubling(near, "col", 0, cols)
        left1 = doubling(near, "col", 1, cols)
        top0 = doubling(mine, "row", 0, rows)
        top1 = doubling(mine, "row", 1, rows)
        tile01 = move(near, [((0, 1), (0, 0))], cols)
        tile11 = move(near, [((1, 1), (0, 0))], cols)
        raws = [left0, left1, top0, top1]
        for r in range(rows):
            for c in range(cols):
                plan[r][c][1:6] = [1, 2, 3, 4, 1]
    meta = jnp.array(plan, jnp.int32)[row, col]
    meta = meta.at[8].set(edge_live.astype(jnp.int32))

    pieces, copies, state = [], [], None
    stages = 6 if routed else 0
    late = []
    for slot in range(count + stages):
        arrived = []
        if slot < count:
            step, local = divmod(slot, steps)
            n = order - local * BLOCK
            if slot == 0:
                args = ("first", owner, n, 2 * n, tiles, tile01)
            elif local == 0:
                args = ("schur", owner, n, n, r2 if routed else tile11, *pieces)
            else:
                args = ("next", owner, n, n + (1 - step) * order, state)
            piece, state = factor_block(*args)
            pieces.append(piece)
            copies.append([])
            if not routed:
                copies[-1].append(doubling(doubling(piece, "row", 0, rows), "col", 0, cols))
        if not routed:
            continue
        for k in range(1, stages + 1):
            p = slot - k
            if not 0 <= p < count:
                continue
            got = copies[p]
            if k == 1:
                got.append(move(pieces[p], [((0, 0), (0, 1))], cols))
            elif k == 2:
                got.append(move(got[0], [((0, 1), (1, 1))], cols))
            elif k == 3:
                via = choose(meta[9:10], [got[0], got[1]])
                got.append(move(via, [((r, 1), (r + 2, 1)) for r in (0, 1)], cols))
            elif k == 4:
                got.append(move(got[2], [((r, 1), (r + 2, 1)) for r in (2, 3)], cols))
            elif k == 5:
                via = choose(meta[10:11], [got[2], got[3]])
                got.append(move(via, [((r, 1), (r, 3)) for r in workers], cols))
            else:
                via = choose(meta[11:12], [got[1], got[2], got[3], got[4]])
                got.append(
                    move(
                        via,
                        [((r, c), (r, c - 1)) for r in workers for c in (1, 3)]
                        + [((1, 1), (1, 0))],
                        cols,
                    )
                )
            arrived.append(p)
        late = []
        if slot == FIRST:
            late = [r2, r3, r4]
        elif slot == SECOND:
            late = [r5, r6, e1]
        elif slot == THIRD:
            late = [r7]
        last = [copies[p][-1] for p in arrived]
        flowing = ([pieces[slot]] if slot < count else []) + ([] if state is None else [state])
        flowing, last, late = lax.optimization_barrier((flowing, last, late))
        if slot < count:
            pieces[slot] = flowing[0]
        if state is not None:
            state = flowing[-1]
        for p, value in zip(arrived, last):
            copies[p][-1] = value
        if slot == FIRST:
            r2, r3, r4 = late
            r5 = move(r2, both_ways([((r, 2), (r, 3)) for r in workers]), cols)
            r6 = move(
                choose(meta[12:13], [r2, r3, r4]),
                both_ways([((2, c), (3, c)) for c in range(4)] + [((4, c), (5, c)) for c in (2, 3)]),
                cols,
            )
            e1 = move(r2, [((edge, 3), (edge - 2, 2))], cols)
        elif slot == SECOND:
            r5, r6, e1 = late
            r7 = move(
                choose(meta[13:14], [r3, r4, r6]),
                [((4, 0), (4, 1)), ((5, 1), (5, 0)), ((2, 1), (2, 0)), ((3, 0), (3, 1))]
                + [((2, 0), (2, 1)), ((3, 1), (3, 0)), ((2, 2), (2, 3)), ((3, 3), (3, 2))],
                cols,
            )
        elif slot == THIRD:
            (r7,) = late

    if routed:
        sets = [pieces] + [[got[k] for got in copies] for k in (1, 2, 3, 4, 5)]
        raws = [r1, r2, r3, r4, r5, r6, r7]
    else:
        sets = [[got[0] for got in copies]]

    def fetch(tile):
        if routed:
            e2 = move(tile, [((edge - 2, 2), (edge - 4, 2))], cols)
            e3 = move(tile + e2, [((r, 2), (r + 1, 2)) for r in (2, 4)], cols)
            return tile + e2 + e3
        total = jnp.zeros_like(tile)
        for r in workers:
            total = total + move(tile, [((edge, 1), (r, 2))], cols)
        return total

    result, panel1 = finish(meta, tiles, raws, sets)

    def edge_parts(args):
        panel1, edge_tile, last_pieces = args
        far = tiles[1]
        edge_tile = fetch(edge_tile)
        last = eliminate_last(edge_tile, last_pieces)
        column = far - dot(panel1, last, NT, lax.Precision.HIGH)
        sent = move(column, [((r, 2), (edge, r % cols)) for r in workers], cols).T
        solved = move(last, [((edge - 2, 2), (edge, 1)), ((edge - 1, 2), (edge, 2))], cols)
        corner = far - dot(solved, solved, NT, lax.Precision.HIGH)
        part0 = jnp.where(col == 1, solved, sent)
        part1 = jnp.where(row == edge, jnp.where(col == 2, corner, sent), column)
        return part0, part1

    def no_edge(args):
        return unset(near), unset(near)

    parts = lax.cond(edge_live, edge_parts, no_edge, (panel1, e1 if routed else near, sets[-1][steps:]))
    at_edge = edge_live & (row == edge)
    flags = jnp.stack(
        [
            at_edge & (col >= 1),
            (at_edge & (col <= 2)) | (edge_live & (row >= 2) & (row < edge) & (col == 2)),
        ]
    ).astype(jnp.int32)
    return patch(flags, result, parts).reshape(kernel_tiles.shape)


def solution(mesh):
    placed = (P(None, "row", None, "col", None, None), P())
    return jax.shard_map(
        on_device,
        mesh=mesh,
        in_specs=placed,
        out_specs=P(None, "row", None, "col", None, None),
        check_vma=False,
    )
```

```python
import jax
import jax.numpy as jnp
from jax import lax
from jax.experimental import pallas as pl
from jax.experimental.pallas import tpu as pltpu
from jax.sharding import PartitionSpec as P

SUB = 8
BASE = 128
BLOCK = 256
STAGES = (6, 3)
NN = ((1,), (0,))
NT = ((1,), (1,))
TN = ((0,), (0,))
ANY = pl.BlockSpec(memory_space=pl.ANY)
SMEM = pl.BlockSpec(memory_space=pltpu.SMEM)
DMA = pltpu.SemaphoreType.DMA
F32 = jnp.float32


def dot(a, b, dims, precision=lax.Precision.HIGHEST):
    return lax.dot_general(
        a, b, (dims, ((), ())), precision=precision, preferred_element_type=jnp.float32
    )


def down(x, j):
    return jnp.broadcast_to(x[j : j + 1, :], x.shape)


def along(x, j):
    return jnp.broadcast_to(x[:, j : j + 1], x.shape)


def factor_base(diag):
    sub = lax.broadcasted_iota(jnp.int32, (SUB, BASE), 0)
    lane = lax.broadcasted_iota(jnp.int32, (SUB, BASE), 1)
    count = BASE // SUB
    left = [diag[SUB * t : SUB * t + SUB, :] for t in range(count)]
    right = [(lane == sub + SUB * t).astype(jnp.float32) for t in range(count)]
    upper, inverse = [], []
    for t in range(count):
        a, b = left[t], right[t]
        cols = [along(a, SUB * t + j) for j in range(SUB)]
        ua, ub, pivots = a, b, None
        for j in range(SUB):
            mine = sub == j
            pivot = down(cols[j], j)
            recip = 1.0 / pivot
            if j:
                ua = jnp.where(sub >= j, a, ua)
                ub = jnp.where(sub >= j, b, ub)
                pivots = jnp.where(sub >= j, pivot, pivots)
            else:
                pivots = pivot
            mult = cols[j]
            row = down(a, j) * recip
            a = jnp.where(mine, row, a - mult * row)
            row = down(b, j) * recip
            b = jnp.where(mine, row, b - mult * row)
            for k in range(j + 1, SUB):
                row = down(cols[k], j) * recip
                cols[k] = jnp.where(mine, row, cols[k] - mult * row)
        scale = lax.rsqrt(pivots)
        upper.append(jnp.where(lane >= sub + SUB * t, ua * scale, 0.0))
        inverse.append(ub * scale)
        if t + 1 < count:
            va = [down(a, j) for j in range(SUB)]
            vb = [down(b, j) for j in range(SUB)]
            for i in range(t + 1, count):
                mult = [along(left[i], SUB * t + j) for j in range(SUB)]
                for j in range(SUB):
                    left[i] = left[i] - mult[j] * va[j]
                    right[i] = right[i] - mult[j] * vb[j]
    return jnp.concatenate(upper, 0), jnp.concatenate(inverse, 0)


def params(limit_mib=48):
    return pltpu.CompilerParams(vmem_limit_bytes=limit_mib << 20)


def shape(*dims):
    return jax.ShapeDtypeStruct(dims, F32)


def factor_kernel(kind, flag_ref, *refs):
    refs = list(refs)
    sources = [refs.pop(0) for _ in range({"first": 3, "next": 1, "schur": 5}[kind])]
    a_ref, f_ref, sems = refs[-3:]
    f_out = refs[0]
    rest_out = refs[1] if len(refs) > 4 else None
    n, m = a_ref.shape
    top, below = pl.ds(0, BLOCK), pl.ds(BLOCK, n - BLOCK)

    @pl.when(flag_ref[0] == 1)
    def _():
        copies = []

        def load(source, target):
            copies.append(pltpu.make_async_copy(source, target, sems.at[len(copies)]))
            copies[-1].start()

        if kind == "first":
            left, right, cut = pl.ds(0, n), pl.ds(n, n), n // 2 - BLOCK
            load(sources[0].at[0, top], a_ref.at[top, left])
            load(sources[1].at[top], a_ref.at[top, right])
            load(sources[0].at[0, below], a_ref.at[below, left])
            load(sources[1].at[pl.ds(BLOCK, cut)], a_ref.at[pl.ds(BLOCK, cut), right])
            load(sources[2], a_ref.at[pl.ds(n // 2, n // 2), right])
            needed = 2
        elif kind == "next":
            load(sources[0].at[top], a_ref.at[top])
            if n > BLOCK:
                load(sources[0].at[below], a_ref.at[below])
            needed = 1
        else:
            parts = refs[-4]
            load(sources[0], a_ref)
            for p, part in enumerate(sources[1:]):
                load(
                    part.at[:, pl.ds(part.shape[1] - n, n)],
                    parts.at[pl.ds(p * BLOCK, BLOCK)],
                )
            needed = len(copies)
        for copy in copies[:needed]:
            copy.wait()
        if kind == "schur":
            for r in range(0, n, BLOCK):
                lhs = parts[:, r : r + BLOCK].T
                for c in range(r, n, BLOCK):
                    a_ref[r : r + BLOCK, c : c + BLOCK] -= dot(lhs, parts[:, c : c + BLOCK], NN)

        first, second = pl.ds(0, BASE), pl.ds(BASE, BASE)
        sub = lax.broadcasted_iota(jnp.int32, (BASE, BASE), 0)
        lane = lax.broadcasted_iota(jnp.int32, (BASE, BASE), 1)
        x_ref = refs[-4] if kind != "schur" else refs[-5]

        def base(b, carry):
            rows = pl.ds(pl.multiple_of(b * BASE, BASE), BASE)
            u, x = factor_base(a_ref[rows, rows])
            f_ref[rows, rows] = jnp.where(sub <= lane, u, x)
            x_ref[rows, rows] = x

            @pl.when(b == 0)
            def _():
                u12 = dot(x, a_ref[first, second], NN)
                f_ref[first, second] = u12
                a_ref[second, second] -= dot(u12, u12, TN)

            return carry

        lax.fori_loop(0, BLOCK // BASE, base, 0)
        x21 = -dot(x_ref[second, second], dot(f_ref[first, second], x_ref[first, first], TN), NN)
        f_ref[second, first] = x21
        x_ref[second, first] = x21
        x_ref[first, second] = jnp.zeros((BASE, BASE), F32)
        x = x_ref[...]
        for c in range(BLOCK, m, BLOCK):
            f_ref[:, c : c + BLOCK] = dot(x, a_ref[top, c : c + BLOCK], NN)
        leaving = [pltpu.make_async_copy(f_ref, f_out, sems.at[len(copies)])]
        leaving[0].start()
        for copy in copies[needed:]:
            copy.wait()
        for r in range(BLOCK, n, BLOCK):
            lhs = f_ref[:, r : r + BLOCK].T
            for c in range(r, m, BLOCK):
                a_ref[r : r + BLOCK, c : c + BLOCK] -= dot(lhs, f_ref[:, c : c + BLOCK], NN)
            rows = pl.ds(r, BLOCK)
            leaving.append(
                pltpu.make_async_copy(
                    a_ref.at[rows, pl.ds(BLOCK, m - BLOCK)],
                    rest_out.at[pl.ds(r - BLOCK, BLOCK)],
                    sems.at[len(copies) + len(leaving)],
                )
            )
            leaving[-1].start()
        for copy in leaving:
            copy.wait()


def factor_block(kind, flag, n, m, *sources):
    shapes = [shape(BLOCK, m)]
    if n > BLOCK:
        shapes.append(shape(n - BLOCK, m - BLOCK))
    scratch = [pltpu.VMEM((BLOCK, BLOCK), F32)]
    if kind == "schur":
        scratch.append(pltpu.VMEM((n, n), F32))
    scratch += [pltpu.VMEM((n, m), F32), pltpu.VMEM((BLOCK, m), F32), DMA((12,))]
    out = pl.pallas_call(
        lambda *refs: factor_kernel(kind, *refs),
        out_shape=shapes,
        in_specs=[SMEM] + [ANY] * len(sources),
        out_specs=[ANY] * len(shapes),
        scratch_shapes=scratch,
        cost_estimate=pl.CostEstimate(
            flops=2_000_000_000, bytes_accessed=8 * n * m, transcendentals=0
        ),
        compiler_params=params(),
    )(flag, *sources)
    return out if n > BLOCK else (out[0], None)


def choose(index, options):
    def kernel(index_ref, *refs):
        *bufs, out_ref, held, sem = refs
        for k, buf in enumerate(bufs):

            @pl.when(index_ref[0] == k)
            def _():
                copy = pltpu.make_async_copy(buf, held, sem)
                copy.start()
                copy.wait()

        @pl.when(index_ref[0] >= 0)
        def _():
            copy = pltpu.make_async_copy(held, out_ref, sem)
            copy.start()
            copy.wait()

    return pl.pallas_call(
        kernel,
        out_shape=shape(*options[0].shape),
        in_specs=[SMEM] + [ANY] * len(options),
        out_specs=ANY,
        scratch_shapes=[pltpu.VMEM(options[0].shape, F32), DMA(())],
        compiler_params=params(8),
    )(index, *options)


def patch(flags, result, parts):
    def kernel(flags_ref, result_ref, *refs):
        *bufs, out_ref, held, sem = refs
        for k, buf in enumerate(bufs):

            @pl.when(flags_ref[k] == 1)
            def _():
                for source, target in ((buf, held), (held, out_ref.at[k])):
                    copy = pltpu.make_async_copy(source, target, sem)
                    copy.start()
                    copy.wait()

    return pl.pallas_call(
        kernel,
        out_shape=shape(*result.shape),
        in_specs=[SMEM] + [ANY] * (1 + len(parts)),
        out_specs=ANY,
        scratch_shapes=[pltpu.VMEM(parts[0].shape, F32), DMA(())],
        input_output_aliases={1: 0},
        compiler_params=params(8),
    )(flags, result, *parts)


def split(x):
    high = x.astype(jnp.bfloat16)
    return high, (x - high.astype(F32)).astype(jnp.bfloat16)


def wide_left(x, axis):
    high, low = split(x)
    return jnp.concatenate([high, high, low], axis)


def wide_right(x, axis):
    high, low = split(x)
    return jnp.concatenate([high, low, high], axis)


def dot_wide(a, b, dims):
    return lax.dot_general(a, b, (dims, ((), ())), preferred_element_type=F32)


PASS, WORK, ZERO, LOWER0, PANEL0, LOWER1 = range(6)


def finish_kernel(n_raw, n_sets, meta_ref, *refs):
    tiles_ref, raws, refs = refs[0], refs[1 : 1 + n_raw], refs[1 + n_raw :]
    order = tiles_ref.shape[-1]
    steps = order // BLOCK
    count = 2 * steps
    sets = [refs[k * count : (k + 1) * count] for k in range(n_sets)]
    out_ref, p1_ref, z, t, spare, wide, others, *fs, sems = refs[n_sets * count :]
    role, transposed, col, edge = (meta_ref[k] for k in (0, 5, 7, 8))
    which = meta_ref[6], meta_ref[14]
    half = pl.ds(0, order), pl.ds(order, order)
    mid = order // 2
    sources = [
        [tiles_ref.at[0, pl.ds(h * mid, mid)]] + [raws[2 * k + h] for k in range(n_raw // 2)]
        for h in range(2)
    ]

    def load_pieces(pieces):
        for k in range(n_sets):
            for step in range(2):

                @pl.when(which[step] == k)
                def _():
                    for p in pieces:
                        if p // steps == step:
                            pltpu.make_async_copy(sets[k][p], fs[p], sems.at[8 + p]).start()

    def await_piece(p):
        pltpu.make_async_copy(sets[0][p], fs[p], sems.at[8 + p]).wait()

    def move_out(source, target, sem):
        copy = pltpu.make_async_copy(source, target, sems.at[sem])
        copy.start()
        return copy

    @pl.when(role == PASS)
    def _():
        held = (t, spare)
        copies = [move_out(tiles_ref.at[k], held[k], k) for k in range(2)]
        for k in range(2):
            copies[k].wait()
            copies[k] = move_out(held[k], out_ref.at[k], k)
        for copy in copies:
            copy.wait()

    @pl.when(role >= ZERO)
    def _():
        t[...] = jnp.zeros((order, order), F32)
        move_out(t, out_ref.at[1], 1).wait()

        def upper_block(p, q, lead):
            base = lead + (q - p) * BLOCK
            return fs[p][:, base : base + BLOCK].T

        def triangle(offset):
            sub = lax.broadcasted_iota(jnp.int32, (BLOCK, BLOCK), 0)
            lane = lax.broadcasted_iota(jnp.int32, (BLOCK, BLOCK), 1)
            for p in range(steps):
                for q in range(p, steps):
                    block = fs[offset + p][:, (q - p) * BLOCK : (q - p + 1) * BLOCK]
                    if p == q:
                        block = jnp.where(sub <= lane, block, 0.0)
                    t[q * BLOCK : (q + 1) * BLOCK, p * BLOCK : (p + 1) * BLOCK] = block.T

        for kind, pieces in (
            (LOWER0, range(steps)),
            (PANEL0, range(steps)),
            (LOWER1, range(steps, count)),
        ):

            @pl.when(role == kind)
            def _():
                load_pieces(pieces)
                for p in pieces:
                    await_piece(p)
                if kind == PANEL0:
                    for p in range(steps):
                        for q in range(steps):
                            t[q * BLOCK : (q + 1) * BLOCK, p * BLOCK : (p + 1) * BLOCK] = (
                                upper_block(p, q, order - p * BLOCK + p * BLOCK)
                            )
                else:
                    triangle(pieces[0])

        move_out(t, out_ref.at[0], 0).wait()

    @pl.when(role == WORK)
    def _():
        places = [
            [z.at[pl.ds(a * order + h * mid, mid), half[b]] for h in range(2)]
            for a in range(2)
            for b in range(2)
        ]
        for s, place in enumerate(places):
            for k in range(len(sources[0])):

                @pl.when(meta_ref[1 + s] == k)
                def _():
                    for h in range(2):
                        sem = sems.at[8 + count + 2 * s + h]
                        pltpu.make_async_copy(sources[h][k], place[h], sem).start()

        load_pieces(range(count))
        for slot, taken in ((1, col < 2), (0, col >= 2)):

            @pl.when(taken)
            def _():
                pltpu.make_async_copy(tiles_ref.at[slot], t, sems.at[4]).start()

        @pl.when(col >= 2)
        def _():
            move_out(tiles_ref.at[1], spare, 5)

        for s, place in enumerate(places):
            for h in range(2):
                sem = sems.at[8 + count + 2 * s + h]
                pltpu.make_async_copy(sources[h][1], place[h], sem).wait()

        @pl.when(transposed == 1)
        def _():
            for left in (0, order):
                for a in range(steps):
                    for b in range(a, steps):
                        ra = order + a * BLOCK, left + a * BLOCK
                        rb = order + b * BLOCK, left + b * BLOCK
                        upper = z[ra[0] : ra[0] + BLOCK, rb[1] : rb[1] + BLOCK].T
                        if a != b:
                            z[ra[0] : ra[0] + BLOCK, rb[1] : rb[1] + BLOCK] = z[
                                rb[0] : rb[0] + BLOCK, ra[1] : ra[1] + BLOCK
                            ].T
                        z[rb[0] : rb[0] + BLOCK, ra[1] : ra[1] + BLOCK] = upper

        sub = lax.broadcasted_iota(jnp.int32, (BLOCK, BLOCK), 0)
        lane = lax.broadcasted_iota(jnp.int32, (BLOCK, BLOCK), 1)
        for p in range(count):
            await_piece(p)
            packed = fs[p][:, :BLOCK]
            inverse = jnp.where(
                sub > lane, packed, jnp.where(sub == lane, 1.0 / packed, 0.0)
            )
            inverse = wide_right(inverse, 1)
            for k, rows in enumerate(half):
                solved = dot_wide(
                    wide_left(z[rows, p * BLOCK : (p + 1) * BLOCK], 1), inverse, NT
                )
                z[rows, p * BLOCK : (p + 1) * BLOCK] = solved
                wide[rows, :] = wide_left(solved, 1)
                if k == 1:
                    others[...] = wide_right(solved, 1)

            def eliminate(q, carry):
                to = pl.ds(pl.multiple_of(q * BLOCK, BLOCK), BLOCK)
                u = wide_right(
                    fs[p][:, pl.ds(pl.multiple_of((q - p) * BLOCK, BLOCK), BLOCK)], 0
                )
                for rows in half:
                    z[rows, to] -= dot_wide(wide[rows, :], u, NN)
                return carry

            lax.fori_loop(p + 1, count, eliminate, 0)
            if p == 0:
                pltpu.make_async_copy(tiles_ref.at[0], t, sems.at[4]).wait()

            def update(r, carry):
                rows = pl.ds(pl.multiple_of(r * BLOCK, BLOCK), BLOCK)
                t[rows, :] -= dot_wide(wide[rows, :], others[...], NT)
                return carry

            lax.fori_loop(0, steps, update, 0)

        @pl.when(col >= 2)
        def _():
            pltpu.make_async_copy(tiles_ref.at[1], spare, sems.at[5]).wait()
            move_out(spare, out_ref.at[1], 5)

        @pl.when(col == 0)
        def _():
            move_out(z.at[half[0], half[0]], out_ref.at[0], 5)

        @pl.when(col == 1)
        def _():
            move_out(z.at[half[0], half[1]], out_ref.at[0], 5)

        for slot, taken in ((1, col < 2), (0, col >= 2)):

            @pl.when(taken)
            def _():
                move_out(t, out_ref.at[slot], 6)

        @pl.when((col == 2) & (edge == 1))
        def _():
            move_out(z.at[half[0], half[1]], p1_ref, 7).wait()

        pltpu.make_async_copy(t, out_ref.at[0], sems.at[5]).wait()
        pltpu.make_async_copy(t, out_ref.at[0], sems.at[6]).wait()


def finish(meta, tiles, raws, sets):
    order = tiles.shape[-1]
    count = len(sets[0])
    flat = [f for s in sets for f in s]
    scratch = [
        pltpu.VMEM((2 * order, 2 * order), F32),
        pltpu.VMEM((order, order), F32),
        pltpu.VMEM((order, order), F32),
        pltpu.VMEM((2 * order, 3 * BLOCK), jnp.bfloat16),
        pltpu.VMEM((order, 3 * BLOCK), jnp.bfloat16),
    ]
    scratch += [pltpu.VMEM(f.shape, F32) for f in sets[0]] + [DMA((16 + count,))]
    return pl.pallas_call(
        lambda *refs: finish_kernel(len(raws), len(sets), *refs),
        out_shape=[shape(*tiles.shape), shape(order, order)],
        in_specs=[SMEM] + [ANY] * (1 + len(raws) + len(flat)),
        out_specs=[ANY, ANY],
        scratch_shapes=scratch,
        cost_estimate=pl.CostEstimate(
            flops=60_000_000_000, bytes_accessed=64 << 20, transcendentals=0
        ),
        compiler_params=params(56),
    )(meta, tiles, *raws, *flat)


def move(value, pairs, cols):
    if isinstance(value, list):
        return [move(v, pairs, cols) for v in value]
    flat = [(a * cols + b, c * cols + d) for (a, b), (c, d) in pairs]
    return lax.ppermute(value, ("row", "col"), flat)


def doubling(value, axis, root, size):
    place = lax.rem(lax.axis_index(axis) - root + size, size)
    reach = 1
    while reach < size:
        pairs = [
            ((root + i) % size, (root + i + reach) % size) for i in range(min(reach, size - reach))
        ]
        value = jnp.where(place >= reach, lax.ppermute(value, axis, pairs), value)
        reach *= 2
    return value


def both_ways(pairs):
    return pairs + [(b, a) for a, b in pairs]


def eliminate_last(panel, pieces):
    done = []
    for f in pieces:
        packed = f[:, :BLOCK]
        inverse = jnp.tril(packed, -1) + jnp.diag(1.0 / jnp.diagonal(packed))
        part = dot(panel[:, :BLOCK], inverse, NT, lax.Precision.HIGH)
        done.append(part)
        if f.shape[1] > BLOCK:
            panel = panel[:, BLOCK:] - dot(part, f[:, BLOCK:], NN, lax.Precision.HIGH)
    return jnp.concatenate(done, 1)


def on_device(kernel_tiles, profile):
    order = kernel_tiles.shape[-1]
    rows, cols = lax.axis_size("row"), lax.axis_size("col")
    row, col = lax.axis_index("row"), lax.axis_index("col")
    tiles = kernel_tiles.reshape(2, order, order)
    near = tiles[0]
    halves = [near[: order // 2], near[order // 2 :]]
    steps = order // BLOCK
    count = 2 * steps
    edge = cols + 2
    edge_live = profile[0, edge] <= 1
    owner = jnp.reshape(((row == 0) & (col == 0)).astype(jnp.int32), (1,))
    workers = range(2, edge)
    routed = cols == 4

    plan = [[[PASS] + [0] * 8 + [-1] * 5 + [0, -1, -1] for _ in range(cols)] for _ in range(rows)]
    for r in range(rows):
        for c in range(cols):
            plan[r][c][7] = c
            if r < 2:
                plan[r][c][0] = ZERO
            elif r < edge:
                plan[r][c][0] = WORK
    plan[0][0][0], plan[1][0][0], plan[1][1][0] = LOWER0, PANEL0, LOWER1

    if routed:
        r1 = move(halves, both_ways([((r, 0), (r, 1)) for r in (0,) + tuple(workers)]), cols)
        r2 = move(
            halves, [((r, c), (r, c + 2)) for r in workers for c in (0, 1)], cols
        )
        r3 = move(
            halves,
            both_ways([((4, c), (5, c)) for c in (0, 1)])
            + [((r, c), (r + 4, c)) for r in (0, 1) for c in (2, 3)],
            cols,
        )
        r4 = move(halves, [((r, c), (r - 2, c)) for r in (4, 5) for c in (0, 1)], cols)
        tile11 = move(near, [((1, 1), (0, 0))], cols)
        tile01 = r1
        for r in workers:
            plan[r][0][1:3] = [0, 1]
            plan[r][1][1:3] = [1, 0]
            plan[r][2][1:3] = [2, 5]
            plan[r][3][1:3] = [5, 2]
            for c in range(4):
                plan[r][c][3:5] = plan[r][c][1:3]
        for place, pair in {
            (2, 0): (4, 7), (2, 1): (7, 6), (3, 0): (6, 7), (3, 1): (7, 4),
            (4, 1): (7, 3), (5, 0): (3, 7), (2, 3): (7, 6), (3, 2): (6, 7),
            (4, 2): (3, 6), (4, 3): (3, 6), (5, 2): (6, 3), (5, 3): (6, 3),
        }.items():
            plan[place[0]][place[1]][3:5] = pair
        for c in (0, 1):
            plan[2][c][12] = plan[3][c][12] = 2
        for c in (2, 3):
            plan[2][c][12] = plan[3][c][12] = 0
            plan[4][c][12] = plan[5][c][12] = 1
        plan[4][0][13] = plan[5][1][13] = 0
        plan[2][1][13] = plan[3][0][13] = 1
        plan[2][0][13] = plan[3][1][13] = plan[2][2][13] = plan[3][3][13] = 2
        for r in (4, 5):
            for c in (2, 3):
                plan[r][c][5] = 1
        plan[1][1][6] = 1
        for r in workers:
            plan[r][1][6] = plan[r][3][6] = 2 if r < 4 else 3
            plan[r][3][6] = 4
        for r in (1,) + tuple(workers):
            plan[r][0][6] = plan[r][2][6] = 5
        plan[1][1][14] = 4
        plan[0][0][15], plan[1][0][15], plan[1][0][16] = 0, 1, 0
        for r in workers:
            plan[r][0][14:17] = [1, -1, 1] if r < 4 else [2, -1, 2]
            plan[r][1][14], plan[r][2][14], plan[r][3][14] = 4, 3, 5
        plan[0][1][9], plan[1][1][9] = 0, 1
        for r in workers:
            plan[r][1][10] = 0 if r < 4 else 1
            plan[r][1][11] = 1 if r < 4 else 2
            plan[r][3][11] = 3
        plan[1][1][11] = 0
    else:
        mine = jnp.where(col < 2, tiles[1], near)
        mine = [mine[: order // 2], mine[order // 2 :]]
        left0 = [doubling(v, "col", 0, cols) for v in halves]
        left1 = [doubling(v, "col", 1, cols) for v in halves]
        top0 = [doubling(v, "row", 0, rows) for v in mine]
        top1 = [doubling(v, "row", 1, rows) for v in mine]
        tile01 = move(halves, [((0, 1), (0, 0))], cols)
        tile11 = move(near, [((1, 1), (0, 0))], cols)
        raws = left0 + left1 + top0 + top1
        for r in range(rows):
            for c in range(cols):
                plan[r][c][1:6] = [1, 2, 3, 4, 1]
    meta = jnp.array(plan, jnp.int32)[row, col]
    meta = meta.at[8].set(edge_live.astype(jnp.int32))

    pieces, copies, state = [], [], None
    r5, r6, r7 = [], [], []
    drain = max(STAGES[0], steps + STAGES[1]) - steps if routed else 0
    for slot in range(count + drain):
        if slot < count:
            step, local = divmod(slot, steps)
            n = order - local * BLOCK
            if slot == 0:
                args = ("first", owner, n, 2 * n, tiles, *tile01)
            elif local == 0:
                args = ("schur", owner, n, n, tile11, *pieces)
            else:
                args = ("next", owner, n, n + (1 - step) * order, state)
            piece, state = factor_block(*args)
            pieces.append(piece)
            copies.append([])
            if not routed:
                copies[-1].append(doubling(doubling(piece, "row", 0, rows), "col", 0, cols))
        if not routed:
            continue
        arrived = {}
        for p in range(max(0, slot - max(STAGES)), min(slot, count)):
            got, k = copies[p], slot - p
            if k > STAGES[p // steps]:
                continue
            if p < steps:
                if k == 1:
                    new = [move(pieces[p], [((0, 0), (0, 1))], cols)]
                elif k == 2:
                    new = [move(got[0], [((0, 1), (1, 1))], cols)]
                elif k == 3:
                    via = choose(meta[9:10], [got[0], got[1]])
                    new = [move(via, [((r, 1), (r + 2, 1)) for r in (0, 1)], cols)]
                elif k == 4:
                    new = [move(got[2], [((r, 1), (r + 2, 1)) for r in (2, 3)], cols)]
                elif k == 5:
                    via = choose(meta[10:11], [got[2], got[3]])
                    new = [move(via, [((r, 1), (r, 3)) for r in workers], cols)]
                else:
                    via = choose(meta[11:12], [got[1], got[2], got[3], got[4]])
                    pairs = [((r, c), (r, c - 1)) for r in workers for c in (1, 3)]
                    new = [move(via, pairs + [((1, 1), (1, 0))], cols)]
            elif k == 1:
                new = [move(pieces[p], [((0, 0), (1, 0))], cols)]
            elif k == 2:
                via = choose(meta[15:16], [pieces[p], got[0]])
                new = [
                    move(via, [((r, 0), (r + far, 0)) for r in (0, 1)], cols) for far in (2, 4)
                ]
            else:
                via = choose(meta[16:17], got)
                new = [
                    move(via, [((r, 0), (r, c)) for r in workers] + also, cols)
                    for c, also in ((2, []), (1, [((1, 0), (1, 1))]), (3, []))
                ]
            arrived[p] = new
        late = []
        if slot == 0:
            late = [r2[0], r3[0], r4[0]]
        elif slot == 1:
            late = [r2[1], r3[1], r4[1]]
        elif slot == 2:
            late = [r5[0], r6[0]]
        elif slot == 3:
            late = [r5[1], r6[1], tile11]
        elif slot == 5:
            late = r7
        flowing = ([pieces[slot]] if slot < count else []) + ([] if state is None else [state])
        flowing, arrived, late = lax.optimization_barrier((flowing, arrived, late))
        if slot < count:
            pieces[slot] = flowing[0]
        if state is not None:
            state = flowing[-1]
        for p, new in arrived.items():
            copies[p] += new
        if slot < 2:
            r2[slot], r3[slot], r4[slot] = late
            r5.append(move(r2[slot], both_ways([((r, 2), (r, 3)) for r in workers]), cols))
            r6.append(
                move(
                    choose(meta[12:13], [r2[slot], r3[slot], r4[slot]]),
                    both_ways([((2, c), (3, c)) for c in range(4)] + [((4, c), (5, c)) for c in (2, 3)]),
                    cols,
                )
            )
        elif slot == 2:
            r5[0], r6[0] = late
        elif slot == 3:
            r5[1], r6[1], tile11 = late
            r7 = [
                move(
                    choose(meta[13:14], [r3[h], r4[h], r6[h]]),
                    [((4, 0), (4, 1)), ((5, 1), (5, 0)), ((2, 1), (2, 0)), ((3, 0), (3, 1))]
                    + [((2, 0), (2, 1)), ((3, 1), (3, 0)), ((2, 2), (2, 3)), ((3, 3), (3, 2))],
                    cols,
                )
                for h in range(2)
            ]
        elif slot == 5:
            r7 = late

    if routed:
        sets = [pieces] + [[got[k] for got in copies] for k in (1, 2, 3, 4, 5)]
        last_pieces = sets[3][steps:]
        raws = r1 + r2 + r3 + r4 + r5 + r6 + r7
    else:
        sets = [[got[0] for got in copies]]
        last_pieces = sets[0][steps:]

    def fetch():
        if routed:
            e0 = move(near, [((edge, 1), (edge - 2, 2))], cols)
            e1 = move(e0, [((edge - 2, 2), (edge - 4, 2))], cols)
            e2 = move(e0 + e1, [((r, 2), (r + 1, 2)) for r in (2, 4)], cols)
            return e0 + e1 + e2
        total = jnp.zeros_like(near)
        for r in workers:
            total = total + move(near, [((edge, 1), (r, 2))], cols)
        return total

    result, panel1 = finish(meta, tiles, raws, sets)
    flags = jnp.stack(
        [
            (row == edge) & (col >= 1),
            ((row == edge) & (col <= 2)) | ((row >= 2) & (row < edge) & (col == 2)),
        ]
    ).astype(jnp.int32)

    def with_edge(_, result):
        far = tiles[1]
        last = eliminate_last(fetch(), last_pieces)
        column = far - dot(panel1, last, NT, lax.Precision.HIGH)
        sent = move(column, [((r, 2), (edge, r % cols)) for r in workers], cols).T
        solved = move(last, [((edge - 2, 2), (edge, 1)), ((edge - 1, 2), (edge, 2))], cols)
        corner = far - dot(solved, solved, NT, lax.Precision.HIGH)
        part0 = jnp.where(col == 1, solved, sent)
        part1 = jnp.where(row == edge, jnp.where(col == 2, corner, sent), column)
        return patch(flags, result, (part0, part1))

    result = lax.fori_loop(0, edge_live.astype(jnp.int32), with_edge, result)
    return result.reshape(kernel_tiles.shape)


def solution(mesh):
    placed = (P(None, "row", None, "col", None, None), P())
    return jax.shard_map(
        on_device,
        mesh=mesh,
        in_specs=placed,
        out_specs=P(None, "row", None, "col", None, None),
        check_vma=False,
    )
```

```python
import jax
import jax.numpy as jnp
from jax import lax
from jax.experimental import pallas as pl
from jax.experimental.pallas import tpu as pltpu
from jax.sharding import PartitionSpec as P

SUB = 8
BASE = 128
BLOCK = 256
STAGES = (6, 3)
FIRST = 2
SECOND = 5
THIRD = 7
NN = ((1,), (0,))
NT = ((1,), (1,))
TN = ((0,), (0,))
ANY = pl.BlockSpec(memory_space=pl.ANY)
SMEM = pl.BlockSpec(memory_space=pltpu.SMEM)
DMA = pltpu.SemaphoreType.DMA
F32 = jnp.float32


def dot(a, b, dims, precision=lax.Precision.HIGHEST):
    return lax.dot_general(
        a, b, (dims, ((), ())), precision=precision, preferred_element_type=jnp.float32
    )


def down(x, j):
    return jnp.broadcast_to(x[j : j + 1, :], x.shape)


def along(x, j):
    return jnp.broadcast_to(x[:, j : j + 1], x.shape)


def factor_base(diag):
    sub = lax.broadcasted_iota(jnp.int32, (SUB, BASE), 0)
    lane = lax.broadcasted_iota(jnp.int32, (SUB, BASE), 1)
    count = BASE // SUB
    left = [diag[SUB * t : SUB * t + SUB, :] for t in range(count)]
    right = [(lane == sub + SUB * t).astype(jnp.float32) for t in range(count)]
    upper, inverse = [], []
    for t in range(count):
        a, b = left[t], right[t]
        cols = [along(a, SUB * t + j) for j in range(SUB)]
        ua, ub, pivots = a, b, None
        for j in range(SUB):
            mine = sub == j
            pivot = down(cols[j], j)
            recip = 1.0 / pivot
            if j:
                ua = jnp.where(sub >= j, a, ua)
                ub = jnp.where(sub >= j, b, ub)
                pivots = jnp.where(sub >= j, pivot, pivots)
            else:
                pivots = pivot
            mult = cols[j]
            row = down(a, j) * recip
            a = jnp.where(mine, row, a - mult * row)
            row = down(b, j) * recip
            b = jnp.where(mine, row, b - mult * row)
            for k in range(j + 1, SUB):
                row = down(cols[k], j) * recip
                cols[k] = jnp.where(mine, row, cols[k] - mult * row)
        scale = lax.rsqrt(pivots)
        upper.append(jnp.where(lane >= sub + SUB * t, ua * scale, 0.0))
        inverse.append(ub * scale)
        if t + 1 < count:
            va = [down(a, j) for j in range(SUB)]
            vb = [down(b, j) for j in range(SUB)]
            for i in range(t + 1, count):
                mult = [along(left[i], SUB * t + j) for j in range(SUB)]
                for j in range(SUB):
                    left[i] = left[i] - mult[j] * va[j]
                    right[i] = right[i] - mult[j] * vb[j]
    return jnp.concatenate(upper, 0), jnp.concatenate(inverse, 0)


def params(limit_mib=48):
    return pltpu.CompilerParams(vmem_limit_bytes=limit_mib << 20)


def shape(*dims):
    return jax.ShapeDtypeStruct(dims, F32)


def factor_kernel(kind, flag_ref, *refs):
    refs = list(refs)
    sources = [refs.pop(0) for _ in range({"first": 2, "next": 1, "schur": 5}[kind])]
    a_ref, f_ref, sems = refs[-3:]
    f_out = refs[0]
    rest_out = refs[1] if len(refs) > 4 else None
    n, m = a_ref.shape
    top, below = pl.ds(0, BLOCK), pl.ds(BLOCK, n - BLOCK)

    @pl.when(flag_ref[0] == 1)
    def _():
        copies = []

        def load(source, target):
            copies.append(pltpu.make_async_copy(source, target, sems.at[len(copies)]))
            copies[-1].start()

        if kind == "first":
            for rows in (top, below):
                load(sources[0].at[0, rows], a_ref.at[rows, pl.ds(0, n)])
                load(sources[1].at[rows], a_ref.at[rows, pl.ds(n, n)])
            needed = 2
        elif kind == "next":
            load(sources[0].at[top], a_ref.at[top])
            if n > BLOCK:
                load(sources[0].at[below], a_ref.at[below])
            needed = 1
        else:
            parts = refs[-4]
            load(sources[0], a_ref)
            for p, part in enumerate(sources[1:]):
                load(
                    part.at[:, pl.ds(part.shape[1] - n, n)],
                    parts.at[pl.ds(p * BLOCK, BLOCK)],
                )
            needed = len(copies)
        for copy in copies[:needed]:
            copy.wait()
        if kind == "schur":
            for r in range(0, n, BLOCK):
                lhs = parts[:, r : r + BLOCK].T
                for c in range(r, n, BLOCK):
                    a_ref[r : r + BLOCK, c : c + BLOCK] -= dot(lhs, parts[:, c : c + BLOCK], NN)

        first, second = pl.ds(0, BASE), pl.ds(BASE, BASE)
        sub = lax.broadcasted_iota(jnp.int32, (BASE, BASE), 0)
        lane = lax.broadcasted_iota(jnp.int32, (BASE, BASE), 1)
        x_ref = refs[-4] if kind != "schur" else refs[-5]

        def base(b, carry):
            rows = pl.ds(pl.multiple_of(b * BASE, BASE), BASE)
            u, x = factor_base(a_ref[rows, rows])
            f_ref[rows, rows] = jnp.where(sub <= lane, u, x)
            x_ref[rows, rows] = x

            @pl.when(b == 0)
            def _():
                u12 = dot(x, a_ref[first, second], NN)
                f_ref[first, second] = u12
                a_ref[second, second] -= dot(u12, u12, TN)

            return carry

        lax.fori_loop(0, BLOCK // BASE, base, 0)
        x21 = -dot(x_ref[second, second], dot(f_ref[first, second], x_ref[first, first], TN), NN)
        f_ref[second, first] = x21
        x_ref[second, first] = x21
        x_ref[first, second] = jnp.zeros((BASE, BASE), F32)
        x = x_ref[...]
        for c in range(BLOCK, m, BLOCK):
            f_ref[:, c : c + BLOCK] = dot(x, a_ref[top, c : c + BLOCK], NN)
        leaving = [pltpu.make_async_copy(f_ref, f_out, sems.at[len(copies)])]
        leaving[0].start()
        for copy in copies[needed:]:
            copy.wait()
        for r in range(BLOCK, n, BLOCK):
            lhs = f_ref[:, r : r + BLOCK].T
            for c in range(r, m, BLOCK):
                a_ref[r : r + BLOCK, c : c + BLOCK] -= dot(lhs, f_ref[:, c : c + BLOCK], NN)
            rows = pl.ds(r, BLOCK)
            leaving.append(
                pltpu.make_async_copy(
                    a_ref.at[rows, pl.ds(BLOCK, m - BLOCK)],
                    rest_out.at[pl.ds(r - BLOCK, BLOCK)],
                    sems.at[len(copies) + len(leaving)],
                )
            )
            leaving[-1].start()
        for copy in leaving:
            copy.wait()


def factor_block(kind, flag, n, m, *sources):
    shapes = [shape(BLOCK, m)]
    if n > BLOCK:
        shapes.append(shape(n - BLOCK, m - BLOCK))
    scratch = [pltpu.VMEM((BLOCK, BLOCK), F32)]
    if kind == "schur":
        scratch.append(pltpu.VMEM((n, n), F32))
    scratch += [pltpu.VMEM((n, m), F32), pltpu.VMEM((BLOCK, m), F32), DMA((12,))]
    out = pl.pallas_call(
        lambda *refs: factor_kernel(kind, *refs),
        out_shape=shapes,
        in_specs=[SMEM] + [ANY] * len(sources),
        out_specs=[ANY] * len(shapes),
        scratch_shapes=scratch,
        cost_estimate=pl.CostEstimate(
            flops=2_000_000_000, bytes_accessed=8 * n * m, transcendentals=0
        ),
        compiler_params=params(),
    )(flag, *sources)
    return out if n > BLOCK else (out[0], None)


def choose(index, options):
    def kernel(index_ref, *refs):
        *bufs, out_ref, held, sem = refs
        for k, buf in enumerate(bufs):

            @pl.when(index_ref[0] == k)
            def _():
                copy = pltpu.make_async_copy(buf, held, sem)
                copy.start()
                copy.wait()

        @pl.when(index_ref[0] >= 0)
        def _():
            copy = pltpu.make_async_copy(held, out_ref, sem)
            copy.start()
            copy.wait()

    return pl.pallas_call(
        kernel,
        out_shape=shape(*options[0].shape),
        in_specs=[SMEM] + [ANY] * len(options),
        out_specs=ANY,
        scratch_shapes=[pltpu.VMEM(options[0].shape, F32), DMA(())],
        compiler_params=params(8),
    )(index, *options)


def unset(like):
    return pl.pallas_call(
        lambda out_ref: None, out_shape=shape(*like.shape), in_specs=[], out_specs=ANY
    )()


def patch(flags, result, parts):
    def kernel(flags_ref, result_ref, *refs):
        *bufs, out_ref, held, sem = refs
        for k, buf in enumerate(bufs):

            @pl.when(flags_ref[k] == 1)
            def _():
                for source, target in ((buf, held), (held, out_ref.at[k])):
                    copy = pltpu.make_async_copy(source, target, sem)
                    copy.start()
                    copy.wait()

    return pl.pallas_call(
        kernel,
        out_shape=shape(*result.shape),
        in_specs=[SMEM] + [ANY] * (1 + len(parts)),
        out_specs=ANY,
        scratch_shapes=[pltpu.VMEM(parts[0].shape, F32), DMA(())],
        input_output_aliases={1: 0},
        compiler_params=params(8),
    )(flags, result, *parts)


def split(x):
    high = x.astype(jnp.bfloat16)
    return high, (x - high.astype(F32)).astype(jnp.bfloat16)


def dot3(a, b, dims):
    total = None
    for x, y in ((a[1], b[0]), (a[0], b[1]), (a[0], b[0])):
        part = lax.dot_general(x, y, (dims, ((), ())), preferred_element_type=F32)
        total = part if total is None else total + part
    return total


PASS, WORK, ZERO, LOWER0, PANEL0, LOWER1 = range(6)


def finish_kernel(n_raw, n_sets, meta_ref, *refs):
    tiles_ref, raws, refs = refs[0], refs[1 : 1 + n_raw], refs[1 + n_raw :]
    order = tiles_ref.shape[-1]
    steps = order // BLOCK
    count = 2 * steps
    sets = [refs[k * count : (k + 1) * count] for k in range(n_sets)]
    out_ref, p1_ref, z, t, spare, high, low, *fs, sems = refs[n_sets * count :]
    role, transposed, col, edge = (meta_ref[k] for k in (0, 5, 7, 8))
    which = meta_ref[6], meta_ref[14]
    half = pl.ds(0, order), pl.ds(order, order)
    sources = [tiles_ref.at[0]] + list(raws)

    def load_pieces(pieces):
        for k in range(n_sets):
            for step in range(2):

                @pl.when(which[step] == k)
                def _():
                    for p in pieces:
                        if p // steps == step:
                            pltpu.make_async_copy(sets[k][p], fs[p], sems.at[8 + p]).start()

    def await_piece(p):
        pltpu.make_async_copy(sets[0][p], fs[p], sems.at[8 + p]).wait()

    def move_out(source, target, sem):
        copy = pltpu.make_async_copy(source, target, sems.at[sem])
        copy.start()
        return copy

    @pl.when(role == PASS)
    def _():
        held = (t, spare)
        copies = [move_out(tiles_ref.at[k], held[k], k) for k in range(2)]
        for k in range(2):
            copies[k].wait()
            copies[k] = move_out(held[k], out_ref.at[k], k)
        for copy in copies:
            copy.wait()

    @pl.when(role >= ZERO)
    def _():
        t[...] = jnp.zeros((order, order), F32)
        move_out(t, out_ref.at[1], 1).wait()

        def upper_block(p, q, lead):
            base = lead + (q - p) * BLOCK
            return fs[p][:, base : base + BLOCK].T

        def triangle(offset):
            sub = lax.broadcasted_iota(jnp.int32, (BLOCK, BLOCK), 0)
            lane = lax.broadcasted_iota(jnp.int32, (BLOCK, BLOCK), 1)
            for p in range(steps):
                for q in range(p, steps):
                    block = fs[offset + p][:, (q - p) * BLOCK : (q - p + 1) * BLOCK]
                    if p == q:
                        block = jnp.where(sub <= lane, block, 0.0)
                    t[q * BLOCK : (q + 1) * BLOCK, p * BLOCK : (p + 1) * BLOCK] = block.T

        for kind, pieces in (
            (LOWER0, range(steps)),
            (PANEL0, range(steps)),
            (LOWER1, range(steps, count)),
        ):

            @pl.when(role == kind)
            def _():
                load_pieces(pieces)
                for p in pieces:
                    await_piece(p)
                if kind == PANEL0:
                    for p in range(steps):
                        for q in range(steps):
                            t[q * BLOCK : (q + 1) * BLOCK, p * BLOCK : (p + 1) * BLOCK] = (
                                upper_block(p, q, order - p * BLOCK + p * BLOCK)
                            )
                else:
                    triangle(pieces[0])

        move_out(t, out_ref.at[0], 0).wait()

    @pl.when(role == WORK)
    def _():
        places = [z.at[half[a], half[b]] for a in range(2) for b in range(2)]
        for s, place in enumerate(places):
            for k, source in enumerate(sources):

                @pl.when(meta_ref[1 + s] == k)
                def _():
                    pltpu.make_async_copy(source, place, sems.at[s]).start()

        load_pieces(range(count))
        for slot, taken in ((1, col < 2), (0, col >= 2)):

            @pl.when(taken)
            def _():
                pltpu.make_async_copy(tiles_ref.at[slot], t, sems.at[4]).start()

        @pl.when(col >= 2)
        def _():
            move_out(tiles_ref.at[1], spare, 5)

        for s, place in enumerate(places):
            pltpu.make_async_copy(sources[1], place, sems.at[s]).wait()

        @pl.when(transposed == 1)
        def _():
            for left in (0, order):
                for a in range(steps):
                    for b in range(a, steps):
                        ra = order + a * BLOCK, left + a * BLOCK
                        rb = order + b * BLOCK, left + b * BLOCK
                        upper = z[ra[0] : ra[0] + BLOCK, rb[1] : rb[1] + BLOCK].T
                        if a != b:
                            z[ra[0] : ra[0] + BLOCK, rb[1] : rb[1] + BLOCK] = z[
                                rb[0] : rb[0] + BLOCK, ra[1] : ra[1] + BLOCK
                            ].T
                        z[rb[0] : rb[0] + BLOCK, ra[1] : ra[1] + BLOCK] = upper

        sub = lax.broadcasted_iota(jnp.int32, (BLOCK, BLOCK), 0)
        lane = lax.broadcasted_iota(jnp.int32, (BLOCK, BLOCK), 1)
        for p in range(count):
            await_piece(p)
            packed = fs[p][:, :BLOCK]
            inverse = jnp.where(
                sub > lane, packed, jnp.where(sub == lane, 1.0 / packed, 0.0)
            )
            inverse = split(inverse)
            for rows in half:
                solved = dot3(
                    split(z[rows, p * BLOCK : (p + 1) * BLOCK]), inverse, NT
                )
                z[rows, p * BLOCK : (p + 1) * BLOCK] = solved
                solved = split(solved)
                high[rows, :] = solved[0]
                low[rows, :] = solved[1]

            def eliminate(q, carry):
                to = pl.ds(pl.multiple_of(q * BLOCK, BLOCK), BLOCK)
                u = split(fs[p][:, pl.ds(pl.multiple_of((q - p) * BLOCK, BLOCK), BLOCK)])
                for rows in half:
                    z[rows, to] -= dot3((high[rows, :], low[rows, :]), u, NN)
                return carry

            lax.fori_loop(p + 1, count, eliminate, 0)
            if p == 0:
                pltpu.make_async_copy(tiles_ref.at[0], t, sems.at[4]).wait()

            def update(r, carry):
                rows = pl.ds(pl.multiple_of(r * BLOCK, BLOCK), BLOCK)
                others = high[half[1], :], low[half[1], :]
                t[rows, :] -= dot3((high[rows, :], low[rows, :]), others, NT)
                return carry

            lax.fori_loop(0, steps, update, 0)

        @pl.when(col >= 2)
        def _():
            pltpu.make_async_copy(tiles_ref.at[1], spare, sems.at[5]).wait()
            move_out(spare, out_ref.at[1], 5)

        @pl.when(col == 0)
        def _():
            move_out(z.at[half[0], half[0]], out_ref.at[0], 5)

        @pl.when(col == 1)
        def _():
            move_out(z.at[half[0], half[1]], out_ref.at[0], 5)

        for slot, taken in ((1, col < 2), (0, col >= 2)):

            @pl.when(taken)
            def _():
                move_out(t, out_ref.at[slot], 6)

        @pl.when((col == 2) & (edge == 1))
        def _():
            move_out(z.at[half[0], half[1]], p1_ref, 7).wait()

        pltpu.make_async_copy(t, out_ref.at[0], sems.at[5]).wait()
        pltpu.make_async_copy(t, out_ref.at[0], sems.at[6]).wait()


def finish(meta, tiles, raws, sets):
    order = tiles.shape[-1]
    count = len(sets[0])
    flat = [f for s in sets for f in s]
    scratch = [
        pltpu.VMEM((2 * order, 2 * order), F32),
        pltpu.VMEM((order, order), F32),
        pltpu.VMEM((order, order), F32),
        pltpu.VMEM((2 * order, BLOCK), jnp.bfloat16),
        pltpu.VMEM((2 * order, BLOCK), jnp.bfloat16),
    ]
    scratch += [pltpu.VMEM(f.shape, F32) for f in sets[0]] + [DMA((8 + count,))]
    return pl.pallas_call(
        lambda *refs: finish_kernel(len(raws), len(sets), *refs),
        out_shape=[shape(*tiles.shape), shape(order, order)],
        in_specs=[SMEM] + [ANY] * (1 + len(raws) + len(flat)),
        out_specs=[ANY, ANY],
        scratch_shapes=scratch,
        cost_estimate=pl.CostEstimate(
            flops=60_000_000_000, bytes_accessed=64 << 20, transcendentals=0
        ),
        compiler_params=params(56),
    )(meta, tiles, *raws, *flat)


def move(value, pairs, cols):
    flat = [(a * cols + b, c * cols + d) for (a, b), (c, d) in pairs]
    return lax.ppermute(value, ("row", "col"), flat)


def doubling(value, axis, root, size):
    place = lax.rem(lax.axis_index(axis) - root + size, size)
    reach = 1
    while reach < size:
        pairs = [
            ((root + i) % size, (root + i + reach) % size) for i in range(min(reach, size - reach))
        ]
        value = jnp.where(place >= reach, lax.ppermute(value, axis, pairs), value)
        reach *= 2
    return value


def both_ways(pairs):
    return pairs + [(b, a) for a, b in pairs]


def eliminate_last(panel, pieces):
    done = []
    for f in pieces:
        packed = f[:, :BLOCK]
        inverse = jnp.tril(packed, -1) + jnp.diag(1.0 / jnp.diagonal(packed))
        part = dot(panel[:, :BLOCK], inverse, NT, lax.Precision.HIGH)
        done.append(part)
        if f.shape[1] > BLOCK:
            panel = panel[:, BLOCK:] - dot(part, f[:, BLOCK:], NN, lax.Precision.HIGH)
    return jnp.concatenate(done, 1)


def on_device(kernel_tiles, profile):
    order = kernel_tiles.shape[-1]
    rows, cols = lax.axis_size("row"), lax.axis_size("col")
    row, col = lax.axis_index("row"), lax.axis_index("col")
    tiles = kernel_tiles.reshape(2, order, order)
    near = tiles[0]
    steps = order // BLOCK
    count = 2 * steps
    edge = cols + 2
    edge_live = profile[0, edge] <= 1
    owner = jnp.reshape(((row == 0) & (col == 0)).astype(jnp.int32), (1,))
    workers = range(2, edge)
    routed = cols == 4

    plan = [[[PASS] + [0] * 8 + [-1] * 5 + [0, -1, -1] for _ in range(cols)] for _ in range(rows)]
    for r in range(rows):
        for c in range(cols):
            plan[r][c][7] = c
            if r < 2:
                plan[r][c][0] = ZERO
            elif r < edge:
                plan[r][c][0] = WORK
    plan[0][0][0], plan[1][0][0], plan[1][1][0] = LOWER0, PANEL0, LOWER1

    if routed:
        r1 = move(near, both_ways([((r, 0), (r, 1)) for r in (0,) + tuple(workers)]), cols)
        r2 = move(
            near,
            [((r, c), (r, c + 2)) for r in workers for c in (0, 1)],
            cols,
        )
        r3 = move(
            near,
            both_ways([((4, c), (5, c)) for c in (0, 1)])
            + [((r, c), (r + 4, c)) for r in (0, 1) for c in (2, 3)],
            cols,
        )
        r4 = move(near, [((r, c), (r - 2, c)) for r in (4, 5) for c in (0, 1)], cols)
        tile01, tile11 = r1, move(near, [((1, 1), (0, 0))], cols)
        for r in workers:
            plan[r][0][1:3] = [0, 1]
            plan[r][1][1:3] = [1, 0]
            plan[r][2][1:3] = [2, 5]
            plan[r][3][1:3] = [5, 2]
            for c in range(4):
                plan[r][c][3:5] = plan[r][c][1:3]
        for place, pair in {
            (2, 0): (4, 7), (2, 1): (7, 6), (3, 0): (6, 7), (3, 1): (7, 4),
            (4, 1): (7, 3), (5, 0): (3, 7), (2, 3): (7, 6), (3, 2): (6, 7),
            (4, 2): (3, 6), (4, 3): (3, 6), (5, 2): (6, 3), (5, 3): (6, 3),
        }.items():
            plan[place[0]][place[1]][3:5] = pair
        for c in (0, 1):
            plan[2][c][12] = plan[3][c][12] = 2
        for c in (2, 3):
            plan[2][c][12] = plan[3][c][12] = 0
            plan[4][c][12] = plan[5][c][12] = 1
        plan[4][0][13] = plan[5][1][13] = 0
        plan[2][1][13] = plan[3][0][13] = 1
        plan[2][0][13] = plan[3][1][13] = plan[2][2][13] = plan[3][3][13] = 2
        for r in (4, 5):
            for c in (2, 3):
                plan[r][c][5] = 1
        plan[1][1][6] = 1
        for r in workers:
            plan[r][1][6] = plan[r][3][6] = 2 if r < 4 else 3
            plan[r][3][6] = 4
        for r in (1,) + tuple(workers):
            plan[r][0][6] = plan[r][2][6] = 5
        plan[1][1][14] = 4
        plan[0][0][15], plan[1][0][15], plan[1][0][16] = 0, 1, 0
        for r in workers:
            plan[r][0][14:17] = [1, -1, 1] if r < 4 else [2, -1, 2]
            plan[r][1][14], plan[r][2][14], plan[r][3][14] = 4, 3, 5
        plan[0][1][9], plan[1][1][9] = 0, 1
        for r in workers:
            plan[r][1][10] = 0 if r < 4 else 1
            plan[r][1][11] = 1 if r < 4 else 2
            plan[r][3][11] = 3
        plan[1][1][11] = 0
    else:
        mine = jnp.where(col < 2, tiles[1], near)
        left0 = doubling(near, "col", 0, cols)
        left1 = doubling(near, "col", 1, cols)
        top0 = doubling(mine, "row", 0, rows)
        top1 = doubling(mine, "row", 1, rows)
        tile01 = move(near, [((0, 1), (0, 0))], cols)
        tile11 = move(near, [((1, 1), (0, 0))], cols)
        raws = [left0, left1, top0, top1]
        for r in range(rows):
            for c in range(cols):
                plan[r][c][1:6] = [1, 2, 3, 4, 1]
    meta = jnp.array(plan, jnp.int32)[row, col]
    meta = meta.at[8].set(edge_live.astype(jnp.int32))

    pieces, copies, state = [], [], None
    drain = max(STAGES[0], steps + STAGES[1]) - steps if routed else 0
    for slot in range(count + drain):
        if slot < count:
            step, local = divmod(slot, steps)
            n = order - local * BLOCK
            if slot == 0:
                args = ("first", owner, n, 2 * n, tiles, tile01)
            elif local == 0:
                args = ("schur", owner, n, n, tile11, *pieces)
            else:
                args = ("next", owner, n, n + (1 - step) * order, state)
            piece, state = factor_block(*args)
            pieces.append(piece)
            copies.append([])
            if not routed:
                copies[-1].append(doubling(doubling(piece, "row", 0, rows), "col", 0, cols))
        if not routed:
            continue
        arrived = {}
        for p in range(max(0, slot - max(STAGES)), min(slot, count)):
            got, k = copies[p], slot - p
            if k > STAGES[p // steps]:
                continue
            if p < steps:
                if k == 1:
                    new = [move(pieces[p], [((0, 0), (0, 1))], cols)]
                elif k == 2:
                    new = [move(got[0], [((0, 1), (1, 1))], cols)]
                elif k == 3:
                    via = choose(meta[9:10], [got[0], got[1]])
                    new = [move(via, [((r, 1), (r + 2, 1)) for r in (0, 1)], cols)]
                elif k == 4:
                    new = [move(got[2], [((r, 1), (r + 2, 1)) for r in (2, 3)], cols)]
                elif k == 5:
                    via = choose(meta[10:11], [got[2], got[3]])
                    new = [move(via, [((r, 1), (r, 3)) for r in workers], cols)]
                else:
                    via = choose(meta[11:12], [got[1], got[2], got[3], got[4]])
                    pairs = [((r, c), (r, c - 1)) for r in workers for c in (1, 3)]
                    new = [move(via, pairs + [((1, 1), (1, 0))], cols)]
            elif k == 1:
                new = [move(pieces[p], [((0, 0), (1, 0))], cols)]
            elif k == 2:
                via = choose(meta[15:16], [pieces[p], got[0]])
                new = [
                    move(via, [((r, 0), (r + far, 0)) for r in (0, 1)], cols) for far in (2, 4)
                ]
            else:
                via = choose(meta[16:17], got)
                new = [
                    move(via, [((r, 0), (r, c)) for r in workers] + also, cols)
                    for c, also in ((2, []), (1, [((1, 0), (1, 1))]), (3, []))
                ]
            arrived[p] = new
        late = []
        if slot == FIRST:
            late = [r2, r3, r4, tile11]
        elif slot == SECOND:
            late = [r5, r6]
        elif slot == THIRD:
            late = [r7]
        flowing = ([pieces[slot]] if slot < count else []) + ([] if state is None else [state])
        flowing, arrived, late = lax.optimization_barrier((flowing, arrived, late))
        if slot < count:
            pieces[slot] = flowing[0]
        if state is not None:
            state = flowing[-1]
        for p, new in arrived.items():
            copies[p] += new
        if slot == FIRST:
            r2, r3, r4, tile11 = late
            r5 = move(r2, both_ways([((r, 2), (r, 3)) for r in workers]), cols)
            r6 = move(
                choose(meta[12:13], [r2, r3, r4]),
                both_ways([((2, c), (3, c)) for c in range(4)] + [((4, c), (5, c)) for c in (2, 3)]),
                cols,
            )
        elif slot == SECOND:
            r5, r6 = late
            r7 = move(
                choose(meta[13:14], [r3, r4, r6]),
                [((4, 0), (4, 1)), ((5, 1), (5, 0)), ((2, 1), (2, 0)), ((3, 0), (3, 1))]
                + [((2, 0), (2, 1)), ((3, 1), (3, 0)), ((2, 2), (2, 3)), ((3, 3), (3, 2))],
                cols,
            )
        elif slot == THIRD:
            (r7,) = late

    if routed:
        sets = [pieces] + [[got[k] for got in copies] for k in (1, 2, 3, 4, 5)]
        last_pieces = sets[3][steps:]
        raws = [r1, r2, r3, r4, r5, r6, r7]
    else:
        sets = [[got[0] for got in copies]]
        last_pieces = sets[0][steps:]

    def fetch():
        if routed:
            e0 = move(near, [((edge, 1), (edge - 2, 2))], cols)
            e1 = move(e0, [((edge - 2, 2), (edge - 4, 2))], cols)
            e2 = move(e0 + e1, [((r, 2), (r + 1, 2)) for r in (2, 4)], cols)
            return e0 + e1 + e2
        total = jnp.zeros_like(near)
        for r in workers:
            total = total + move(near, [((edge, 1), (r, 2))], cols)
        return total

    result, panel1 = finish(meta, tiles, raws, sets)
    at_edge = edge_live & (row == edge)
    flags = jnp.stack(
        [
            at_edge & (col >= 1),
            (at_edge & (col <= 2)) | (edge_live & (row >= 2) & (row < edge) & (col == 2)),
        ]
    ).astype(jnp.int32)

    def edge_parts(args):
        panel1, last_pieces = args
        far = tiles[1]
        last = eliminate_last(fetch(), last_pieces)
        column = far - dot(panel1, last, NT, lax.Precision.HIGH)
        sent = move(column, [((r, 2), (edge, r % cols)) for r in workers], cols).T
        solved = move(last, [((edge - 2, 2), (edge, 1)), ((edge - 1, 2), (edge, 2))], cols)
        corner = far - dot(solved, solved, NT, lax.Precision.HIGH)
        part0 = jnp.where(col == 1, solved, sent)
        part1 = jnp.where(row == edge, jnp.where(col == 2, corner, sent), column)
        return part0, part1

    def no_edge(args):
        return unset(near), unset(near)

    parts = lax.cond(edge_live, edge_parts, no_edge, (panel1, last_pieces))
    return patch(flags, result, parts).reshape(kernel_tiles.shape)


def solution(mesh):
    placed = (P(None, "row", None, "col", None, None), P())
    return jax.shard_map(
        on_device,
        mesh=mesh,
        in_specs=placed,
        out_specs=P(None, "row", None, "col", None, None),
        check_vma=False,
    )
```

```python
import jax
import jax.numpy as jnp
from jax import lax
from jax.experimental import pallas as pl
from jax.experimental.pallas import tpu as pltpu
from jax.sharding import PartitionSpec as P

SUB = 8
BASE = 128
BLOCK = 256
STAGES = (6, 3)
FIRST = 2
SECOND = (4, 6)
THIRD = 8
NN = ((1,), (0,))
NT = ((1,), (1,))
TN = ((0,), (0,))
ANY = pl.BlockSpec(memory_space=pl.ANY)
SMEM = pl.BlockSpec(memory_space=pltpu.SMEM)
DMA = pltpu.SemaphoreType.DMA
F32 = jnp.float32


def dot(a, b, dims, precision=lax.Precision.HIGHEST):
    return lax.dot_general(
        a, b, (dims, ((), ())), precision=precision, preferred_element_type=jnp.float32
    )


def down(x, j):
    return jnp.broadcast_to(x[j : j + 1, :], x.shape)


def along(x, j):
    return jnp.broadcast_to(x[:, j : j + 1], x.shape)


def factor_base(diag):
    sub = lax.broadcasted_iota(jnp.int32, (SUB, BASE), 0)
    lane = lax.broadcasted_iota(jnp.int32, (SUB, BASE), 1)
    count = BASE // SUB
    left = [diag[SUB * t : SUB * t + SUB, :] for t in range(count)]
    right = [(lane == sub + SUB * t).astype(jnp.float32) for t in range(count)]
    upper, inverse = [], []
    for t in range(count):
        a, b = left[t], right[t]
        cols = [along(a, SUB * t + j) for j in range(SUB)]
        ua, ub, pivots = a, b, None
        for j in range(SUB):
            mine = sub == j
            pivot = down(cols[j], j)
            recip = 1.0 / pivot
            if j:
                ua = jnp.where(sub >= j, a, ua)
                ub = jnp.where(sub >= j, b, ub)
                pivots = jnp.where(sub >= j, pivot, pivots)
            else:
                pivots = pivot
            mult = cols[j]
            row = down(a, j) * recip
            a = jnp.where(mine, row, a - mult * row)
            row = down(b, j) * recip
            b = jnp.where(mine, row, b - mult * row)
            for k in range(j + 1, SUB):
                row = down(cols[k], j) * recip
                cols[k] = jnp.where(mine, row, cols[k] - mult * row)
        scale = lax.rsqrt(pivots)
        upper.append(jnp.where(lane >= sub + SUB * t, ua * scale, 0.0))
        inverse.append(ub * scale)
        if t + 1 < count:
            va = [down(a, j) for j in range(SUB)]
            vb = [down(b, j) for j in range(SUB)]
            for i in range(t + 1, count):
                mult = [along(left[i], SUB * t + j) for j in range(SUB)]
                for j in range(SUB):
                    left[i] = left[i] - mult[j] * va[j]
                    right[i] = right[i] - mult[j] * vb[j]
    return jnp.concatenate(upper, 0), jnp.concatenate(inverse, 0)


def params(limit_mib=48):
    return pltpu.CompilerParams(vmem_limit_bytes=limit_mib << 20)


def shape(*dims):
    return jax.ShapeDtypeStruct(dims, F32)


def factor_kernel(kind, flag_ref, *refs):
    refs = list(refs)
    sources = [refs.pop(0) for _ in range({"first": 2, "next": 1, "schur": 5}[kind])]
    a_ref, f_ref, sems = refs[-3:]
    f_out = refs[0]
    rest_out = refs[1] if len(refs) > 4 else None
    n, m = a_ref.shape
    top, below = pl.ds(0, BLOCK), pl.ds(BLOCK, n - BLOCK)

    @pl.when(flag_ref[0] == 1)
    def _():
        copies = []

        def load(source, target):
            copies.append(pltpu.make_async_copy(source, target, sems.at[len(copies)]))
            copies[-1].start()

        if kind == "first":
            for rows in (top, below):
                load(sources[0].at[0, rows], a_ref.at[rows, pl.ds(0, n)])
                load(sources[1].at[rows], a_ref.at[rows, pl.ds(n, n)])
            needed = 2
        elif kind == "next":
            load(sources[0].at[top], a_ref.at[top])
            if n > BLOCK:
                load(sources[0].at[below], a_ref.at[below])
            needed = 1
        else:
            parts = refs[-4]
            load(sources[0], a_ref)
            for p, part in enumerate(sources[1:]):
                load(
                    part.at[:, pl.ds(part.shape[1] - n, n)],
                    parts.at[pl.ds(p * BLOCK, BLOCK)],
                )
            needed = len(copies)
        for copy in copies[:needed]:
            copy.wait()
        if kind == "schur":
            for r in range(0, n, BLOCK):
                lhs = parts[:, r : r + BLOCK].T
                for c in range(r, n, BLOCK):
                    a_ref[r : r + BLOCK, c : c + BLOCK] -= dot(lhs, parts[:, c : c + BLOCK], NN)

        first, second = pl.ds(0, BASE), pl.ds(BASE, BASE)
        sub = lax.broadcasted_iota(jnp.int32, (BASE, BASE), 0)
        lane = lax.broadcasted_iota(jnp.int32, (BASE, BASE), 1)
        x_ref = refs[-4] if kind != "schur" else refs[-5]

        def base(b, carry):
            rows = pl.ds(pl.multiple_of(b * BASE, BASE), BASE)
            u, x = factor_base(a_ref[rows, rows])
            f_ref[rows, rows] = jnp.where(sub <= lane, u, x)
            x_ref[rows, rows] = x

            @pl.when(b == 0)
            def _():
                u12 = dot(x, a_ref[first, second], NN)
                f_ref[first, second] = u12
                a_ref[second, second] -= dot(u12, u12, TN)

            return carry

        lax.fori_loop(0, BLOCK // BASE, base, 0)
        x21 = -dot(x_ref[second, second], dot(f_ref[first, second], x_ref[first, first], TN), NN)
        f_ref[second, first] = x21
        x_ref[second, first] = x21
        x_ref[first, second] = jnp.zeros((BASE, BASE), F32)
        x = x_ref[...]
        for c in range(BLOCK, m, BLOCK):
            f_ref[:, c : c + BLOCK] = dot(x, a_ref[top, c : c + BLOCK], NN)
        leaving = [pltpu.make_async_copy(f_ref, f_out, sems.at[len(copies)])]
        leaving[0].start()
        for copy in copies[needed:]:
            copy.wait()
        for r in range(BLOCK, n, BLOCK):
            lhs = f_ref[:, r : r + BLOCK].T
            for c in range(r, m, BLOCK):
                a_ref[r : r + BLOCK, c : c + BLOCK] -= dot(lhs, f_ref[:, c : c + BLOCK], NN)
            rows = pl.ds(r, BLOCK)
            leaving.append(
                pltpu.make_async_copy(
                    a_ref.at[rows, pl.ds(BLOCK, m - BLOCK)],
                    rest_out.at[pl.ds(r - BLOCK, BLOCK)],
                    sems.at[len(copies) + len(leaving)],
                )
            )
            leaving[-1].start()
        for copy in leaving:
            copy.wait()


def factor_block(kind, flag, n, m, *sources):
    shapes = [shape(BLOCK, m)]
    if n > BLOCK:
        shapes.append(shape(n - BLOCK, m - BLOCK))
    scratch = [pltpu.VMEM((BLOCK, BLOCK), F32)]
    if kind == "schur":
        scratch.append(pltpu.VMEM((n, n), F32))
    scratch += [pltpu.VMEM((n, m), F32), pltpu.VMEM((BLOCK, m), F32), DMA((12,))]
    out = pl.pallas_call(
        lambda *refs: factor_kernel(kind, *refs),
        out_shape=shapes,
        in_specs=[SMEM] + [ANY] * len(sources),
        out_specs=[ANY] * len(shapes),
        scratch_shapes=scratch,
        cost_estimate=pl.CostEstimate(
            flops=2_000_000_000, bytes_accessed=8 * n * m, transcendentals=0
        ),
        compiler_params=params(),
    )(flag, *sources)
    return out if n > BLOCK else (out[0], None)


def choose(index, options, rows=None):
    options = [o if isinstance(o, list) else [o] for o in options]
    total, width = sum(a.shape[0] for a in options[0]), options[0][0].shape[1]
    start, size = rows or (0, total)

    def kernel(index_ref, *refs):
        *bufs, out_ref, held, sem = refs
        for k, option in enumerate(options):
            parts, bufs = bufs[: len(option)], bufs[len(option) :]

            @pl.when(index_ref[0] == k)
            def _():
                at = 0
                for part in parts:
                    high = min(part.shape[0], size)
                    copy = pltpu.make_async_copy(
                        part.at[pl.ds(start if rows else 0, high)], held.at[pl.ds(at, high)], sem
                    )
                    copy.start()
                    copy.wait()
                    at += high

        @pl.when(index_ref[0] >= 0)
        def _():
            copy = pltpu.make_async_copy(held, out_ref, sem)
            copy.start()
            copy.wait()

    flat = [a for option in options for a in option]
    return pl.pallas_call(
        kernel,
        out_shape=shape(size, width),
        in_specs=[SMEM] + [ANY] * len(flat),
        out_specs=ANY,
        scratch_shapes=[pltpu.VMEM((size, width), F32), DMA(())],
        compiler_params=params(8),
    )(index, *flat)


def unset(like):
    return pl.pallas_call(
        lambda out_ref: None, out_shape=shape(*like.shape), in_specs=[], out_specs=ANY
    )()


def patch(flags, result, parts):
    def kernel(flags_ref, result_ref, *refs):
        *bufs, out_ref, held, sem = refs
        for k, buf in enumerate(bufs):

            @pl.when(flags_ref[k] == 1)
            def _():
                for source, target in ((buf, held), (held, out_ref.at[k])):
                    copy = pltpu.make_async_copy(source, target, sem)
                    copy.start()
                    copy.wait()

    return pl.pallas_call(
        kernel,
        out_shape=shape(*result.shape),
        in_specs=[SMEM] + [ANY] * (1 + len(parts)),
        out_specs=ANY,
        scratch_shapes=[pltpu.VMEM(parts[0].shape, F32), DMA(())],
        input_output_aliases={1: 0},
        compiler_params=params(8),
    )(flags, result, *parts)


def split(x):
    high = x.astype(jnp.bfloat16)
    return high, (x - high.astype(F32)).astype(jnp.bfloat16)


def dot3(a, b, dims):
    total = None
    for x, y in ((a[1], b[0]), (a[0], b[1]), (a[0], b[0])):
        part = lax.dot_general(x, y, (dims, ((), ())), preferred_element_type=F32)
        total = part if total is None else total + part
    return total


PASS, WORK, ZERO, LOWER0, PANEL0, LOWER1 = range(6)


def finish_kernel(n_raw, n_sets, meta_ref, *refs):
    tiles_ref, raws, refs = refs[0], refs[1 : 1 + n_raw], refs[1 + n_raw :]
    order = tiles_ref.shape[-1]
    steps = order // BLOCK
    count = 2 * steps
    sets = [refs[k * count : (k + 1) * count] for k in range(n_sets)]
    out_ref, p1_ref, z, t, spare, high, low, *fs, sems = refs[n_sets * count :]
    role, transposed, col, edge = (meta_ref[k] for k in (0, 5, 7, 8))
    which = meta_ref[6], meta_ref[14]
    half = pl.ds(0, order), pl.ds(order, order)
    sources = [[tiles_ref.at[0]]]
    for ref in raws:
        if ref.shape[0] < order and len(sources[-1]) == 1 and sources[-1][0].shape[0] < order:
            sources[-1].append(ref)
        else:
            sources.append([ref])

    def load_pieces(pieces):
        for k in range(n_sets):
            for step in range(2):

                @pl.when(which[step] == k)
                def _():
                    for p in pieces:
                        if p // steps == step:
                            pltpu.make_async_copy(sets[k][p], fs[p], sems.at[8 + p]).start()

    def await_piece(p):
        pltpu.make_async_copy(sets[0][p], fs[p], sems.at[8 + p]).wait()

    def move_out(source, target, sem):
        copy = pltpu.make_async_copy(source, target, sems.at[sem])
        copy.start()
        return copy

    @pl.when(role == PASS)
    def _():
        held = (t, spare)
        copies = [move_out(tiles_ref.at[k], held[k], k) for k in range(2)]
        for k in range(2):
            copies[k].wait()
            copies[k] = move_out(held[k], out_ref.at[k], k)
        for copy in copies:
            copy.wait()

    @pl.when(role >= ZERO)
    def _():
        t[...] = jnp.zeros((order, order), F32)
        move_out(t, out_ref.at[1], 1).wait()

        def upper_block(p, q, lead):
            base = lead + (q - p) * BLOCK
            return fs[p][:, base : base + BLOCK].T

        def triangle(offset):
            sub = lax.broadcasted_iota(jnp.int32, (BLOCK, BLOCK), 0)
            lane = lax.broadcasted_iota(jnp.int32, (BLOCK, BLOCK), 1)
            for p in range(steps):
                for q in range(p, steps):
                    block = fs[offset + p][:, (q - p) * BLOCK : (q - p + 1) * BLOCK]
                    if p == q:
                        block = jnp.where(sub <= lane, block, 0.0)
                    t[q * BLOCK : (q + 1) * BLOCK, p * BLOCK : (p + 1) * BLOCK] = block.T

        for kind, pieces in (
            (LOWER0, range(steps)),
            (PANEL0, range(steps)),
            (LOWER1, range(steps, count)),
        ):

            @pl.when(role == kind)
            def _():
                load_pieces(pieces)
                for p in pieces:
                    await_piece(p)
                if kind == PANEL0:
                    for p in range(steps):
                        for q in range(steps):
                            t[q * BLOCK : (q + 1) * BLOCK, p * BLOCK : (p + 1) * BLOCK] = (
                                upper_block(p, q, order - p * BLOCK + p * BLOCK)
                            )
                else:
                    triangle(pieces[0])

        move_out(t, out_ref.at[0], 0).wait()

    @pl.when(role == WORK)
    def _():
        places = [z.at[half[a], half[b]] for a in range(2) for b in range(2)]
        for s, place in enumerate(places):
            for k, source in enumerate(sources):

                @pl.when(meta_ref[1 + s] == k)
                def _():
                    high = order // len(source)
                    for h, part in enumerate(source):
                        rows = pl.ds((s // 2) * order + h * high, high)
                        target = z.at[rows, half[s % 2]]
                        pltpu.make_async_copy(part, target, sems.at[s]).start()

        load_pieces(range(count))
        for slot, taken in ((1, col < 2), (0, col >= 2)):

            @pl.when(taken)
            def _():
                pltpu.make_async_copy(tiles_ref.at[slot], t, sems.at[4]).start()

        @pl.when(col >= 2)
        def _():
            move_out(tiles_ref.at[1], spare, 5)

        for s, place in enumerate(places):
            pltpu.make_async_copy(sources[1][0], place, sems.at[s]).wait()

        @pl.when(transposed == 1)
        def _():
            for left in (0, order):
                for a in range(steps):
                    for b in range(a, steps):
                        ra = order + a * BLOCK, left + a * BLOCK
                        rb = order + b * BLOCK, left + b * BLOCK
                        upper = z[ra[0] : ra[0] + BLOCK, rb[1] : rb[1] + BLOCK].T
                        if a != b:
                            z[ra[0] : ra[0] + BLOCK, rb[1] : rb[1] + BLOCK] = z[
                                rb[0] : rb[0] + BLOCK, ra[1] : ra[1] + BLOCK
                            ].T
                        z[rb[0] : rb[0] + BLOCK, ra[1] : ra[1] + BLOCK] = upper

        sub = lax.broadcasted_iota(jnp.int32, (BLOCK, BLOCK), 0)
        lane = lax.broadcasted_iota(jnp.int32, (BLOCK, BLOCK), 1)
        for p in range(count):
            await_piece(p)
            packed = fs[p][:, :BLOCK]
            inverse = jnp.where(
                sub > lane, packed, jnp.where(sub == lane, 1.0 / packed, 0.0)
            )
            inverse = split(inverse)
            for rows in half:
                solved = dot3(
                    split(z[rows, p * BLOCK : (p + 1) * BLOCK]), inverse, NT
                )
                z[rows, p * BLOCK : (p + 1) * BLOCK] = solved
                solved = split(solved)
                high[rows, :] = solved[0]
                low[rows, :] = solved[1]

            def eliminate(q, carry):
                to = pl.ds(pl.multiple_of(q * BLOCK, BLOCK), BLOCK)
                u = split(fs[p][:, pl.ds(pl.multiple_of((q - p) * BLOCK, BLOCK), BLOCK)])
                for rows in half:
                    z[rows, to] -= dot3((high[rows, :], low[rows, :]), u, NN)
                return carry

            lax.fori_loop(p + 1, count, eliminate, 0)
            if p == 0:
                pltpu.make_async_copy(tiles_ref.at[0], t, sems.at[4]).wait()

            def update(r, carry):
                rows = pl.ds(pl.multiple_of(r * BLOCK, BLOCK), BLOCK)
                others = high[half[1], :], low[half[1], :]
                t[rows, :] -= dot3((high[rows, :], low[rows, :]), others, NT)
                return carry

            lax.fori_loop(0, steps, update, 0)

        @pl.when(col >= 2)
        def _():
            pltpu.make_async_copy(tiles_ref.at[1], spare, sems.at[5]).wait()
            move_out(spare, out_ref.at[1], 5)

        @pl.when(col == 0)
        def _():
            move_out(z.at[half[0], half[0]], out_ref.at[0], 5)

        @pl.when(col == 1)
        def _():
            move_out(z.at[half[0], half[1]], out_ref.at[0], 5)

        for slot, taken in ((1, col < 2), (0, col >= 2)):

            @pl.when(taken)
            def _():
                move_out(t, out_ref.at[slot], 6)

        @pl.when((col == 2) & (edge == 1))
        def _():
            move_out(z.at[half[0], half[1]], p1_ref, 7).wait()

        pltpu.make_async_copy(t, out_ref.at[0], sems.at[5]).wait()
        pltpu.make_async_copy(t, out_ref.at[0], sems.at[6]).wait()


def finish(meta, tiles, raws, sets):
    order = tiles.shape[-1]
    count = len(sets[0])
    flat = [f for s in sets for f in s]
    scratch = [
        pltpu.VMEM((2 * order, 2 * order), F32),
        pltpu.VMEM((order, order), F32),
        pltpu.VMEM((order, order), F32),
        pltpu.VMEM((2 * order, BLOCK), jnp.bfloat16),
        pltpu.VMEM((2 * order, BLOCK), jnp.bfloat16),
    ]
    scratch += [pltpu.VMEM(f.shape, F32) for f in sets[0]] + [DMA((8 + count,))]
    return pl.pallas_call(
        lambda *refs: finish_kernel(len(raws), len(sets), *refs),
        out_shape=[shape(*tiles.shape), shape(order, order)],
        in_specs=[SMEM] + [ANY] * (1 + len(raws) + len(flat)),
        out_specs=[ANY, ANY],
        scratch_shapes=scratch,
        cost_estimate=pl.CostEstimate(
            flops=60_000_000_000, bytes_accessed=64 << 20, transcendentals=0
        ),
        compiler_params=params(56),
    )(meta, tiles, *raws, *flat)


def move(value, pairs, cols):
    flat = [(a * cols + b, c * cols + d) for (a, b), (c, d) in pairs]
    return lax.ppermute(value, ("row", "col"), flat)


def doubling(value, axis, root, size):
    place = lax.rem(lax.axis_index(axis) - root + size, size)
    reach = 1
    while reach < size:
        pairs = [
            ((root + i) % size, (root + i + reach) % size) for i in range(min(reach, size - reach))
        ]
        value = jnp.where(place >= reach, lax.ppermute(value, axis, pairs), value)
        reach *= 2
    return value


def both_ways(pairs):
    return pairs + [(b, a) for a, b in pairs]


def eliminate_last(panel, pieces):
    done = []
    for f in pieces:
        packed = f[:, :BLOCK]
        inverse = jnp.tril(packed, -1) + jnp.diag(1.0 / jnp.diagonal(packed))
        part = dot(panel[:, :BLOCK], inverse, NT, lax.Precision.HIGH)
        done.append(part)
        if f.shape[1] > BLOCK:
            panel = panel[:, BLOCK:] - dot(part, f[:, BLOCK:], NN, lax.Precision.HIGH)
    return jnp.concatenate(done, 1)


def on_device(kernel_tiles, profile):
    order = kernel_tiles.shape[-1]
    rows, cols = lax.axis_size("row"), lax.axis_size("col")
    row, col = lax.axis_index("row"), lax.axis_index("col")
    tiles = kernel_tiles.reshape(2, order, order)
    near = tiles[0]
    steps = order // BLOCK
    count = 2 * steps
    edge = cols + 2
    edge_live = profile[0, edge] <= 1
    owner = jnp.reshape(((row == 0) & (col == 0)).astype(jnp.int32), (1,))
    workers = range(2, edge)
    routed = cols == 4

    plan = [[[PASS] + [0] * 8 + [-1] * 5 + [0, -1, -1] for _ in range(cols)] for _ in range(rows)]
    for r in range(rows):
        for c in range(cols):
            plan[r][c][7] = c
            if r < 2:
                plan[r][c][0] = ZERO
            elif r < edge:
                plan[r][c][0] = WORK
    plan[0][0][0], plan[1][0][0], plan[1][1][0] = LOWER0, PANEL0, LOWER1

    if routed:
        r1 = move(near, both_ways([((r, 0), (r, 1)) for r in (0,) + tuple(workers)]), cols)
        r2 = move(
            near,
            [((r, c), (r, c + 2)) for r in workers for c in (0, 1)],
            cols,
        )
        r3 = move(
            near,
            both_ways([((4, c), (5, c)) for c in (0, 1)])
            + [((r, c), (r + 4, c)) for r in (0, 1) for c in (2, 3)],
            cols,
        )
        r4 = move(near, [((r, c), (r - 2, c)) for r in (4, 5) for c in (0, 1)], cols)
        tile01, tile11 = r1, move(near, [((1, 1), (0, 0))], cols)
        for r in workers:
            plan[r][0][1:3] = [0, 1]
            plan[r][1][1:3] = [1, 0]
            plan[r][2][1:3] = [2, 5]
            plan[r][3][1:3] = [5, 2]
            for c in range(4):
                plan[r][c][3:5] = plan[r][c][1:3]
        for place, pair in {
            (2, 0): (4, 7), (2, 1): (7, 6), (3, 0): (6, 7), (3, 1): (7, 4),
            (4, 1): (7, 3), (5, 0): (3, 7), (2, 3): (7, 6), (3, 2): (6, 7),
            (4, 2): (3, 6), (4, 3): (3, 6), (5, 2): (6, 3), (5, 3): (6, 3),
        }.items():
            plan[place[0]][place[1]][3:5] = pair
        for c in (0, 1):
            plan[2][c][12] = plan[3][c][12] = 2
        for c in (2, 3):
            plan[2][c][12] = plan[3][c][12] = 0
            plan[4][c][12] = plan[5][c][12] = 1
        plan[4][0][13] = plan[5][1][13] = 0
        plan[2][1][13] = plan[3][0][13] = 1
        plan[2][0][13] = plan[3][1][13] = plan[2][2][13] = plan[3][3][13] = 2
        for r in (4, 5):
            for c in (2, 3):
                plan[r][c][5] = 1
        plan[1][1][6] = 1
        for r in workers:
            plan[r][1][6] = plan[r][3][6] = 3 if r < 4 else 4
        for r in (1,) + tuple(workers):
            plan[r][0][6] = plan[r][2][6] = 5
        plan[1][1][14] = 4
        plan[0][0][15], plan[1][0][15], plan[1][0][16] = 0, 1, 0
        for r in workers:
            plan[r][0][14:17] = [1, -1, 1] if r < 4 else [2, -1, 2]
            plan[r][1][14], plan[r][2][14], plan[r][3][14] = 4, 3, 5
        plan[0][1][9], plan[1][1][9] = 0, 1
        plan[0][1][10:12], plan[1][1][10:12] = [0, -1], [1, 0]
        plan[0][3][10], plan[1][3][10] = 2, 2
        for r in workers:
            plan[r][1][11] = plan[r][3][11] = 1 if r < 4 else 2
    else:
        mine = jnp.where(col < 2, tiles[1], near)
        left0 = doubling(near, "col", 0, cols)
        left1 = doubling(near, "col", 1, cols)
        top0 = doubling(mine, "row", 0, rows)
        top1 = doubling(mine, "row", 1, rows)
        tile01 = move(near, [((0, 1), (0, 0))], cols)
        tile11 = move(near, [((1, 1), (0, 0))], cols)
        raws = [left0, left1, top0, top1]
        for r in range(rows):
            for c in range(cols):
                plan[r][c][1:6] = [1, 2, 3, 4, 1]
    meta = jnp.array(plan, jnp.int32)[row, col]
    meta = meta.at[8].set(edge_live.astype(jnp.int32))

    pieces, copies, state = [], [], None
    drain = max(STAGES[0], steps + STAGES[1]) - steps if routed else 0
    for slot in range(count + drain):
        if slot < count:
            step, local = divmod(slot, steps)
            n = order - local * BLOCK
            if slot == 0:
                args = ("first", owner, n, 2 * n, tiles, tile01)
            elif local == 0:
                args = ("schur", owner, n, n, tile11, *pieces)
            else:
                args = ("next", owner, n, n + (1 - step) * order, state)
            piece, state = factor_block(*args)
            pieces.append(piece)
            copies.append([])
            if not routed:
                copies[-1].append(doubling(doubling(piece, "row", 0, rows), "col", 0, cols))
        if not routed:
            continue
        arrived = {}
        for p in range(max(0, slot - max(STAGES)), min(slot, count)):
            got, k = copies[p], slot - p
            if k > STAGES[p // steps]:
                continue
            if p < steps:
                if k == 1:
                    new = [move(pieces[p], [((0, 0), (0, 1))], cols)]
                elif k == 2:
                    new = [move(got[0], [((0, 1), (1, 1))], cols)]
                elif k == 3:
                    via = choose(meta[9:10], got)
                    new = [move(via, [((r, 1), (r, 3)) for r in (0, 1)], cols)]
                elif k == 4:
                    via = choose(meta[10:11], got)
                    pairs = [((r, c), (r + 2, c)) for r in (0, 1) for c in (1, 3)]
                    new = [move(via, pairs, cols)]
                elif k == 5:
                    pairs = [((r, c), (r + 2, c)) for r in (2, 3) for c in (1, 3)]
                    new = [move(got[3], pairs, cols)]
                else:
                    via = choose(meta[11:12], [got[1], got[3], got[4]])
                    pairs = [((r, c), (r, c - 1)) for r in workers for c in (1, 3)]
                    new = [move(via, pairs + [((1, 1), (1, 0))], cols)]
            elif k == 1:
                new = [move(pieces[p], [((0, 0), (1, 0))], cols)]
            elif k == 2:
                via = choose(meta[15:16], [pieces[p], got[0]])
                new = [
                    move(via, [((r, 0), (r + far, 0)) for r in (0, 1)], cols) for far in (2, 4)
                ]
            else:
                via = choose(meta[16:17], got)
                new = [
                    move(via, [((r, 0), (r, c)) for r in workers] + also, cols)
                    for c, also in ((2, []), (1, [((1, 0), (1, 1))]), (3, []))
                ]
            arrived[p] = new
        late = []
        if slot == FIRST:
            late = [r2, r3, r4, tile11]
        elif slot == SECOND[0]:
            late = [r5, r6[0]]
        elif slot == SECOND[1]:
            late = [r6[1]]
        elif slot == THIRD:
            late = [r7]
        flowing = ([pieces[slot]] if slot < count else []) + ([] if state is None else [state])
        flowing, arrived, late = lax.optimization_barrier((flowing, arrived, late))
        if slot < count:
            pieces[slot] = flowing[0]
        if state is not None:
            state = flowing[-1]
        for p, new in arrived.items():
            copies[p] += new
        if slot == FIRST:
            r2, r3, r4, tile11 = late
            r5 = move(r2, both_ways([((r, 2), (r, 3)) for r in workers]), cols)
            across = both_ways(
                [((2, c), (3, c)) for c in range(4)] + [((4, c), (5, c)) for c in (2, 3)]
            )
            high = order // 2
            r6 = [move(choose(meta[12:13], [r2, r3, r4], (0, high)), across, cols), None]
        elif slot == SECOND[0]:
            r5, r6[0] = late
            r6[1] = move(choose(meta[12:13], [r2, r3, r4], (high, high)), across, cols)
        elif slot == SECOND[1]:
            (r6[1],) = late
            r7 = move(
                choose(meta[13:14], [r3, r4, r6]),
                [((4, 0), (4, 1)), ((5, 1), (5, 0)), ((2, 1), (2, 0)), ((3, 0), (3, 1))]
                + [((2, 0), (2, 1)), ((3, 1), (3, 0)), ((2, 2), (2, 3)), ((3, 3), (3, 2))],
                cols,
            )
        elif slot == THIRD:
            (r7,) = late

    if routed:
        sets = [pieces] + [[got[k] for got in copies] for k in (1, 2, 3, 4, 5)]
        last_pieces = sets[3][steps:]
        raws = [r1, r2, r3, r4, r5, *r6, r7]
    else:
        sets = [[got[0] for got in copies]]
        last_pieces = sets[0][steps:]

    def fetch():
        if routed:
            e0 = move(near, [((edge, 1), (edge - 2, 2))], cols)
            e1 = move(e0, [((edge - 2, 2), (edge - 4, 2))], cols)
            e2 = move(e0 + e1, [((r, 2), (r + 1, 2)) for r in (2, 4)], cols)
            return e0 + e1 + e2
        total = jnp.zeros_like(near)
        for r in workers:
            total = total + move(near, [((edge, 1), (r, 2))], cols)
        return total

    result, panel1 = finish(meta, tiles, raws, sets)
    at_edge = edge_live & (row == edge)
    flags = jnp.stack(
        [
            at_edge & (col >= 1),
            (at_edge & (col <= 2)) | (edge_live & (row >= 2) & (row < edge) & (col == 2)),
        ]
    ).astype(jnp.int32)

    def edge_parts(args):
        panel1, last_pieces = args
        far = tiles[1]
        last = eliminate_last(fetch(), last_pieces)
        column = far - dot(panel1, last, NT, lax.Precision.HIGH)
        sent = move(column, [((r, 2), (edge, r % cols)) for r in workers], cols).T
        solved = move(last, [((edge - 2, 2), (edge, 1)), ((edge - 1, 2), (edge, 2))], cols)
        corner = far - dot(solved, solved, NT, lax.Precision.HIGH)
        part0 = jnp.where(col == 1, solved, sent)
        part1 = jnp.where(row == edge, jnp.where(col == 2, corner, sent), column)
        return part0, part1

    def no_edge(args):
        return unset(near), unset(near)

    parts = lax.cond(edge_live, edge_parts, no_edge, (panel1, last_pieces))
    return patch(flags, result, parts).reshape(kernel_tiles.shape)


def solution(mesh):
    placed = (P(None, "row", None, "col", None, None), P())
    return jax.shard_map(
        on_device,
        mesh=mesh,
        in_specs=placed,
        out_specs=P(None, "row", None, "col", None, None),
        check_vma=False,
    )
```

```python
import jax
import jax.numpy as jnp
from jax import lax
from jax.experimental import pallas as pl
from jax.experimental.pallas import tpu as pltpu
from jax.sharding import PartitionSpec as P

SUB = 8
BASE = 128
BLOCK = 256
STAGES = (6, 3)
FIRST = 3
SECOND = (5, 7)
THIRD = 8
NN = ((1,), (0,))
NT = ((1,), (1,))
TN = ((0,), (0,))
ANY = pl.BlockSpec(memory_space=pl.ANY)
SMEM = pl.BlockSpec(memory_space=pltpu.SMEM)
DMA = pltpu.SemaphoreType.DMA
F32 = jnp.float32


def dot(a, b, dims, precision=lax.Precision.HIGHEST):
    return lax.dot_general(
        a, b, (dims, ((), ())), precision=precision, preferred_element_type=jnp.float32
    )


def down(x, j):
    return jnp.broadcast_to(x[j : j + 1, :], x.shape)


def along(x, j):
    return jnp.broadcast_to(x[:, j : j + 1], x.shape)


def factor_base(diag):
    sub = lax.broadcasted_iota(jnp.int32, (SUB, BASE), 0)
    lane = lax.broadcasted_iota(jnp.int32, (SUB, BASE), 1)
    count = BASE // SUB
    left = [diag[SUB * t : SUB * t + SUB, :] for t in range(count)]
    right = [(lane == sub + SUB * t).astype(jnp.float32) for t in range(count)]
    upper, inverse = [], []
    for t in range(count):
        a, b = left[t], right[t]
        cols = [along(a, SUB * t + j) for j in range(SUB)]
        ua, ub, pivots = a, b, None
        for j in range(SUB):
            mine = sub == j
            pivot = down(cols[j], j)
            recip = 1.0 / pivot
            if j:
                ua = jnp.where(sub >= j, a, ua)
                ub = jnp.where(sub >= j, b, ub)
                pivots = jnp.where(sub >= j, pivot, pivots)
            else:
                pivots = pivot
            mult = cols[j]
            row = down(a, j) * recip
            a = jnp.where(mine, row, a - mult * row)
            row = down(b, j) * recip
            b = jnp.where(mine, row, b - mult * row)
            for k in range(j + 1, SUB):
                row = down(cols[k], j) * recip
                cols[k] = jnp.where(mine, row, cols[k] - mult * row)
        scale = lax.rsqrt(pivots)
        upper.append(jnp.where(lane >= sub + SUB * t, ua * scale, 0.0))
        inverse.append(ub * scale)
        if t + 1 < count:
            va = [down(a, j) for j in range(SUB)]
            vb = [down(b, j) for j in range(SUB)]
            for i in range(t + 1, count):
                mult = [along(left[i], SUB * t + j) for j in range(SUB)]
                for j in range(SUB):
                    left[i] = left[i] - mult[j] * va[j]
                    right[i] = right[i] - mult[j] * vb[j]
    return jnp.concatenate(upper, 0), jnp.concatenate(inverse, 0)


def params(limit_mib=48):
    return pltpu.CompilerParams(vmem_limit_bytes=limit_mib << 20)


def shape(*dims):
    return jax.ShapeDtypeStruct(dims, F32)


def factor_kernel(kind, flag_ref, *refs):
    refs = list(refs)
    sources = [refs.pop(0) for _ in range({"first": 2, "next": 1, "schur": 5}[kind])]
    a_ref, f_ref, sems = refs[-3:]
    f_out = refs[0]
    rest_out = refs[1] if len(refs) > 4 else None
    n, m = a_ref.shape
    top, below = pl.ds(0, BLOCK), pl.ds(BLOCK, n - BLOCK)

    @pl.when(flag_ref[0] == 1)
    def _():
        copies = []

        def load(source, target):
            copies.append(pltpu.make_async_copy(source, target, sems.at[len(copies)]))
            copies[-1].start()

        if kind == "first":
            for rows in (top, below):
                load(sources[0].at[0, rows], a_ref.at[rows, pl.ds(0, n)])
                load(sources[1].at[rows], a_ref.at[rows, pl.ds(n, n)])
            needed = 2
        elif kind == "next":
            load(sources[0].at[top], a_ref.at[top])
            if n > BLOCK:
                load(sources[0].at[below], a_ref.at[below])
            needed = 1
        else:
            parts = refs[-4]
            load(sources[0], a_ref)
            for p, part in enumerate(sources[1:]):
                load(
                    part.at[:, pl.ds(part.shape[1] - n, n)],
                    parts.at[pl.ds(p * BLOCK, BLOCK)],
                )
            needed = len(copies)
        for copy in copies[:needed]:
            copy.wait()
        if kind == "schur":
            for r in range(0, n, BLOCK):
                lhs = parts[:, r : r + BLOCK].T
                for c in range(r, n, BLOCK):
                    a_ref[r : r + BLOCK, c : c + BLOCK] -= dot(lhs, parts[:, c : c + BLOCK], NN)

        first, second = pl.ds(0, BASE), pl.ds(BASE, BASE)
        sub = lax.broadcasted_iota(jnp.int32, (BASE, BASE), 0)
        lane = lax.broadcasted_iota(jnp.int32, (BASE, BASE), 1)
        x_ref = refs[-4] if kind != "schur" else refs[-5]

        def base(b, carry):
            rows = pl.ds(pl.multiple_of(b * BASE, BASE), BASE)
            u, x = factor_base(a_ref[rows, rows])
            f_ref[rows, rows] = jnp.where(sub <= lane, u, x)
            x_ref[rows, rows] = x

            @pl.when(b == 0)
            def _():
                u12 = dot(x, a_ref[first, second], NN)
                f_ref[first, second] = u12
                a_ref[second, second] -= dot(u12, u12, TN)

            return carry

        lax.fori_loop(0, BLOCK // BASE, base, 0)
        x21 = -dot(x_ref[second, second], dot(f_ref[first, second], x_ref[first, first], TN), NN)
        f_ref[second, first] = x21
        x_ref[second, first] = x21
        x_ref[first, second] = jnp.zeros((BASE, BASE), F32)
        x = x_ref[...]
        for c in range(BLOCK, m, BLOCK):
            f_ref[:, c : c + BLOCK] = dot(x, a_ref[top, c : c + BLOCK], NN)
        leaving = [pltpu.make_async_copy(f_ref, f_out, sems.at[len(copies)])]
        leaving[0].start()
        for copy in copies[needed:]:
            copy.wait()
        for r in range(BLOCK, n, BLOCK):
            lhs = f_ref[:, r : r + BLOCK].T
            for c in range(r, m, BLOCK):
                a_ref[r : r + BLOCK, c : c + BLOCK] -= dot(lhs, f_ref[:, c : c + BLOCK], NN)
            rows = pl.ds(r, BLOCK)
            leaving.append(
                pltpu.make_async_copy(
                    a_ref.at[rows, pl.ds(BLOCK, m - BLOCK)],
                    rest_out.at[pl.ds(r - BLOCK, BLOCK)],
                    sems.at[len(copies) + len(leaving)],
                )
            )
            leaving[-1].start()
        for copy in leaving:
            copy.wait()


def factor_block(kind, flag, n, m, *sources):
    shapes = [shape(BLOCK, m)]
    if n > BLOCK:
        shapes.append(shape(n - BLOCK, m - BLOCK))
    scratch = [pltpu.VMEM((BLOCK, BLOCK), F32)]
    if kind == "schur":
        scratch.append(pltpu.VMEM((n, n), F32))
    scratch += [pltpu.VMEM((n, m), F32), pltpu.VMEM((BLOCK, m), F32), DMA((12,))]
    out = pl.pallas_call(
        lambda *refs: factor_kernel(kind, *refs),
        out_shape=shapes,
        in_specs=[SMEM] + [ANY] * len(sources),
        out_specs=[ANY] * len(shapes),
        scratch_shapes=scratch,
        cost_estimate=pl.CostEstimate(
            flops=2_000_000_000, bytes_accessed=8 * n * m, transcendentals=0
        ),
        compiler_params=params(),
    )(flag, *sources)
    return out if n > BLOCK else (out[0], None)


def choose(index, options, rows=None):
    options = [o if isinstance(o, list) else [o] for o in options]
    total, width = sum(a.shape[0] for a in options[0]), options[0][0].shape[1]
    start, size = rows or (0, total)

    def kernel(index_ref, *refs):
        *bufs, out_ref, held, sem = refs
        for k, option in enumerate(options):
            parts, bufs = bufs[: len(option)], bufs[len(option) :]

            @pl.when(index_ref[0] == k)
            def _():
                at = 0
                for part in parts:
                    high = min(part.shape[0], size)
                    copy = pltpu.make_async_copy(
                        part.at[pl.ds(start if rows else 0, high)], held.at[pl.ds(at, high)], sem
                    )
                    copy.start()
                    copy.wait()
                    at += high

        @pl.when(index_ref[0] >= 0)
        def _():
            copy = pltpu.make_async_copy(held, out_ref, sem)
            copy.start()
            copy.wait()

    flat = [a for option in options for a in option]
    return pl.pallas_call(
        kernel,
        out_shape=shape(size, width),
        in_specs=[SMEM] + [ANY] * len(flat),
        out_specs=ANY,
        scratch_shapes=[pltpu.VMEM((size, width), F32), DMA(())],
        compiler_params=params(8),
    )(index, *flat)


def unset(like):
    return pl.pallas_call(
        lambda out_ref: None, out_shape=shape(*like.shape), in_specs=[], out_specs=ANY
    )()


def patch(flags, result, parts):
    def kernel(flags_ref, result_ref, *refs):
        *bufs, out_ref, held, sem = refs
        for k, buf in enumerate(bufs):

            @pl.when(flags_ref[k] == 1)
            def _():
                for source, target in ((buf, held), (held, out_ref.at[k])):
                    copy = pltpu.make_async_copy(source, target, sem)
                    copy.start()
                    copy.wait()

    return pl.pallas_call(
        kernel,
        out_shape=shape(*result.shape),
        in_specs=[SMEM] + [ANY] * (1 + len(parts)),
        out_specs=ANY,
        scratch_shapes=[pltpu.VMEM(parts[0].shape, F32), DMA(())],
        input_output_aliases={1: 0},
        compiler_params=params(8),
    )(flags, result, *parts)


def split(x):
    high = x.astype(jnp.bfloat16)
    return high, (x - high.astype(F32)).astype(jnp.bfloat16)


def dot3(a, b, dims):
    total = None
    for x, y in ((a[1], b[0]), (a[0], b[1]), (a[0], b[0])):
        part = lax.dot_general(x, y, (dims, ((), ())), preferred_element_type=F32)
        total = part if total is None else total + part
    return total


PASS, WORK, ZERO, LOWER0, PANEL0, LOWER1 = range(6)


def finish_kernel(n_raw, n_sets, meta_ref, *refs):
    tiles_ref, raws, refs = refs[0], refs[1 : 1 + n_raw], refs[1 + n_raw :]
    order = tiles_ref.shape[-1]
    steps = order // BLOCK
    count = 2 * steps
    sets = [refs[k * count : (k + 1) * count] for k in range(n_sets)]
    out_ref, p1_ref, z, t, spare, high, low, *fs, sems = refs[n_sets * count :]
    role, transposed, col, edge = (meta_ref[k] for k in (0, 5, 7, 8))
    which = meta_ref[6], meta_ref[14]
    half = pl.ds(0, order), pl.ds(order, order)
    sources = [[tiles_ref.at[0]]]
    for ref in raws:
        if ref.shape[0] < order and len(sources[-1]) == 1 and sources[-1][0].shape[0] < order:
            sources[-1].append(ref)
        else:
            sources.append([ref])

    def load_pieces(pieces):
        for k in range(n_sets):
            for step in range(2):

                @pl.when(which[step] == k)
                def _():
                    for p in pieces:
                        if p // steps == step:
                            pltpu.make_async_copy(sets[k][p], fs[p], sems.at[8 + p]).start()

    def await_piece(p):
        pltpu.make_async_copy(sets[0][p], fs[p], sems.at[8 + p]).wait()

    def move_out(source, target, sem):
        copy = pltpu.make_async_copy(source, target, sems.at[sem])
        copy.start()
        return copy

    @pl.when(role == PASS)
    def _():
        held = (t, spare)
        copies = [move_out(tiles_ref.at[k], held[k], k) for k in range(2)]
        for k in range(2):
            copies[k].wait()
            copies[k] = move_out(held[k], out_ref.at[k], k)
        for copy in copies:
            copy.wait()

    @pl.when(role >= ZERO)
    def _():
        t[...] = jnp.zeros((order, order), F32)
        move_out(t, out_ref.at[1], 1).wait()

        def upper_block(p, q, lead):
            base = lead + (q - p) * BLOCK
            return fs[p][:, base : base + BLOCK].T

        def triangle(offset):
            sub = lax.broadcasted_iota(jnp.int32, (BLOCK, BLOCK), 0)
            lane = lax.broadcasted_iota(jnp.int32, (BLOCK, BLOCK), 1)
            for p in range(steps):
                for q in range(p, steps):
                    block = fs[offset + p][:, (q - p) * BLOCK : (q - p + 1) * BLOCK]
                    if p == q:
                        block = jnp.where(sub <= lane, block, 0.0)
                    t[q * BLOCK : (q + 1) * BLOCK, p * BLOCK : (p + 1) * BLOCK] = block.T

        for kind, pieces in (
            (LOWER0, range(steps)),
            (PANEL0, range(steps)),
            (LOWER1, range(steps, count)),
        ):

            @pl.when(role == kind)
            def _():
                load_pieces(pieces)
                for p in pieces:
                    await_piece(p)
                if kind == PANEL0:
                    for p in range(steps):
                        for q in range(steps):
                            t[q * BLOCK : (q + 1) * BLOCK, p * BLOCK : (p + 1) * BLOCK] = (
                                upper_block(p, q, order - p * BLOCK + p * BLOCK)
                            )
                else:
                    triangle(pieces[0])

        move_out(t, out_ref.at[0], 0).wait()

    @pl.when(role == WORK)
    def _():
        places = [z.at[half[a], half[b]] for a in range(2) for b in range(2)]
        for s, place in enumerate(places):
            for k, source in enumerate(sources):

                @pl.when(meta_ref[1 + s] == k)
                def _():
                    high = order // len(source)
                    for h, part in enumerate(source):
                        rows = pl.ds((s // 2) * order + h * high, high)
                        target = z.at[rows, half[s % 2]]
                        pltpu.make_async_copy(part, target, sems.at[s]).start()

        load_pieces(range(count))
        for slot, taken in ((1, col < 2), (0, col >= 2)):

            @pl.when(taken)
            def _():
                pltpu.make_async_copy(tiles_ref.at[slot], t, sems.at[4]).start()

        @pl.when(col >= 2)
        def _():
            move_out(tiles_ref.at[1], spare, 5)

        for s, place in enumerate(places):
            pltpu.make_async_copy(sources[1][0], place, sems.at[s]).wait()

        @pl.when(transposed == 1)
        def _():
            for left in (0, order):
                for a in range(steps):
                    for b in range(a, steps):
                        ra = order + a * BLOCK, left + a * BLOCK
                        rb = order + b * BLOCK, left + b * BLOCK
                        upper = z[ra[0] : ra[0] + BLOCK, rb[1] : rb[1] + BLOCK].T
                        if a != b:
                            z[ra[0] : ra[0] + BLOCK, rb[1] : rb[1] + BLOCK] = z[
                                rb[0] : rb[0] + BLOCK, ra[1] : ra[1] + BLOCK
                            ].T
                        z[rb[0] : rb[0] + BLOCK, ra[1] : ra[1] + BLOCK] = upper

        sub = lax.broadcasted_iota(jnp.int32, (BLOCK, BLOCK), 0)
        lane = lax.broadcasted_iota(jnp.int32, (BLOCK, BLOCK), 1)
        for p in range(count):
            await_piece(p)
            packed = fs[p][:, :BLOCK]
            inverse = jnp.where(
                sub > lane, packed, jnp.where(sub == lane, 1.0 / packed, 0.0)
            )
            inverse = split(inverse)
            for rows in half:
                solved = dot3(
                    split(z[rows, p * BLOCK : (p + 1) * BLOCK]), inverse, NT
                )
                z[rows, p * BLOCK : (p + 1) * BLOCK] = solved
                solved = split(solved)
                high[rows, :] = solved[0]
                low[rows, :] = solved[1]

            def eliminate(q, carry):
                to = pl.ds(pl.multiple_of(q * BLOCK, BLOCK), BLOCK)
                u = split(fs[p][:, pl.ds(pl.multiple_of((q - p) * BLOCK, BLOCK), BLOCK)])
                for rows in half:
                    z[rows, to] -= dot3((high[rows, :], low[rows, :]), u, NN)
                return carry

            lax.fori_loop(p + 1, count, eliminate, 0)
            if p == 0:
                pltpu.make_async_copy(tiles_ref.at[0], t, sems.at[4]).wait()

            def update(r, carry):
                rows = pl.ds(pl.multiple_of(r * BLOCK, BLOCK), BLOCK)
                others = high[half[1], :], low[half[1], :]
                t[rows, :] -= dot3((high[rows, :], low[rows, :]), others, NT)
                return carry

            lax.fori_loop(0, steps, update, 0)

        @pl.when(col >= 2)
        def _():
            pltpu.make_async_copy(tiles_ref.at[1], spare, sems.at[5]).wait()
            move_out(spare, out_ref.at[1], 5)

        @pl.when(col == 0)
        def _():
            move_out(z.at[half[0], half[0]], out_ref.at[0], 5)

        @pl.when(col == 1)
        def _():
            move_out(z.at[half[0], half[1]], out_ref.at[0], 5)

        for slot, taken in ((1, col < 2), (0, col >= 2)):

            @pl.when(taken)
            def _():
                move_out(t, out_ref.at[slot], 6)

        @pl.when((col == 2) & (edge == 1))
        def _():
            move_out(z.at[half[0], half[1]], p1_ref, 7).wait()

        pltpu.make_async_copy(t, out_ref.at[0], sems.at[5]).wait()
        pltpu.make_async_copy(t, out_ref.at[0], sems.at[6]).wait()


def finish(meta, tiles, raws, sets):
    order = tiles.shape[-1]
    count = len(sets[0])
    flat = [f for s in sets for f in s]
    scratch = [
        pltpu.VMEM((2 * order, 2 * order), F32),
        pltpu.VMEM((order, order), F32),
        pltpu.VMEM((order, order), F32),
        pltpu.VMEM((2 * order, BLOCK), jnp.bfloat16),
        pltpu.VMEM((2 * order, BLOCK), jnp.bfloat16),
    ]
    scratch += [pltpu.VMEM(f.shape, F32) for f in sets[0]] + [DMA((8 + count,))]
    return pl.pallas_call(
        lambda *refs: finish_kernel(len(raws), len(sets), *refs),
        out_shape=[shape(*tiles.shape), shape(order, order)],
        in_specs=[SMEM] + [ANY] * (1 + len(raws) + len(flat)),
        out_specs=[ANY, ANY],
        scratch_shapes=scratch,
        cost_estimate=pl.CostEstimate(
            flops=60_000_000_000, bytes_accessed=64 << 20, transcendentals=0
        ),
        compiler_params=params(56),
    )(meta, tiles, *raws, *flat)


def move(value, pairs, cols):
    flat = [(a * cols + b, c * cols + d) for (a, b), (c, d) in pairs]
    return lax.ppermute(value, ("row", "col"), flat)


def doubling(value, axis, root, size):
    place = lax.rem(lax.axis_index(axis) - root + size, size)
    reach = 1
    while reach < size:
        pairs = [
            ((root + i) % size, (root + i + reach) % size) for i in range(min(reach, size - reach))
        ]
        value = jnp.where(place >= reach, lax.ppermute(value, axis, pairs), value)
        reach *= 2
    return value


def both_ways(pairs):
    return pairs + [(b, a) for a, b in pairs]


def eliminate_last(panel, pieces):
    done = []
    for f in pieces:
        packed = f[:, :BLOCK]
        inverse = jnp.tril(packed, -1) + jnp.diag(1.0 / jnp.diagonal(packed))
        part = dot(panel[:, :BLOCK], inverse, NT, lax.Precision.HIGH)
        done.append(part)
        if f.shape[1] > BLOCK:
            panel = panel[:, BLOCK:] - dot(part, f[:, BLOCK:], NN, lax.Precision.HIGH)
    return jnp.concatenate(done, 1)


def on_device(kernel_tiles, profile):
    order = kernel_tiles.shape[-1]
    rows, cols = lax.axis_size("row"), lax.axis_size("col")
    row, col = lax.axis_index("row"), lax.axis_index("col")
    tiles = kernel_tiles.reshape(2, order, order)
    near = tiles[0]
    steps = order // BLOCK
    count = 2 * steps
    edge = cols + 2
    edge_live = profile[0, edge] <= 1
    owner = jnp.reshape(((row == 0) & (col == 0)).astype(jnp.int32), (1,))
    workers = range(2, edge)
    routed = cols == 4

    plan = [[[PASS] + [0] * 8 + [-1] * 5 + [0, -1, -1] for _ in range(cols)] for _ in range(rows)]
    for r in range(rows):
        for c in range(cols):
            plan[r][c][7] = c
            if r < 2:
                plan[r][c][0] = ZERO
            elif r < edge:
                plan[r][c][0] = WORK
    plan[0][0][0], plan[1][0][0], plan[1][1][0] = LOWER0, PANEL0, LOWER1

    if routed:
        r1 = move(near, both_ways([((r, 0), (r, 1)) for r in (0,) + tuple(workers)]), cols)
        r2 = move(
            near,
            [((r, c), (r, c + 2)) for r in workers for c in (0, 1)],
            cols,
        )
        r3 = move(
            near,
            both_ways([((4, c), (5, c)) for c in (0, 1)])
            + [((r, c), (r + 4, c)) for r in (0, 1) for c in (2, 3)],
            cols,
        )
        r4 = move(near, [((r, c), (r - 2, c)) for r in (4, 5) for c in (0, 1)], cols)
        tile01, tile11 = r1, move(near, [((1, 1), (0, 0))], cols)
        for r in workers:
            plan[r][0][1:3] = [0, 1]
            plan[r][1][1:3] = [1, 0]
            plan[r][2][1:3] = [2, 5]
            plan[r][3][1:3] = [5, 2]
            for c in range(4):
                plan[r][c][3:5] = plan[r][c][1:3]
        for place, pair in {
            (2, 0): (4, 7), (2, 1): (7, 6), (3, 0): (6, 7), (3, 1): (7, 4),
            (4, 1): (7, 3), (5, 0): (3, 7), (2, 3): (7, 6), (3, 2): (6, 7),
            (4, 2): (3, 6), (4, 3): (3, 6), (5, 2): (6, 3), (5, 3): (6, 3),
        }.items():
            plan[place[0]][place[1]][3:5] = pair
        for c in (0, 1):
            plan[2][c][12] = plan[3][c][12] = 2
        for c in (2, 3):
            plan[2][c][12] = plan[3][c][12] = 0
            plan[4][c][12] = plan[5][c][12] = 1
        plan[4][0][13] = plan[5][1][13] = 0
        plan[2][1][13] = plan[3][0][13] = 1
        plan[2][0][13] = plan[3][1][13] = plan[2][2][13] = plan[3][3][13] = 2
        for r in (4, 5):
            for c in (2, 3):
                plan[r][c][5] = 1
        plan[1][1][6] = 1
        for r in workers:
            plan[r][1][6] = plan[r][3][6] = 3 if r < 4 else 4
        for r in (1,) + tuple(workers):
            plan[r][0][6] = plan[r][2][6] = 5
        plan[1][1][14] = 4
        plan[0][0][15], plan[1][0][15], plan[1][0][16] = 0, 1, 0
        for r in workers:
            plan[r][0][14:17] = [1, -1, 1] if r < 4 else [2, -1, 2]
            plan[r][1][14], plan[r][2][14], plan[r][3][14] = 4, 3, 5
        plan[0][1][9], plan[1][1][9] = 0, 1
        plan[0][1][10:12], plan[1][1][10:12] = [0, -1], [1, 0]
        plan[0][3][10], plan[1][3][10] = 2, 2
        for r in workers:
            plan[r][1][11] = plan[r][3][11] = 1 if r < 4 else 2
    else:
        mine = jnp.where(col < 2, tiles[1], near)
        left0 = doubling(near, "col", 0, cols)
        left1 = doubling(near, "col", 1, cols)
        top0 = doubling(mine, "row", 0, rows)
        top1 = doubling(mine, "row", 1, rows)
        tile01 = move(near, [((0, 1), (0, 0))], cols)
        tile11 = move(near, [((1, 1), (0, 0))], cols)
        raws = [left0, left1, top0, top1]
        for r in range(rows):
            for c in range(cols):
                plan[r][c][1:6] = [1, 2, 3, 4, 1]
    meta = jnp.array(plan, jnp.int32)[row, col]
    meta = meta.at[8].set(edge_live.astype(jnp.int32))

    pieces, copies, state = [], [], None
    drain = max(STAGES[0], steps + STAGES[1]) - steps if routed else 0
    for slot in range(count + drain):
        if slot < count:
            step, local = divmod(slot, steps)
            n = order - local * BLOCK
            if slot == 0:
                args = ("first", owner, n, 2 * n, tiles, tile01)
            elif local == 0:
                args = ("schur", owner, n, n, tile11, *pieces)
            else:
                args = ("next", owner, n, n + (1 - step) * order, state)
            piece, state = factor_block(*args)
            pieces.append(piece)
            copies.append([])
            if not routed:
                copies[-1].append(doubling(doubling(piece, "row", 0, rows), "col", 0, cols))
        if not routed:
            continue
        arrived = {}
        for p in range(max(0, slot - max(STAGES)), min(slot, count)):
            got, k = copies[p], slot - p
            if k > STAGES[p // steps]:
                continue
            if p < steps:
                if k == 1:
                    new = [move(pieces[p], [((0, 0), (0, 1))], cols)]
                elif k == 2:
                    new = [move(got[0], [((0, 1), (1, 1))], cols)]
                elif k == 3:
                    via = choose(meta[9:10], got)
                    new = [move(via, [((r, 1), (r, 3)) for r in (0, 1)], cols)]
                elif k == 4:
                    via = choose(meta[10:11], got)
                    pairs = [((r, c), (r + 2, c)) for r in (0, 1) for c in (1, 3)]
                    new = [move(via, pairs, cols)]
                elif k == 5:
                    pairs = [((r, c), (r + 2, c)) for r in (2, 3) for c in (1, 3)]
                    new = [move(got[3], pairs, cols)]
                else:
                    via = choose(meta[11:12], [got[1], got[3], got[4]])
                    pairs = [((r, c), (r, c - 1)) for r in workers for c in (1, 3)]
                    new = [move(via, pairs + [((1, 1), (1, 0))], cols)]
            elif k == 1:
                new = [move(pieces[p], [((0, 0), (1, 0))], cols)]
            elif k == 2:
                via = choose(meta[15:16], [pieces[p], got[0]])
                new = [
                    move(via, [((r, 0), (r + far, 0)) for r in (0, 1)], cols) for far in (2, 4)
                ]
            else:
                via = choose(meta[16:17], got)
                new = [
                    move(via, [((r, 0), (r, c)) for r in workers] + also, cols)
                    for c, also in ((2, []), (1, [((1, 0), (1, 1))]), (3, []))
                ]
            arrived[p] = new
        late = []
        if slot == FIRST:
            late = [r2, r3, r4, tile11]
        elif slot == SECOND[0]:
            late = [r5, r6[0]]
        elif slot == SECOND[1]:
            late = [r6[1]]
        elif slot == THIRD:
            late = [r7]
        flowing = ([pieces[slot]] if slot < count else []) + ([] if state is None else [state])
        flowing, arrived, late = lax.optimization_barrier((flowing, arrived, late))
        if slot < count:
            pieces[slot] = flowing[0]
        if state is not None:
            state = flowing[-1]
        for p, new in arrived.items():
            copies[p] += new
        if slot == FIRST:
            r2, r3, r4, tile11 = late
            r5 = move(r2, both_ways([((r, 2), (r, 3)) for r in workers]), cols)
            across = both_ways(
                [((2, c), (3, c)) for c in range(4)] + [((4, c), (5, c)) for c in (2, 3)]
            )
            high = order // 2
            r6 = [move(choose(meta[12:13], [r2, r3, r4], (0, high)), across, cols), None]
        elif slot == SECOND[0]:
            r5, r6[0] = late
            r6[1] = move(choose(meta[12:13], [r2, r3, r4], (high, high)), across, cols)
        elif slot == SECOND[1]:
            (r6[1],) = late
            r7 = move(
                choose(meta[13:14], [r3, r4, r6]),
                [((4, 0), (4, 1)), ((5, 1), (5, 0)), ((2, 1), (2, 0)), ((3, 0), (3, 1))]
                + [((2, 0), (2, 1)), ((3, 1), (3, 0)), ((2, 2), (2, 3)), ((3, 3), (3, 2))],
                cols,
            )
        elif slot == THIRD:
            (r7,) = late

    if routed:
        sets = [pieces] + [[got[k] for got in copies] for k in (1, 2, 3, 4, 5)]
        last_pieces = sets[3][steps:]
        raws = [r1, r2, r3, r4, r5, *r6, r7]
    else:
        sets = [[got[0] for got in copies]]
        last_pieces = sets[0][steps:]

    def fetch():
        if routed:
            e0 = move(near, [((edge, 1), (edge - 2, 2))], cols)
            e1 = move(e0, [((edge - 2, 2), (edge - 4, 2))], cols)
            e2 = move(e0 + e1, [((r, 2), (r + 1, 2)) for r in (2, 4)], cols)
            return e0 + e1 + e2
        total = jnp.zeros_like(near)
        for r in workers:
            total = total + move(near, [((edge, 1), (r, 2))], cols)
        return total

    result, panel1 = finish(meta, tiles, raws, sets)
    at_edge = edge_live & (row == edge)
    flags = jnp.stack(
        [
            at_edge & (col >= 1),
            (at_edge & (col <= 2)) | (edge_live & (row >= 2) & (row < edge) & (col == 2)),
        ]
    ).astype(jnp.int32)

    def edge_parts(args):
        panel1, last_pieces = args
        far = tiles[1]
        last = eliminate_last(fetch(), last_pieces)
        column = far - dot(panel1, last, NT, lax.Precision.HIGH)
        sent = move(column, [((r, 2), (edge, r % cols)) for r in workers], cols).T
        solved = move(last, [((edge - 2, 2), (edge, 1)), ((edge - 1, 2), (edge, 2))], cols)
        corner = far - dot(solved, solved, NT, lax.Precision.HIGH)
        part0 = jnp.where(col == 1, solved, sent)
        part1 = jnp.where(row == edge, jnp.where(col == 2, corner, sent), column)
        return part0, part1

    def no_edge(args):
        return unset(near), unset(near)

    parts = lax.cond(edge_live, edge_parts, no_edge, (panel1, last_pieces))
    return patch(flags, result, parts).reshape(kernel_tiles.shape)


def solution(mesh):
    placed = (P(None, "row", None, "col", None, None), P())
    return jax.shard_map(
        on_device,
        mesh=mesh,
        in_specs=placed,
        out_specs=P(None, "row", None, "col", None, None),
        check_vma=False,
    )
```

```python
import jax
import jax.numpy as jnp
from jax import lax
from jax.experimental import pallas as pl
from jax.experimental.pallas import tpu as pltpu
from jax.sharding import PartitionSpec as P

SUB = 8
BASE = 128
BLOCK = 256
STAGES = (6, 3)
EDGE = 1
FIRST = 2
SECOND = (4, 6)
THIRD = 8
NN = ((1,), (0,))
NT = ((1,), (1,))
TN = ((0,), (0,))
ANY = pl.BlockSpec(memory_space=pl.ANY)
SMEM = pl.BlockSpec(memory_space=pltpu.SMEM)
DMA = pltpu.SemaphoreType.DMA
F32 = jnp.float32


def dot(a, b, dims, precision=lax.Precision.HIGHEST):
    return lax.dot_general(
        a, b, (dims, ((), ())), precision=precision, preferred_element_type=jnp.float32
    )


def down(x, j):
    return jnp.broadcast_to(x[j : j + 1, :], x.shape)


def along(x, j):
    return jnp.broadcast_to(x[:, j : j + 1], x.shape)


def factor_base(diag):
    sub = lax.broadcasted_iota(jnp.int32, (SUB, BASE), 0)
    lane = lax.broadcasted_iota(jnp.int32, (SUB, BASE), 1)
    count = BASE // SUB
    left = [diag[SUB * t : SUB * t + SUB, :] for t in range(count)]
    right = [(lane == sub + SUB * t).astype(jnp.float32) for t in range(count)]
    upper, inverse = [], []
    for t in range(count):
        a, b = left[t], right[t]
        cols = [along(a, SUB * t + j) for j in range(SUB)]
        ua, ub, pivots = a, b, None
        for j in range(SUB):
            mine = sub == j
            pivot = down(cols[j], j)
            recip = 1.0 / pivot
            if j:
                ua = jnp.where(sub >= j, a, ua)
                ub = jnp.where(sub >= j, b, ub)
                pivots = jnp.where(sub >= j, pivot, pivots)
            else:
                pivots = pivot
            mult = cols[j]
            row = down(a, j) * recip
            a = jnp.where(mine, row, a - mult * row)
            row = down(b, j) * recip
            b = jnp.where(mine, row, b - mult * row)
            for k in range(j + 1, SUB):
                row = down(cols[k], j) * recip
                cols[k] = jnp.where(mine, row, cols[k] - mult * row)
        scale = lax.rsqrt(pivots)
        upper.append(jnp.where(lane >= sub + SUB * t, ua * scale, 0.0))
        inverse.append(ub * scale)
        if t + 1 < count:
            va = [down(a, j) for j in range(SUB)]
            vb = [down(b, j) for j in range(SUB)]
            for i in range(t + 1, count):
                mult = [along(left[i], SUB * t + j) for j in range(SUB)]
                for j in range(SUB):
                    left[i] = left[i] - mult[j] * va[j]
                    right[i] = right[i] - mult[j] * vb[j]
    return jnp.concatenate(upper, 0), jnp.concatenate(inverse, 0)


def params(limit_mib=48):
    return pltpu.CompilerParams(vmem_limit_bytes=limit_mib << 20)


def shape(*dims):
    return jax.ShapeDtypeStruct(dims, F32)


def factor_kernel(kind, flag_ref, *refs):
    refs = list(refs)
    sources = [refs.pop(0) for _ in range({"first": 2, "next": 1, "schur": 5}[kind])]
    a_ref, f_ref, sems = refs[-3:]
    f_out = refs[0]
    rest_out = refs[1] if len(refs) > 4 else None
    n, m = a_ref.shape
    top, below = pl.ds(0, BLOCK), pl.ds(BLOCK, n - BLOCK)

    @pl.when(flag_ref[0] == 1)
    def _():
        copies = []

        def load(source, target):
            copies.append(pltpu.make_async_copy(source, target, sems.at[len(copies)]))
            copies[-1].start()

        if kind == "first":
            for rows in (top, below):
                load(sources[0].at[0, rows], a_ref.at[rows, pl.ds(0, n)])
                load(sources[1].at[rows], a_ref.at[rows, pl.ds(n, n)])
            needed = 2
        elif kind == "next":
            load(sources[0].at[top], a_ref.at[top])
            if n > BLOCK:
                load(sources[0].at[below], a_ref.at[below])
            needed = 1
        else:
            parts = refs[-4]
            load(sources[0], a_ref)
            for p, part in enumerate(sources[1:]):
                load(
                    part.at[:, pl.ds(part.shape[1] - n, n)],
                    parts.at[pl.ds(p * BLOCK, BLOCK)],
                )
            needed = len(copies)
        for copy in copies[:needed]:
            copy.wait()
        if kind == "schur":
            for r in range(0, n, BLOCK):
                lhs = parts[:, r : r + BLOCK].T
                for c in range(r, n, BLOCK):
                    a_ref[r : r + BLOCK, c : c + BLOCK] -= dot(lhs, parts[:, c : c + BLOCK], NN)

        first, second = pl.ds(0, BASE), pl.ds(BASE, BASE)
        sub = lax.broadcasted_iota(jnp.int32, (BASE, BASE), 0)
        lane = lax.broadcasted_iota(jnp.int32, (BASE, BASE), 1)
        x_ref = refs[-4] if kind != "schur" else refs[-5]

        def base(b, carry):
            rows = pl.ds(pl.multiple_of(b * BASE, BASE), BASE)
            u, x = factor_base(a_ref[rows, rows])
            f_ref[rows, rows] = jnp.where(sub <= lane, u, x)
            x_ref[rows, rows] = x

            @pl.when(b == 0)
            def _():
                u12 = dot(x, a_ref[first, second], NN)
                f_ref[first, second] = u12
                a_ref[second, second] -= dot(u12, u12, TN)

            return carry

        lax.fori_loop(0, BLOCK // BASE, base, 0)
        x21 = -dot(x_ref[second, second], dot(f_ref[first, second], x_ref[first, first], TN), NN)
        f_ref[second, first] = x21
        x_ref[second, first] = x21
        x_ref[first, second] = jnp.zeros((BASE, BASE), F32)
        x = x_ref[...]
        for c in range(BLOCK, m, BLOCK):
            f_ref[:, c : c + BLOCK] = dot(x, a_ref[top, c : c + BLOCK], NN)
        leaving = [pltpu.make_async_copy(f_ref, f_out, sems.at[len(copies)])]
        leaving[0].start()
        for copy in copies[needed:]:
            copy.wait()
        for r in range(BLOCK, n, BLOCK):
            lhs = f_ref[:, r : r + BLOCK].T
            for c in range(r, m, BLOCK):
                a_ref[r : r + BLOCK, c : c + BLOCK] -= dot(lhs, f_ref[:, c : c + BLOCK], NN)
            rows = pl.ds(r, BLOCK)
            leaving.append(
                pltpu.make_async_copy(
                    a_ref.at[rows, pl.ds(BLOCK, m - BLOCK)],
                    rest_out.at[pl.ds(r - BLOCK, BLOCK)],
                    sems.at[len(copies) + len(leaving)],
                )
            )
            leaving[-1].start()
        for copy in leaving:
            copy.wait()


def factor_block(kind, flag, n, m, *sources):
    shapes = [shape(BLOCK, m)]
    if n > BLOCK:
        shapes.append(shape(n - BLOCK, m - BLOCK))
    scratch = [pltpu.VMEM((BLOCK, BLOCK), F32)]
    if kind == "schur":
        scratch.append(pltpu.VMEM((n, n), F32))
    scratch += [pltpu.VMEM((n, m), F32), pltpu.VMEM((BLOCK, m), F32), DMA((12,))]
    out = pl.pallas_call(
        lambda *refs: factor_kernel(kind, *refs),
        out_shape=shapes,
        in_specs=[SMEM] + [ANY] * len(sources),
        out_specs=[ANY] * len(shapes),
        scratch_shapes=scratch,
        cost_estimate=pl.CostEstimate(
            flops=2_000_000_000, bytes_accessed=8 * n * m, transcendentals=0
        ),
        compiler_params=params(),
    )(flag, *sources)
    return out if n > BLOCK else (out[0], None)


def choose(index, options, rows=None):
    options = [o if isinstance(o, list) else [o] for o in options]
    total, width = sum(a.shape[0] for a in options[0]), options[0][0].shape[1]
    start, size = rows or (0, total)

    def kernel(index_ref, *refs):
        *bufs, out_ref, held, sem = refs
        for k, option in enumerate(options):
            parts, bufs = bufs[: len(option)], bufs[len(option) :]

            @pl.when(index_ref[0] == k)
            def _():
                at = 0
                for part in parts:
                    high = min(part.shape[0], size)
                    copy = pltpu.make_async_copy(
                        part.at[pl.ds(start if rows else 0, high)], held.at[pl.ds(at, high)], sem
                    )
                    copy.start()
                    copy.wait()
                    at += high

        @pl.when(index_ref[0] >= 0)
        def _():
            copy = pltpu.make_async_copy(held, out_ref, sem)
            copy.start()
            copy.wait()

    flat = [a for option in options for a in option]
    return pl.pallas_call(
        kernel,
        out_shape=shape(size, width),
        in_specs=[SMEM] + [ANY] * len(flat),
        out_specs=ANY,
        scratch_shapes=[pltpu.VMEM((size, width), F32), DMA(())],
        compiler_params=params(8),
    )(index, *flat)


def unset(like):
    return pl.pallas_call(
        lambda out_ref: None, out_shape=shape(*like.shape), in_specs=[], out_specs=ANY
    )()


def patch(flags, result, parts):
    def kernel(flags_ref, result_ref, *refs):
        *bufs, out_ref, held, sem = refs
        for k, buf in enumerate(bufs):

            @pl.when(flags_ref[k] == 1)
            def _():
                for source, target in ((buf, held), (held, out_ref.at[k])):
                    copy = pltpu.make_async_copy(source, target, sem)
                    copy.start()
                    copy.wait()

    return pl.pallas_call(
        kernel,
        out_shape=shape(*result.shape),
        in_specs=[SMEM] + [ANY] * (1 + len(parts)),
        out_specs=ANY,
        scratch_shapes=[pltpu.VMEM(parts[0].shape, F32), DMA(())],
        input_output_aliases={1: 0},
        compiler_params=params(8),
    )(flags, result, *parts)


def split(x):
    high = x.astype(jnp.bfloat16)
    return high, (x - high.astype(F32)).astype(jnp.bfloat16)


def dot3(a, b, dims):
    total = None
    for x, y in ((a[1], b[0]), (a[0], b[1]), (a[0], b[0])):
        part = lax.dot_general(x, y, (dims, ((), ())), preferred_element_type=F32)
        total = part if total is None else total + part
    return total


PASS, WORK, ZERO, LOWER0, PANEL0, LOWER1 = range(6)


def finish_kernel(n_raw, n_sets, meta_ref, *refs):
    tiles_ref, raws, refs = refs[0], refs[1 : 1 + n_raw], refs[1 + n_raw :]
    order = tiles_ref.shape[-1]
    steps = order // BLOCK
    count = 2 * steps
    sets = [refs[k * count : (k + 1) * count] for k in range(n_sets)]
    out_ref, p1_ref, z, t, spare, high, low, *fs, sems = refs[n_sets * count :]
    role, transposed, col, edge = (meta_ref[k] for k in (0, 5, 7, 8))
    which = meta_ref[6], meta_ref[14]
    half = pl.ds(0, order), pl.ds(order, order)
    sources = [[tiles_ref.at[0]]]
    for ref in raws:
        if ref.shape[0] < order and len(sources[-1]) == 1 and sources[-1][0].shape[0] < order:
            sources[-1].append(ref)
        else:
            sources.append([ref])

    def load_pieces(pieces):
        for k in range(n_sets):
            for step in range(2):

                @pl.when(which[step] == k)
                def _():
                    for p in pieces:
                        if p // steps == step:
                            pltpu.make_async_copy(sets[k][p], fs[p], sems.at[8 + p]).start()

    def await_piece(p):
        pltpu.make_async_copy(sets[0][p], fs[p], sems.at[8 + p]).wait()

    def move_out(source, target, sem):
        copy = pltpu.make_async_copy(source, target, sems.at[sem])
        copy.start()
        return copy

    @pl.when(role == PASS)
    def _():
        held = (t, spare)
        copies = [move_out(tiles_ref.at[k], held[k], k) for k in range(2)]
        for k in range(2):
            copies[k].wait()
            copies[k] = move_out(held[k], out_ref.at[k], k)
        for copy in copies:
            copy.wait()

    @pl.when(role >= ZERO)
    def _():
        t[...] = jnp.zeros((order, order), F32)
        move_out(t, out_ref.at[1], 1).wait()

        def upper_block(p, q, lead):
            base = lead + (q - p) * BLOCK
            return fs[p][:, base : base + BLOCK].T

        def triangle(offset):
            sub = lax.broadcasted_iota(jnp.int32, (BLOCK, BLOCK), 0)
            lane = lax.broadcasted_iota(jnp.int32, (BLOCK, BLOCK), 1)
            for p in range(steps):
                for q in range(p, steps):
                    block = fs[offset + p][:, (q - p) * BLOCK : (q - p + 1) * BLOCK]
                    if p == q:
                        block = jnp.where(sub <= lane, block, 0.0)
                    t[q * BLOCK : (q + 1) * BLOCK, p * BLOCK : (p + 1) * BLOCK] = block.T

        for kind, pieces in (
            (LOWER0, range(steps)),
            (PANEL0, range(steps)),
            (LOWER1, range(steps, count)),
        ):

            @pl.when(role == kind)
            def _():
                load_pieces(pieces)
                for p in pieces:
                    await_piece(p)
                if kind == PANEL0:
                    for p in range(steps):
                        for q in range(steps):
                            t[q * BLOCK : (q + 1) * BLOCK, p * BLOCK : (p + 1) * BLOCK] = (
                                upper_block(p, q, order - p * BLOCK + p * BLOCK)
                            )
                else:
                    triangle(pieces[0])

        move_out(t, out_ref.at[0], 0).wait()

    @pl.when(role == WORK)
    def _():
        places = [z.at[half[a], half[b]] for a in range(2) for b in range(2)]
        for s, place in enumerate(places):
            for k, source in enumerate(sources):

                @pl.when(meta_ref[1 + s] == k)
                def _():
                    high = order // len(source)
                    for h, part in enumerate(source):
                        rows = pl.ds((s // 2) * order + h * high, high)
                        target = z.at[rows, half[s % 2]]
                        pltpu.make_async_copy(part, target, sems.at[s]).start()

        load_pieces(range(count))
        for slot, taken in ((1, col < 2), (0, col >= 2)):

            @pl.when(taken)
            def _():
                pltpu.make_async_copy(tiles_ref.at[slot], t, sems.at[4]).start()

        @pl.when(col >= 2)
        def _():
            move_out(tiles_ref.at[1], spare, 5)

        for s, place in enumerate(places):
            pltpu.make_async_copy(sources[1][0], place, sems.at[s]).wait()

        @pl.when(transposed == 1)
        def _():
            for left in (0, order):
                for a in range(steps):
                    for b in range(a, steps):
                        ra = order + a * BLOCK, left + a * BLOCK
                        rb = order + b * BLOCK, left + b * BLOCK
                        upper = z[ra[0] : ra[0] + BLOCK, rb[1] : rb[1] + BLOCK].T
                        if a != b:
                            z[ra[0] : ra[0] + BLOCK, rb[1] : rb[1] + BLOCK] = z[
                                rb[0] : rb[0] + BLOCK, ra[1] : ra[1] + BLOCK
                            ].T
                        z[rb[0] : rb[0] + BLOCK, ra[1] : ra[1] + BLOCK] = upper

        sub = lax.broadcasted_iota(jnp.int32, (BLOCK, BLOCK), 0)
        lane = lax.broadcasted_iota(jnp.int32, (BLOCK, BLOCK), 1)
        for p in range(count):
            await_piece(p)
            packed = fs[p][:, :BLOCK]
            inverse = jnp.where(
                sub > lane, packed, jnp.where(sub == lane, 1.0 / packed, 0.0)
            )
            inverse = split(inverse)
            for rows in half:
                solved = dot3(
                    split(z[rows, p * BLOCK : (p + 1) * BLOCK]), inverse, NT
                )
                z[rows, p * BLOCK : (p + 1) * BLOCK] = solved
                solved = split(solved)
                high[rows, :] = solved[0]
                low[rows, :] = solved[1]

            def eliminate(q, carry):
                to = pl.ds(pl.multiple_of(q * BLOCK, BLOCK), BLOCK)
                u = split(fs[p][:, pl.ds(pl.multiple_of((q - p) * BLOCK, BLOCK), BLOCK)])
                for rows in half:
                    z[rows, to] -= dot3((high[rows, :], low[rows, :]), u, NN)
                return carry

            lax.fori_loop(p + 1, count, eliminate, 0)
            if p == 0:
                pltpu.make_async_copy(tiles_ref.at[0], t, sems.at[4]).wait()

            def update(r, carry):
                rows = pl.ds(pl.multiple_of(r * BLOCK, BLOCK), BLOCK)
                others = high[half[1], :], low[half[1], :]
                t[rows, :] -= dot3((high[rows, :], low[rows, :]), others, NT)
                return carry

            lax.fori_loop(0, steps, update, 0)

        @pl.when(col >= 2)
        def _():
            pltpu.make_async_copy(tiles_ref.at[1], spare, sems.at[5]).wait()
            move_out(spare, out_ref.at[1], 5)

        @pl.when(col == 0)
        def _():
            move_out(z.at[half[0], half[0]], out_ref.at[0], 5)

        @pl.when(col == 1)
        def _():
            move_out(z.at[half[0], half[1]], out_ref.at[0], 5)

        for slot, taken in ((1, col < 2), (0, col >= 2)):

            @pl.when(taken)
            def _():
                move_out(t, out_ref.at[slot], 6)

        @pl.when((col == 2) & (edge == 1))
        def _():
            move_out(z.at[half[0], half[1]], p1_ref, 7).wait()

        pltpu.make_async_copy(t, out_ref.at[0], sems.at[5]).wait()
        pltpu.make_async_copy(t, out_ref.at[0], sems.at[6]).wait()


def finish(meta, tiles, raws, sets):
    order = tiles.shape[-1]
    count = len(sets[0])
    flat = [f for s in sets for f in s]
    scratch = [
        pltpu.VMEM((2 * order, 2 * order), F32),
        pltpu.VMEM((order, order), F32),
        pltpu.VMEM((order, order), F32),
        pltpu.VMEM((2 * order, BLOCK), jnp.bfloat16),
        pltpu.VMEM((2 * order, BLOCK), jnp.bfloat16),
    ]
    scratch += [pltpu.VMEM(f.shape, F32) for f in sets[0]] + [DMA((8 + count,))]
    return pl.pallas_call(
        lambda *refs: finish_kernel(len(raws), len(sets), *refs),
        out_shape=[shape(*tiles.shape), shape(order, order)],
        in_specs=[SMEM] + [ANY] * (1 + len(raws) + len(flat)),
        out_specs=[ANY, ANY],
        scratch_shapes=scratch,
        cost_estimate=pl.CostEstimate(
            flops=60_000_000_000, bytes_accessed=64 << 20, transcendentals=0
        ),
        compiler_params=params(56),
    )(meta, tiles, *raws, *flat)


def move(value, pairs, cols):
    flat = [(a * cols + b, c * cols + d) for (a, b), (c, d) in pairs]
    return lax.ppermute(value, ("row", "col"), flat)


def doubling(value, axis, root, size):
    place = lax.rem(lax.axis_index(axis) - root + size, size)
    reach = 1
    while reach < size:
        pairs = [
            ((root + i) % size, (root + i + reach) % size) for i in range(min(reach, size - reach))
        ]
        value = jnp.where(place >= reach, lax.ppermute(value, axis, pairs), value)
        reach *= 2
    return value


def both_ways(pairs):
    return pairs + [(b, a) for a, b in pairs]


def eliminate_last(panel, pieces):
    done = []
    for f in pieces:
        packed = f[:, :BLOCK]
        inverse = jnp.tril(packed, -1) + jnp.diag(1.0 / jnp.diagonal(packed))
        part = dot(panel[:, :BLOCK], inverse, NT, lax.Precision.HIGH)
        done.append(part)
        if f.shape[1] > BLOCK:
            panel = panel[:, BLOCK:] - dot(part, f[:, BLOCK:], NN, lax.Precision.HIGH)
    return jnp.concatenate(done, 1)


def on_device(kernel_tiles, profile):
    order = kernel_tiles.shape[-1]
    rows, cols = lax.axis_size("row"), lax.axis_size("col")
    row, col = lax.axis_index("row"), lax.axis_index("col")
    tiles = kernel_tiles.reshape(2, order, order)
    near = tiles[0]
    steps = order // BLOCK
    count = 2 * steps
    edge = cols + 2
    edge_live = profile[0, edge] <= 1
    owner = jnp.reshape(((row == 0) & (col == 0)).astype(jnp.int32), (1,))
    workers = range(2, edge)
    routed = cols == 4

    plan = [[[PASS] + [0] * 8 + [-1] * 5 + [0, -1, -1] for _ in range(cols)] for _ in range(rows)]
    for r in range(rows):
        for c in range(cols):
            plan[r][c][7] = c
            if r < 2:
                plan[r][c][0] = ZERO
            elif r < edge:
                plan[r][c][0] = WORK
    plan[0][0][0], plan[1][0][0], plan[1][1][0] = LOWER0, PANEL0, LOWER1

    if routed:
        r1 = move(near, both_ways([((r, 0), (r, 1)) for r in (0,) + tuple(workers)]), cols)
        r2 = move(
            near,
            [((r, c), (r, c + 2)) for r in workers for c in (0, 1)],
            cols,
        )
        r3 = move(
            near,
            both_ways([((4, c), (5, c)) for c in (0, 1)])
            + [((r, c), (r + 4, c)) for r in (0, 1) for c in (2, 3)],
            cols,
        )
        r4 = move(near, [((r, c), (r - 2, c)) for r in (4, 5) for c in (0, 1)], cols)
        tile01, tile11 = r1, move(near, [((1, 1), (0, 0))], cols)
        for r in workers:
            plan[r][0][1:3] = [0, 1]
            plan[r][1][1:3] = [1, 0]
            plan[r][2][1:3] = [2, 5]
            plan[r][3][1:3] = [5, 2]
            for c in range(4):
                plan[r][c][3:5] = plan[r][c][1:3]
        for place, pair in {
            (2, 0): (4, 7), (2, 1): (7, 6), (3, 0): (6, 7), (3, 1): (7, 4),
            (4, 1): (7, 3), (5, 0): (3, 7), (2, 3): (7, 6), (3, 2): (6, 7),
            (4, 2): (3, 6), (4, 3): (3, 6), (5, 2): (6, 3), (5, 3): (6, 3),
        }.items():
            plan[place[0]][place[1]][3:5] = pair
        for c in (0, 1):
            plan[2][c][12] = plan[3][c][12] = 2
        for c in (2, 3):
            plan[2][c][12] = plan[3][c][12] = 0
            plan[4][c][12] = plan[5][c][12] = 1
        plan[4][0][13] = plan[5][1][13] = 0
        plan[2][1][13] = plan[3][0][13] = 1
        plan[2][0][13] = plan[3][1][13] = plan[2][2][13] = plan[3][3][13] = 2
        for r in (4, 5):
            for c in (2, 3):
                plan[r][c][5] = 1
        plan[1][1][6] = 1
        for r in workers:
            plan[r][1][6] = plan[r][3][6] = 3 if r < 4 else 4
        for r in (1,) + tuple(workers):
            plan[r][0][6] = plan[r][2][6] = 5
        plan[1][1][14] = 4
        plan[0][0][15], plan[1][0][15], plan[1][0][16] = 0, 1, 0
        for r in workers:
            plan[r][0][14:17] = [1, -1, 1] if r < 4 else [2, -1, 2]
            plan[r][1][14], plan[r][2][14], plan[r][3][14] = 4, 3, 5
        plan[0][1][9], plan[1][1][9] = 0, 1
        plan[0][1][10:12], plan[1][1][10:12] = [0, -1], [1, 0]
        plan[0][3][10], plan[1][3][10] = 2, 2
        for r in workers:
            plan[r][1][11] = plan[r][3][11] = 1 if r < 4 else 2
    else:
        mine = jnp.where(col < 2, tiles[1], near)
        left0 = doubling(near, "col", 0, cols)
        left1 = doubling(near, "col", 1, cols)
        top0 = doubling(mine, "row", 0, rows)
        top1 = doubling(mine, "row", 1, rows)
        tile01 = move(near, [((0, 1), (0, 0))], cols)
        tile11 = move(near, [((1, 1), (0, 0))], cols)
        raws = [left0, left1, top0, top1]
        for r in range(rows):
            for c in range(cols):
                plan[r][c][1:6] = [1, 2, 3, 4, 1]
    meta = jnp.array(plan, jnp.int32)[row, col]
    meta = meta.at[8].set(edge_live.astype(jnp.int32))

    def fetch():
        if routed:
            e0 = move(near, [((edge, 1), (edge - 2, 2))], cols)
            e1 = move(e0, [((edge - 2, 2), (edge - 4, 2))], cols)
            e2 = move(e0 + e1, [((r, 2), (r + 1, 2)) for r in (2, 4)], cols)
            return e0 + e1 + e2
        total = jnp.zeros_like(near)
        for r in workers:
            total = total + move(near, [((edge, 1), (r, 2))], cols)
        return total

    edge_tile = lax.cond(edge_live, lambda _: fetch(), lambda _: unset(near), 0)

    pieces, copies, state = [], [], None
    drain = max(STAGES[0], steps + STAGES[1]) - steps if routed else 0
    for slot in range(count + drain):
        if slot < count:
            step, local = divmod(slot, steps)
            n = order - local * BLOCK
            if slot == 0:
                args = ("first", owner, n, 2 * n, tiles, tile01)
            elif local == 0:
                args = ("schur", owner, n, n, tile11, *pieces)
            else:
                args = ("next", owner, n, n + (1 - step) * order, state)
            piece, state = factor_block(*args)
            pieces.append(piece)
            copies.append([])
            if not routed:
                copies[-1].append(doubling(doubling(piece, "row", 0, rows), "col", 0, cols))
        if not routed:
            continue
        arrived = {}
        for p in range(max(0, slot - max(STAGES)), min(slot, count)):
            got, k = copies[p], slot - p
            if k > STAGES[p // steps]:
                continue
            if p < steps:
                if k == 1:
                    new = [move(pieces[p], [((0, 0), (0, 1))], cols)]
                elif k == 2:
                    new = [move(got[0], [((0, 1), (1, 1))], cols)]
                elif k == 3:
                    via = choose(meta[9:10], got)
                    new = [move(via, [((r, 1), (r, 3)) for r in (0, 1)], cols)]
                elif k == 4:
                    via = choose(meta[10:11], got)
                    pairs = [((r, c), (r + 2, c)) for r in (0, 1) for c in (1, 3)]
                    new = [move(via, pairs, cols)]
                elif k == 5:
                    pairs = [((r, c), (r + 2, c)) for r in (2, 3) for c in (1, 3)]
                    new = [move(got[3], pairs, cols)]
                else:
                    via = choose(meta[11:12], [got[1], got[3], got[4]])
                    pairs = [((r, c), (r, c - 1)) for r in workers for c in (1, 3)]
                    new = [move(via, pairs + [((1, 1), (1, 0))], cols)]
            elif k == 1:
                new = [move(pieces[p], [((0, 0), (1, 0))], cols)]
            elif k == 2:
                via = choose(meta[15:16], [pieces[p], got[0]])
                new = [
                    move(via, [((r, 0), (r + far, 0)) for r in (0, 1)], cols) for far in (2, 4)
                ]
            else:
                via = choose(meta[16:17], got)
                new = [
                    move(via, [((r, 0), (r, c)) for r in workers] + also, cols)
                    for c, also in ((2, []), (1, [((1, 0), (1, 1))]), (3, []))
                ]
            arrived[p] = new
        late = []
        if slot == EDGE:
            late = [edge_tile]
        elif slot == FIRST:
            late = [r2, r3, r4, tile11]
        elif slot == SECOND[0]:
            late = [r5, r6[0]]
        elif slot == SECOND[1]:
            late = [r6[1]]
        elif slot == THIRD:
            late = [r7]
        flowing = ([pieces[slot]] if slot < count else []) + ([] if state is None else [state])
        flowing, arrived, late = lax.optimization_barrier((flowing, arrived, late))
        if slot < count:
            pieces[slot] = flowing[0]
        if state is not None:
            state = flowing[-1]
        for p, new in arrived.items():
            copies[p] += new
        if slot == EDGE:
            (edge_tile,) = late
        elif slot == FIRST:
            r2, r3, r4, tile11 = late
            r5 = move(r2, both_ways([((r, 2), (r, 3)) for r in workers]), cols)
            across = both_ways(
                [((2, c), (3, c)) for c in range(4)] + [((4, c), (5, c)) for c in (2, 3)]
            )
            high = order // 2
            r6 = [move(choose(meta[12:13], [r2, r3, r4], (0, high)), across, cols), None]
        elif slot == SECOND[0]:
            r5, r6[0] = late
            r6[1] = move(choose(meta[12:13], [r2, r3, r4], (high, high)), across, cols)
        elif slot == SECOND[1]:
            (r6[1],) = late
            r7 = move(
                choose(meta[13:14], [r3, r4, r6]),
                [((4, 0), (4, 1)), ((5, 1), (5, 0)), ((2, 1), (2, 0)), ((3, 0), (3, 1))]
                + [((2, 0), (2, 1)), ((3, 1), (3, 0)), ((2, 2), (2, 3)), ((3, 3), (3, 2))],
                cols,
            )
        elif slot == THIRD:
            (r7,) = late

    if routed:
        sets = [pieces] + [[got[k] for got in copies] for k in (1, 2, 3, 4, 5)]
        last_pieces = sets[3][steps:]
        raws = [r1, r2, r3, r4, r5, *r6, r7]
    else:
        sets = [[got[0] for got in copies]]
        last_pieces = sets[0][steps:]

    result, panel1 = finish(meta, tiles, raws, sets)
    at_edge = edge_live & (row == edge)
    flags = jnp.stack(
        [
            at_edge & (col >= 1),
            (at_edge & (col <= 2)) | (edge_live & (row >= 2) & (row < edge) & (col == 2)),
        ]
    ).astype(jnp.int32)

    def edge_parts(args):
        panel1, edge_tile, last_pieces = args
        far = tiles[1]
        last = eliminate_last(edge_tile, last_pieces)
        column = far - dot(panel1, last, NT, lax.Precision.HIGH)
        sent = move(column, [((r, 2), (edge, r % cols)) for r in workers], cols).T
        solved = move(last, [((edge - 2, 2), (edge, 1)), ((edge - 1, 2), (edge, 2))], cols)
        corner = far - dot(solved, solved, NT, lax.Precision.HIGH)
        part0 = jnp.where(col == 1, solved, sent)
        part1 = jnp.where(row == edge, jnp.where(col == 2, corner, sent), column)
        return part0, part1

    def no_edge(args):
        return unset(near), unset(near)

    parts = lax.cond(edge_live, edge_parts, no_edge, (panel1, edge_tile, last_pieces))
    return patch(flags, result, parts).reshape(kernel_tiles.shape)


def solution(mesh):
    placed = (P(None, "row", None, "col", None, None), P())
    return jax.shard_map(
        on_device,
        mesh=mesh,
        in_specs=placed,
        out_specs=P(None, "row", None, "col", None, None),
        check_vma=False,
    )
```
